32 devices in a mesh: seq: 8 (over y, x, core), rank: 4 (over z).
Axes of the slice: x: 2, y: 2, z: 4, core: 2. Of those that a mesh axis runs over, the one named last changes fastest.
Arguments:
- tokens_in: bfloat16 [4608, 2048], P('seq'), may hold values from -6 to 6
- norm1_gain: float32 [2048], replicated, may hold values from 0.5 to 1.5
- q_down: bfloat16 [2048, 1024], P(None, 'rank'), may hold values from -1 to 1
- latent_gain: float32 [1024], P('rank'), may hold values from 0.5 to 1.5
- q_up: bfloat16 [1024, 4096], P('rank'), may hold values from -1 to 1
- kv_weight: bfloat16 [2048, 512], replicated, may hold values from -0.125 to 0.125
- out_weight: bfloat16 [4096, 2048], P('rank'), may hold values from -0.375 to 0.375
- norm2_gain: float32 [2048], replicated, may hold values from 0.5 to 1.5
- gate_weight: bfloat16 [2048, 5632], P(None, 'rank'), may hold values from -0.125 to 0.125
- up_weight: bfloat16 [2048, 5632], P(None, 'rank'), may hold values from -0.125 to 0.125
- down_weight: bfloat16 [5632, 2048], P('rank'), may hold values from -0.15625 to 0.15625
- doc_ids: int32 [4608], replicated, may hold values from 0 to 8, as said below
- out_grad: bfloat16 [4608, 2048], P('seq'), may hold values from -6 to 6
Outputs:
- layer_out: bfloat16 [4608, 2048], P('seq')
- grad_in: float32 [4608, 2048], P('seq', 'rank')
- grad_norm1: float32 [2048], P('rank')
- grad_q_down: float32 [2048, 1024], P(None, 'rank')
- grad_latent_gain: float32 [1024], P('rank')
- grad_q_up: float32 [1024, 4096], P('rank')
- grad_kv_weight: float32 [2048, 512], P('rank')
- grad_out: float32 [4096, 2048], P('rank')
- grad_norm2: float32 [2048], replicated
- grad_gate: float32 [2048, 5632], P(None, 'rank')
- grad_up: float32 [2048, 5632], P(None, 'rank')
- grad_down: float32 [5632, 2048], P('rank')
The draws below stay inside these ranges and needn't reach their ends.
Inputs may be any that keep to these rules, and one draw needn't show every extreme that they name: `doc_ids`: document numbers never fall along the row; equal numbers in a run mark one document.
All inputs are finite; a program needn't handle non-finite values.
Results may differ from the reference program's by a relative error of at most 0.022.
Values may be sent and summed in bfloat16 or wider, within the bound.
No kernel may reach another device: no remote copies, remote signals or barrier semaphores. Data moves between devices by JAX's collectives and lax.ppermute only.
A program may use at most 320 MiB of HBM per device.

```python
import math
import jax
import jax.numpy as jnp
from jax import lax

D = 2048
R = 1024
H = 16
HD = 256
FF = 5632
TOK_DEV = 576
TOKENS = 4608


SPAN = 30.0


def rank_scale(key):
    raw = jax.random.uniform(jax.random.fold_in(key, 101), (R,), jnp.float32)
    second = (SPAN * SPAN - 1.0) / (2.0 * math.log(SPAN))
    return jnp.exp(raw * math.log(SPAN)) / math.sqrt(second)


def fourth_moment():
    second = (SPAN * SPAN - 1.0) / (2.0 * math.log(SPAN))
    fourth = (SPAN ** 4 - 1.0) / (4.0 * math.log(SPAN))
    return fourth / (second * second)


def draw_q_down(key, part):
    shared = rank_scale(key)
    key = jax.random.fold_in(key, 3)
    entries = jax.random.truncated_normal(key, -3.0, 3.0, (D, R), jnp.float32) / math.sqrt(D)
    return (entries * shared[None, :]).astype(jnp.bfloat16)


def draw_q_up(key, part):
    shared = rank_scale(key)
    key = jax.random.fold_in(key, 5)
    entries = jax.random.truncated_normal(key, -3.0, 3.0, (R, H * HD), jnp.float32)
    entries = entries / math.sqrt(R * fourth_moment())
    return (entries * shared[:, None]).astype(jnp.bfloat16)


def draw_doc_ids(key, part):
    key = jax.random.fold_in(key, 7)
    keys_all = jax.random.split(key, 4)
    first_cut = jax.random.randint(keys_all[0], (), 1, TOK_DEV)
    last_cut = TOKENS - jax.random.randint(keys_all[1], (), 1, TOK_DEV)
    left_cuts = jax.random.randint(keys_all[2], (3,), 1, first_cut + 1)
    right_cuts = jax.random.randint(keys_all[3], (3,), last_cut, TOKENS)
    cut_points = jnp.concatenate([left_cuts, first_cut[None], last_cut[None], right_cuts])
    index_all = jnp.arange(TOKENS, dtype=jnp.int32)
    return jnp.sum((index_all[:, None] >= cut_points[None, :]).astype(jnp.int32), axis=1)


def shard_levels(own_key, shape, shards, smallest, high):
    def one(axis_at, parts):
        heights = jax.random.uniform(jax.random.fold_in(jax.random.fold_in(own_key, 6), axis_at), (parts,), jnp.float32, smallest / len(shards), high / len(shards))
        return jnp.repeat(jnp.exp(heights), shape[axis_at] // parts).reshape((-1,) + (1,) * (len(shape) - axis_at - 1))

    level = one(*shards[0])
    for cut in shards[1:]:
        level = level * one(*cut)
    return level


def normal_values(stream_key, dims, spread, reach, shards=(), held_as=jnp.bfloat16):
    factor_of = shard_levels(stream_key, dims, shards, -0.22, 0.18) if shards else 1.0
    array = jax.random.normal(stream_key, dims, jnp.float32) * spread * factor_of
    return jnp.minimum(jnp.maximum(array, -reach), reach).astype(held_as)


def setup_inputs(seed: int = 0) -> dict:
    splits = jax.random.split(jax.random.key(seed), 14)
    return {
        "tokens_in": normal_values(splits[0], (TOKENS, D), 1.0, 6.0, ((0, 8),)),
        "norm1_gain": jnp.clip(1.0 + 0.1 * jax.random.normal(splits[1], (D,), jnp.float32), 0.5, 1.5),
        "q_down": draw_q_down(jax.random.fold_in(splits[13], 71), 0),
        "latent_gain": jnp.clip(1.0 + 0.1 * jax.random.normal(splits[3], (R,), jnp.float32), 0.5, 1.5),
        "q_up": draw_q_up(jax.random.fold_in(splits[13], 71), 0),
        "kv_weight": normal_values(splits[5], (D, 2 * HD), D ** -0.5, 0.125),
        "out_weight": normal_values(splits[6], (H * HD, D), HD ** -0.5, 0.375, ((0, 4),)),
        "norm2_gain": jnp.clip(1.0 + 0.1 * jax.random.normal(splits[7], (D,), jnp.float32), 0.5, 1.5),
        "gate_weight": normal_values(splits[8], (D, FF), D ** -0.5, 0.125, ((1, 4),)),
        "up_weight": normal_values(splits[9], (D, FF), D ** -0.5, 0.125, ((1, 4),)),
        "down_weight": normal_values(splits[10], (FF, D), (FF // 4) ** -0.5, 0.15625, ((0, 4),)),
        "doc_ids": draw_doc_ids(jax.random.fold_in(splits[13], 71), 0),
        "out_grad": normal_values(splits[12], (TOKENS, D), 1.0, 6.0, ((0, 8),)),
    }


EPS = 1e-05
BASE = 10000.0
NEG = -1e+30

@jax.custom_vjp
def low(v):
    return lax.optimization_barrier(v.astype(jnp.bfloat16)).astype(jnp.float32)

@jax.custom_vjp
def low_back(v):
    return v

def low_keep(v):
    return (low(v), None)

def low_pass(kept, grad):
    return (grad,)

def back_keep(v):
    return (v, None)

def back_low(kept, grad):
    return (low(grad),)
low.defvjp(low_keep, low_pass)
low_back.defvjp(back_keep, back_low)

def matmul_hi(left, right):
    return jnp.dot(left, right, precision=lax.Precision.HIGHEST, preferred_element_type=jnp.float32)

def rms_norm(values, gain):
    recip = lax.rsqrt(lax.optimization_barrier(jnp.mean(values * values, -1, keepdims=True)) + EPS)
    return values * recip * gain

def rotate(values, cosine_rows, sine_rows):
    half_dim = values.shape[-1] // 2
    front_half = values[..., :half_dim]
    back_half = values[..., half_dim:]
    return jnp.concatenate([front_half * cosine_rows - back_half * sine_rows, front_half * sine_rows + back_half * cosine_rows], -1)

def rope_tables(doc_ids):
    index_all = jnp.arange(doc_ids.shape[0], dtype=jnp.int32)
    changed = jnp.concatenate([jnp.ones((1,), dtype=bool), doc_ids[1:] != doc_ids[:-1]])
    starts = lax.cummax(jnp.where(changed, index_all, 0).astype(jnp.int32), axis=0)
    position = (index_all - starts).astype(jnp.float32)
    half_dim = HD // 2
    freqs = BASE ** (-jnp.arange(half_dim, dtype=jnp.float32) / half_dim)
    angle = position[:, None] * freqs[None, :]
    return (jnp.cos(angle), jnp.sin(angle))

def reference(tokens_in, norm1_gain, q_down, latent_gain, q_up, kv_weight, out_weight, norm2_gain, gate_weight, up_weight, down_weight, doc_ids, out_grad):
    cosine_tab, sine_tab = rope_tables(doc_ids)
    key_count = doc_ids.shape[0]
    block_rows = 512 if key_count % 512 == 0 else key_count
    index_all = jnp.arange(key_count, dtype=jnp.int32)
    score_scale = HD ** (-0.5)

    def attend(query, keys, values):

        def one_block(args):
            query_blk, ids_blk, index_blk = args
            raw = jnp.einsum('bhd,nd->hbn', query_blk, keys, precision=lax.Precision.HIGHEST)
            scores = low_back(raw * score_scale)
            allowed = (ids_blk[:, None] == doc_ids[None, :]) & (index_all[None, :] <= index_blk[:, None])
            scores = jnp.where(allowed[None], scores, NEG)
            attn_probs = low(jax.nn.softmax(scores, axis=-1))
            mixed_blk = jnp.einsum('hbn,nd->bhd', attn_probs, values, precision=lax.Precision.HIGHEST)
            return mixed_blk.reshape(mixed_blk.shape[0], H * HD)
        blocks = key_count // block_rows
        result = lax.map(jax.checkpoint(one_block), (query.reshape(blocks, block_rows, H, HD), doc_ids.reshape(blocks, block_rows), index_all.reshape(blocks, block_rows)))
        return result.reshape(key_count, H * HD)

    def forward(tokens_f, gain_first, qdown_mat, gain_latent, qup_mat, kv_mat, out_mat, gain_second, gate_mat, up_mat, down_mat):
        normed_in = low(rms_norm(tokens_f, gain_first))
        latent = low_back(matmul_hi(normed_in, qdown_mat))
        latent_n = low(rms_norm(latent, gain_latent))
        query_pre = low_back(matmul_hi(latent_n, qup_mat)).reshape(key_count, H, HD)
        query = low_back(low(rotate(query_pre, cosine_tab[:, None, :], sine_tab[:, None, :])))
        kv_pre = low_back(matmul_hi(normed_in, kv_mat))
        keys = low_back(low(rotate(kv_pre[:, :HD], cosine_tab, sine_tab)))
        values = low(kv_pre[:, HD:])
        attn_vals = low_back(low(attend(query, keys, values)))
        residual = tokens_f + low_back(matmul_hi(attn_vals, out_mat))
        normed_mid = low(rms_norm(residual, gain_second))
        gate_pre = low_back(matmul_hi(normed_mid, gate_mat))
        up_pre = low_back(matmul_hi(normed_mid, up_mat))
        hidden = low(jax.nn.silu(gate_pre) * up_pre)
        return residual + matmul_hi(hidden, down_mat)
    primals = (tokens_in.astype(jnp.float32), norm1_gain.astype(jnp.float32), q_down.astype(jnp.float32), latent_gain.astype(jnp.float32), q_up.astype(jnp.float32), kv_weight.astype(jnp.float32), out_weight.astype(jnp.float32), norm2_gain.astype(jnp.float32), gate_weight.astype(jnp.float32), up_weight.astype(jnp.float32), down_weight.astype(jnp.float32))
    layer_f, pullback = jax.vjp(forward, *primals)
    grads = pullback(out_grad.astype(jnp.float32))
    return (layer_f.astype(jnp.bfloat16), grads[0], grads[1], grads[2], grads[3], grads[4], grads[5], grads[6], grads[7], grads[8], grads[9], grads[10])
```

```python
import functools

import jax
import jax.numpy as jnp
from jax import lax
from jax.experimental import pallas as pl
from jax.experimental.pallas import tpu as pltpu
from jax.sharding import PartitionSpec as P

EPS = 1e-05
BASE = 10000.0
NEG = -1e30
LOG2E = 1.4426950408889634
BF = jnp.bfloat16
F32 = jnp.float32
I32 = jnp.int32


def norm_rows(values, gain):
    recip = lax.rsqrt(jnp.mean(values * values, -1, keepdims=True) + EPS)
    return (values * recip * gain, recip)


def rotate(values, cosine_rows, sine_rows):
    half_dim = values.shape[-1] // 2
    front_half = values[..., :half_dim]
    back_half = values[..., half_dim:]
    return jnp.concatenate(
        [
            front_half * cosine_rows - back_half * sine_rows,
            front_half * sine_rows + back_half * cosine_rows,
        ],
        -1,
    )


def dense(left, right):
    return jnp.dot(left, right, preferred_element_type=F32)


def dense_tn(left, right):
    return lax.dot_general(left, right, (((0,), (0,)), ((), ())), preferred_element_type=F32)


def dense_nt(left, right):
    return lax.dot_general(left, right, (((1,), (1,)), ((), ())), preferred_element_type=F32)


def key_block(key_count):
    for size in (512, 256, 128):
        if key_count % size == 0:
            return size
    return key_count


def row_tile(rows):
    for parts in (3, 2):
        if rows % (parts * 128) == 0:
            return rows // parts
    return rows


def over_key_blocks(info_ref, size, tokens, run):
    first, low, high = info_ref[0], info_ref[1], info_ref[2]
    begin = low // size
    whole_end = jnp.maximum(first // size, begin)
    whole_begin = jnp.clip((high + size - 1) // size, begin, whole_end)
    end = (first + tokens + size - 1) // size
    lax.fori_loop(begin, whole_begin, lambda j, c: run(j, True), None)
    lax.fori_loop(whole_begin, whole_end, lambda j, c: run(j, False), None)
    lax.fori_loop(whole_end, end, lambda j, c: run(j, True), None)


def attend_kernel(
    size, tile, heads, info_ref, pre_ref, cos_ref, sin_ref, kv_ref, start_ref, index_ref,
    query_ref, out_ref, log_ref, max_ref, sum_ref, acc_ref,
):
    tokens = pre_ref.shape[0]
    width = kv_ref.shape[1] // 2
    half = width // 2
    scale = width**-0.5 * LOG2E
    cosine, sine = cos_ref[...], sin_ref[...]
    for h in range(heads):
        front = pre_ref[:, h * width : h * width + half]
        back = pre_ref[:, h * width + half : (h + 1) * width]
        rows = slice(h * tokens, (h + 1) * tokens)
        query_ref[rows, :half] = (front * cosine - back * sine).astype(BF)
        query_ref[rows, half:] = (front * sine + back * cosine).astype(BF)
    max_ref[...] = jnp.full(max_ref.shape, NEG, F32)
    sum_ref[...] = jnp.zeros(sum_ref.shape, F32)
    acc_ref[...] = jnp.zeros(acc_ref.shape, F32)

    def run(j, masked):
        base = pl.multiple_of(j * size, size)
        keys = kv_ref[pl.ds(base, size), :width]
        values = kv_ref[pl.ds(base, size), width:]
        for i in range(heads * tokens // tile):
            r = slice(i * tile, (i + 1) * tile)
            scores = dense_nt(keys, query_ref[r, :])
            if masked:
                at = base + lax.broadcasted_iota(I32, (size, tile), 0)
                allowed = (at >= start_ref[:, r]) & (at <= index_ref[:, r])
                scores = jnp.where(allowed, scores, NEG)
            old = max_ref[:, r]
            new = jnp.maximum(old, jnp.max(scores, 0, keepdims=True) * scale)
            probs = jnp.exp2(scores * scale - new)
            if masked:
                probs = jnp.where(allowed, probs, 0.0)
            fade = jnp.exp2(old - new)
            max_ref[:, r] = new
            sum_ref[:, r] = fade * sum_ref[:, r] + jnp.sum(probs, 0, keepdims=True)
            acc_ref[:, r] = fade * acc_ref[:, r] + dense_tn(values, probs.astype(BF))
        return None

    over_key_blocks(info_ref, size, tokens, run)
    total = sum_ref[...]
    log_ref[...] = max_ref[...] + jnp.log2(total)
    out = (acc_ref[...] * (1.0 / total)).T
    for h in range(heads):
        out_ref[:, h * width : (h + 1) * width] = out[h * tokens : (h + 1) * tokens, :]


def in_vmem(count):
    return [pl.BlockSpec(memory_space=pltpu.VMEM) for _ in range(count)]


def attend(info, query_pre, cosine, sine, kv, start, index):
    tokens, all_heads = query_pre.shape
    keys, width = kv.shape[0], kv.shape[1] // 2
    rows = tokens * (all_heads // width)
    return pl.pallas_call(
        functools.partial(attend_kernel, key_block(keys), row_tile(rows), all_heads // width),
        out_shape=(
            jax.ShapeDtypeStruct((rows, width), BF),
            jax.ShapeDtypeStruct((tokens, all_heads), F32),
            jax.ShapeDtypeStruct((1, rows), F32),
        ),
        in_specs=[pl.BlockSpec(memory_space=pltpu.SMEM)] + in_vmem(6),
        out_specs=tuple(in_vmem(3)),
        scratch_shapes=[
            pltpu.VMEM((1, rows), F32),
            pltpu.VMEM((1, rows), F32),
            pltpu.VMEM((width, rows), F32),
        ],
        compiler_params=pltpu.CompilerParams(vmem_limit_bytes=48 * 2**20),
        cost_estimate=pl.CostEstimate(
            flops=4 * rows * keys * width,
            bytes_accessed=12 * rows * width + 4 * keys * width,
            transcendentals=rows * keys,
        ),
        name="attend",
    )(info, query_pre, cosine, sine, kv, start, index)


def attend_back_kernel(
    size, tile, heads, info_ref, query_ref, grad_ref, delta_ref, log_ref, cos_ref, sin_ref, kv_ref, start_ref, index_ref,
    gq_ref, near_ref, far_ref, gout_ref, gk_ref, gv_ref, gqt_ref,
):
    tokens = grad_ref.shape[0]
    width = kv_ref.shape[1] // 2
    half = width // 2
    scale = width**-0.5
    for h in range(heads):
        gout_ref[h * tokens : (h + 1) * tokens, :] = grad_ref[:, h * width : (h + 1) * width]
    gk_ref[...] = jnp.zeros(gk_ref.shape, F32)
    gv_ref[...] = jnp.zeros(gv_ref.shape, F32)
    gqt_ref[...] = jnp.zeros(gqt_ref.shape, F32)

    def run(j, masked):
        base = pl.multiple_of(j * size, size)
        at_keys = pl.ds(base, size)
        keys = kv_ref[at_keys, :width]
        values = kv_ref[at_keys, width:]
        for i in range(heads * tokens // tile):
            r = slice(i * tile, (i + 1) * tile)
            query, gout = query_ref[r, :], gout_ref[r, :]
            probs = jnp.exp2(dense_nt(keys, query) * (scale * LOG2E) - log_ref[:, r])
            if masked:
                at = base + lax.broadcasted_iota(I32, (size, tile), 0)
                allowed = (at >= start_ref[:, r]) & (at <= index_ref[:, r])
                probs = jnp.where(allowed, probs, 0.0)
            gscores = (probs * (dense_nt(values, gout) - delta_ref[:, r])).astype(BF)
            gv_ref[at_keys, :] += dense(probs.astype(BF), gout)
            gk_ref[at_keys, :] += dense(gscores, query)
            gqt_ref[:, r] += dense_tn(keys, gscores)
        return None

    over_key_blocks(info_ref, size, tokens, run)
    mine = info_ref[3]
    for s in range(kv_ref.shape[0] // tokens):
        rows = slice(s * tokens, (s + 1) * tokens)
        gk = (gk_ref[rows, :] * scale).astype(BF)
        gv = gv_ref[rows, :].astype(BF)

        @pl.when(mine == s % 2)
        def _(s=s, gk=gk, gv=gv):
            near_ref[s // 2, :, :width] = gk
            near_ref[s // 2, :, width:] = gv

        @pl.when(mine != s % 2)
        def _(s=s, gk=gk, gv=gv):
            far_ref[s // 2, :, :width] = gk
            far_ref[s // 2, :, width:] = gv

    gq = (gqt_ref[...] * scale).T.astype(BF).astype(F32)
    cosine, sine = cos_ref[...], sin_ref[...]
    for h in range(heads):
        front = gq[h * tokens : (h + 1) * tokens, :half]
        back = gq[h * tokens : (h + 1) * tokens, half:]
        gq_ref[:, h * width : h * width + half] = (front * cosine + back * sine).astype(BF)
        gq_ref[:, h * width + half : (h + 1) * width] = (back * cosine - front * sine).astype(BF)


def attend_back(info, query, grad, delta, log, cosine, sine, kv, start, index):
    tokens, all_heads = grad.shape
    keys, width = kv.shape[0], kv.shape[1] // 2
    rows = tokens * (all_heads // width)
    blocks = keys // tokens
    return pl.pallas_call(
        functools.partial(attend_back_kernel, key_block(keys), row_tile(rows), all_heads // width),
        out_shape=(
            jax.ShapeDtypeStruct((tokens, all_heads), BF),
            jax.ShapeDtypeStruct((blocks // 2, tokens, 2 * width), BF),
            jax.ShapeDtypeStruct((blocks // 2, tokens, 2 * width), BF),
        ),
        in_specs=[pl.BlockSpec(memory_space=pltpu.SMEM)] + in_vmem(9),
        out_specs=tuple(in_vmem(3)),
        scratch_shapes=[
            pltpu.VMEM((rows, width), BF),
            pltpu.VMEM((keys, width), F32),
            pltpu.VMEM((keys, width), F32),
            pltpu.VMEM((width, rows), F32),
        ],
        compiler_params=pltpu.CompilerParams(vmem_limit_bytes=56 * 2**20),
        cost_estimate=pl.CostEstimate(
            flops=10 * rows * keys * width,
            bytes_accessed=6 * rows * width + 8 * keys * width,
            transcendentals=rows * keys,
        ),
        name="attend_back",
    )(info, query, grad, delta, log, cosine, sine, kv, start, index)


def swap(value, bit):
    count = lax.axis_size("seq")
    return lax.ppermute(value, "seq", [(i, i ^ (1 << bit)) for i in range(count)])


def bit_of(index, bit):
    return (index >> bit) & 1


def add_low(left, right):
    return (left.astype(F32) + right.astype(F32)).astype(BF)


def halve(value, axis, bit, seq_ix):
    own = bit_of(seq_ix, bit)
    keep = lax.dynamic_index_in_dim(value, own, axis, keepdims=False)
    send = lax.dynamic_index_in_dim(value, 1 - own, axis, keepdims=False)
    return add_low(keep, swap(send, bit))


def scatter_chips(value, seq_ix):
    bits = value.shape[0].bit_length() - 1
    shape = (2,) * bits + value.shape[2:]
    first, last = value[:, 0].reshape(shape), value[:, 1].reshape(shape)
    first_axes = list(range(bits))
    last_axes = list(range(bits))
    for step in range(bits):
        bit = step + 1
        axis = first_axes.index(bits - bit)
        first = halve(first, axis, bit, seq_ix)
        del first_axes[axis]
        bit = bits - step
        axis = last_axes.index(bits - bit)
        last = halve(last, axis, bit, seq_ix)
        del last_axes[axis]
    return jnp.stack([first, last])


def scatter_rows(near, far, seq_ix):
    return scatter_chips(add_low(near, swap(far, 0)), seq_ix)


def split_product(left, right, seq_ix):
    chips = lax.axis_size("seq") // 2
    rows = left.shape[1] // 2
    own = bit_of(seq_ix, 0)
    parts = []
    for core in (own, 1 - own):
        piece = lax.dynamic_slice_in_dim(left, core * rows, rows, 1)
        parts.append(dense_tn(piece, right).astype(BF))
    shape = (2, chips, rows // (2 * chips), right.shape[1])
    return [jnp.swapaxes(part.reshape(shape), 0, 1) for part in parts]


def gather_rows(piece):
    seq = lax.axis_size("seq")
    whole = lax.all_gather(piece, "seq", axis=0, tiled=False)
    whole = whole.reshape((seq // 2, 2) + piece.shape)
    whole = jnp.transpose(whole, (1, 2, 0, 3, 4))
    return whole.reshape(seq * piece.shape[0] * piece.shape[1], piece.shape[2])


def reduce_product(left, right, seq_ix):
    near, far = split_product(left, right, seq_ix)
    return gather_rows(scatter_rows(near, far, seq_ix)).astype(F32)


def gather_kv(local, seq_ix):
    seq = lax.axis_size("seq")
    if seq != 8:
        return lax.all_gather(local, "seq", axis=0, tiled=True)
    half = local.shape[0] // 2
    by_x = swap(local, 1)
    by_y = swap(local, 2)
    across = jnp.concatenate([swap(by_x[:half], 2), swap(by_y[half:], 1)], 0)
    blocks = {0: local, 2: by_x, 4: by_y, 6: across}
    for mask in (0, 2, 4, 6):
        blocks[mask + 1] = swap(blocks[mask], 0)
    whole = jnp.zeros((seq * local.shape[0], local.shape[1]), local.dtype)
    for mask, block in blocks.items():
        whole = lax.dynamic_update_slice_in_dim(
            whole, block, (seq_ix ^ mask) * local.shape[0], 0
        )
    return whole


def high_low(values):
    high = values.astype(BF)
    return [high, (values - high.astype(F32)).astype(BF)]


def per_device(
    tokens_in,
    norm1_gain,
    q_down,
    latent_gain,
    q_up,
    kv_weight,
    out_weight,
    norm2_gain,
    gate_weight,
    up_weight,
    down_weight,
    doc_ids,
    out_grad,
):
    row_count, model_width = tokens_in.shape
    rank_count = lax.axis_size("rank")
    seq_count = lax.axis_size("seq")
    rank_ix = lax.axis_index("rank")
    seq_ix = lax.axis_index("seq")
    head_dim = kv_weight.shape[1] // 2
    local_heads = out_weight.shape[0] // head_dim
    first_row = seq_ix * row_count
    core = bit_of(seq_ix, 0)
    own_rows = row_count // rank_count
    rank_cols = q_down.shape[1]
    rank_width = rank_cols * rank_count

    half_rows = q_up.shape[0] // 2
    up_half = lax.dynamic_slice_in_dim(q_up, core * half_rows, half_rows, 0)
    up_half = lax.all_to_all(up_half, "rank", 1, 0, tiled=True)
    up_other = swap(up_half, 0)
    up_half = up_half.reshape(rank_count, 1, half_rows, -1)
    up_other = up_other.reshape(rank_count, 1, half_rows, -1)
    q_up_own = jnp.concatenate(
        [jnp.where(core == 0, up_half, up_other), jnp.where(core == 0, up_other, up_half)], 1
    ).reshape(rank_width, -1)

    ids_local = lax.dynamic_slice_in_dim(doc_ids, first_row, row_count, 0)
    start = jnp.sum((doc_ids[None, :] < ids_local[:, None]).astype(I32), 1)
    query_index = first_row + jnp.arange(row_count, dtype=I32)
    position = (query_index - start).astype(F32)
    half_dim = head_dim // 2
    freqs = BASE ** (-jnp.arange(half_dim, dtype=F32) / half_dim)
    angle = position[:, None] * freqs[None, :]
    cosine_rows, sine_rows = jnp.cos(angle), jnp.sin(angle)
    start_rows = jnp.tile(start, local_heads)[None]
    index_rows = jnp.tile(query_index, local_heads)[None]
    info = jnp.stack([first_row, start[0], start[-1], core]).astype(I32)

    tokens = tokens_in.astype(F32)
    normed_in, recip1 = norm_rows(tokens, norm1_gain)
    normed_low = normed_in.astype(BF)
    kv_pre = dense(normed_low, kv_weight)
    key_local = rotate(kv_pre[:, :head_dim], cosine_rows, sine_rows)
    kv_local = jnp.concatenate([key_local, kv_pre[:, head_dim:]], -1).astype(BF)
    kv_all = gather_kv(kv_local, seq_ix)

    latent = dense(normed_low, q_down)
    high, rest = high_low(latent_gain)
    low = (latent_gain - high.astype(F32) - rest.astype(F32)).astype(BF)
    gain_rows = jnp.stack([high, rest, low] + [jnp.zeros_like(high)] * 13)
    gathered = lax.all_gather(
        jnp.concatenate([latent.astype(BF), gain_rows], 0), "rank", axis=1, tiled=True
    ).astype(F32)
    latent_all = gathered[:row_count]
    gain_all = gathered[row_count] + gathered[row_count + 1] + gathered[row_count + 2]
    recip_c = lax.rsqrt(jnp.mean(latent_all * latent_all, -1, keepdims=True) + EPS)
    latent_low = (latent_all * recip_c * gain_all).astype(BF)
    query_pre = dense(latent_low, q_up_own)

    query, attn_vals, log_total = attend(
        info, query_pre, cosine_rows, sine_rows, kv_all, start_rows, index_rows
    )
    attn_low = attn_vals.astype(BF)
    branch = lax.psum_scatter(
        dense(attn_low, out_weight).astype(BF), "rank", scatter_dimension=0, tiled=True
    )
    tokens_rows = lax.dynamic_slice_in_dim(tokens_in, rank_ix * own_rows, own_rows, 0)
    residual = tokens_rows.astype(F32) + branch.astype(F32)
    normed_mid, recip2 = norm_rows(residual, norm2_gain)
    mid_low = lax.all_gather(normed_mid.astype(BF), "rank", axis=0, tiled=True)

    grad_hidden = dense_nt(out_grad, down_weight)
    gate_pre = dense(mid_low, gate_weight)
    up_pre = dense(mid_low, up_weight)
    sigmoid_gate = jax.nn.sigmoid(gate_pre)
    activated = gate_pre * sigmoid_gate
    hidden_low = (activated * up_pre).astype(BF)
    grad_gate_pre = (
        grad_hidden * up_pre * sigmoid_gate * (1.0 + gate_pre * (1.0 - sigmoid_gate))
    ).astype(BF)
    grad_up_pre = (grad_hidden * activated).astype(BF)
    grad_mid = lax.psum_scatter(
        (dense_nt(grad_gate_pre, gate_weight) + dense_nt(grad_up_pre, up_weight)).astype(BF),
        "rank",
        scatter_dimension=0,
        tiled=True,
    ).astype(F32)
    feed_out = lax.psum_scatter(
        dense(hidden_low, down_weight).astype(BF), "rank", scatter_dimension=0, tiled=True
    )
    layer_out = lax.all_gather(
        (residual + feed_out.astype(F32)).astype(BF), "rank", axis=0, tiled=True
    )
    grad_gate = reduce_product(mid_low, grad_gate_pre, seq_ix)
    grad_up = reduce_product(mid_low, grad_up_pre, seq_ix)
    grad_down = reduce_product(hidden_low, out_grad, seq_ix)

    gained_mid = grad_mid * norm2_gain
    stat_mid = jnp.sum(residual * gained_mid, -1, keepdims=True)
    out_grad_rows = lax.dynamic_slice_in_dim(out_grad, rank_ix * own_rows, own_rows, 0)
    grad_residual = (
        out_grad_rows.astype(F32)
        + recip2 * gained_mid
        - residual * recip2**3 * stat_mid / model_width
    )
    grad_norm2 = jnp.sum(grad_mid * residual * recip2, 0)
    grad_branch = lax.all_gather(grad_residual.astype(BF), "rank", axis=0, tiled=True)
    grad_attn_wide = dense_nt(grad_branch, out_weight)
    grad_attn = grad_attn_wide.astype(BF)
    grad_out = reduce_product(attn_low, grad_branch, seq_ix)
    delta = jnp.sum(
        (grad_attn.astype(F32) * attn_vals).reshape(row_count, local_heads, head_dim), -1
    ).T.reshape(1, -1)

    grad_query, near, far = attend_back(
        info, query, grad_attn, delta, log_total, cosine_rows, sine_rows, kv_all, start_rows, index_rows
    )

    chips = seq_count // 2
    kv_shape = (chips, 2, row_count // 2, 2 * head_dim)
    summed = scatter_rows(near.reshape(kv_shape), far.reshape(kv_shape), seq_ix)
    summed = lax.psum(summed.reshape(row_count, 2 * head_dim), "rank").astype(F32)
    key_back = rotate(summed[:, :head_dim], cosine_rows, -sine_rows)
    grad_kv = jnp.concatenate([key_back, summed[:, head_dim:]], -1).astype(BF)

    grad_latent_part = dense_nt(grad_query, q_up_own).astype(BF)
    norm2_rows = jnp.concatenate(high_low(grad_norm2)).reshape(-1, rank_width)
    extra = norm2_rows.shape[0]
    norm2_rows = jnp.pad(norm2_rows, ((0, -extra % 16), (0, 0)))
    over_ranks = lax.psum(jnp.concatenate([grad_latent_part, norm2_rows], 0), "rank").astype(F32)
    grad_latent_in = over_ranks[:row_count]
    grad_norm2 = jnp.sum(
        over_ranks[row_count : row_count + extra].reshape(2, model_width), 0
    )
    gained_latent = grad_latent_in * gain_all
    stat_latent = jnp.sum(latent_all * gained_latent, -1, keepdims=True)
    grad_latent = (
        recip_c * gained_latent - latent_all * recip_c**3 * stat_latent / rank_width
    ).astype(BF)
    own_latent = lambda v: lax.dynamic_slice_in_dim(v, rank_ix * rank_cols, rank_cols, 1)
    grad_latent_gain = jnp.sum(own_latent(grad_latent_in) * latent * recip_c, 0)

    near, far = split_product(grad_query, latent_low, seq_ix)
    piece = scatter_rows(near, far, seq_ix)
    piece = lax.all_to_all(piece, "rank", 2, 0, tiled=True)
    piece = piece.reshape(rank_count * 2, piece.shape[1], rank_cols)
    whole = lax.all_gather(piece, "seq", axis=0, tiled=False)
    whole = whole.reshape(chips, 2, rank_count, 2, piece.shape[1], rank_cols)
    grad_q_up = jnp.transpose(whole, (5, 2, 1, 3, 0, 4)).reshape(rank_cols, -1).astype(F32)

    col_count = model_width // rank_count
    col_start = rank_ix * col_count
    cols = lambda v: lax.dynamic_slice_in_dim(v, col_start, col_count, v.ndim - 1)
    q_down_rows = lax.all_to_all(q_down, "rank", 0, 1, tiled=True)
    kv_rows = lax.dynamic_slice_in_dim(kv_weight, col_start, col_count, 0)
    grad_normed = dense_nt(grad_latent, q_down_rows) + dense_nt(grad_kv, kv_rows)
    norm1_stat = (
        jnp.sum(grad_latent.astype(F32) * latent_all, -1, keepdims=True)
        + jnp.sum(grad_kv.astype(F32) * kv_pre, -1, keepdims=True)
    ) / recip1
    tokens_own = cols(tokens_in).astype(F32)
    grad_in = (
        cols(grad_branch).astype(F32)
        + recip1 * cols(norm1_gain) * grad_normed
        - tokens_own * recip1**3 * norm1_stat / model_width
    )
    grad_norm1 = jnp.sum(grad_normed * tokens_own * recip1, 0)

    grad_q_down = lax.psum(
        dense_tn(normed_low, own_latent(grad_latent)).astype(BF), "seq"
    ).astype(F32)
    grad_kv_weight = dense_tn(cols(normed_low), grad_kv).astype(BF)
    small = jnp.concatenate([grad_norm1, grad_latent_gain, grad_norm2])
    small = jnp.concatenate(high_low(small)).reshape(2, -1)
    count = small.shape[1]
    kv_cols = grad_kv_weight.shape[1]
    small_rows = jnp.pad(small.reshape(-1), (0, -2 * count % (16 * kv_cols))).reshape(-1, kv_cols)
    last = lax.psum(jnp.concatenate([grad_kv_weight, small_rows], 0), "seq").astype(F32)
    grad_kv_weight = last[:col_count]
    small = jnp.sum(last[col_count:].reshape(-1)[: 2 * count].reshape(2, count), 0)
    grad_norm1 = small[:col_count]
    grad_latent_gain = small[col_count : col_count + rank_cols]
    grad_norm2 = small[col_count + rank_cols :]
    return (
        layer_out,
        grad_in,
        grad_norm1,
        grad_q_down,
        grad_latent_gain,
        grad_q_up,
        grad_kv_weight,
        grad_out,
        grad_norm2,
        grad_gate,
        grad_up,
        grad_down,
    )


def solution(mesh):
    return jax.shard_map(
        per_device,
        mesh=mesh,
        in_specs=(
            P("seq", None),
            P(),
            P(None, "rank"),
            P("rank"),
            P("rank", None),
            P(),
            P("rank", None),
            P(),
            P(None, "rank"),
            P(None, "rank"),
            P("rank", None),
            P(),
            P("seq", None),
        ),
        out_specs=(
            P("seq", None),
            P("seq", "rank"),
            P("rank"),
            P(None, "rank"),
            P("rank"),
            P("rank", None),
            P("rank", None),
            P("rank", None),
            P(),
            P(None, "rank"),
            P(None, "rank"),
            P("rank", None),
        ),
        check_vma=False,
    )
```

```python
import functools

import jax
import jax.numpy as jnp
from jax import lax
from jax.experimental import pallas as pl
from jax.experimental.pallas import tpu as pltpu
from jax.sharding import PartitionSpec as P

EPS = 1e-05
BASE = 10000.0
NEG = -1e30
LOG2E = 1.4426950408889634
BF = jnp.bfloat16
F32 = jnp.float32
I32 = jnp.int32
LANES = 128

def norm_rows(values, gain):
    recip = lax.rsqrt(jnp.mean(values * values, -1, keepdims=True) + EPS)
    return (values * recip * gain, recip)


def rotate(values, cosine_rows, sine_rows):
    half_dim = values.shape[-1] // 2
    front_half = values[..., :half_dim]
    back_half = values[..., half_dim:]
    return jnp.concatenate(
        [
            front_half * cosine_rows - back_half * sine_rows,
            front_half * sine_rows + back_half * cosine_rows,
        ],
        -1,
    )


def dense(left, right):
    return jnp.dot(left, right, preferred_element_type=F32)


def dense_tn(left, right):
    return lax.dot_general(left, right, (((0,), (0,)), ((), ())), preferred_element_type=F32)


def dense_nt(left, right):
    return lax.dot_general(left, right, (((1,), (1,)), ((), ())), preferred_element_type=F32)


def key_block(key_count, most):
    for size in (1536, 1024, 512, 256, 128):
        if size <= most and key_count % size == 0:
            return size
    return key_count


def row_tile(rows):
    for parts in (3, 2):
        if rows % (parts * 128) == 0:
            return rows // parts
    return rows


def over_key_blocks(info_ref, size, tokens, run):
    first, low, high = info_ref[0], info_ref[1], info_ref[2]
    begin = low // size
    whole_end = jnp.maximum(first // size, begin)
    whole_begin = jnp.clip((high + size - 1) // size, begin, whole_end)
    end = (first + tokens + size - 1) // size
    lax.fori_loop(begin, whole_begin, lambda j, c: run(j, True), None)
    lax.fori_loop(whole_begin, whole_end, lambda j, c: run(j, False), None)
    lax.fori_loop(whole_end, end, lambda j, c: run(j, True), None)


def attend_kernel(
    size, tile, heads, places, info_ref, pre_ref, cos_ref, sin_ref, first_ref, *refs
):
    pieces_in = refs[: len(places)]
    query_ref, out_ref, low_ref, log_ref, kv_ref = refs[len(places) : len(places) + 5]
    max_ref, sum_ref, acc_ref, scores_ref, start_ref, index_ref, sems = refs[len(places) + 5 :]
    tokens = pre_ref.shape[0]
    copies = []
    for n, (mask, offset) in enumerate(places):
        at = lax.bitwise_xor(info_ref[5], mask) * tokens + offset if mask is not None else 0
        rows = pl.ds(pl.multiple_of(at, 16), pieces_in[n].shape[0])
        copies.append(pltpu.make_async_copy(pieces_in[n], kv_ref.at[rows, :], sems.at[n]))
    for copy in copies:
        copy.start()
    width = kv_ref.shape[1] // 2
    half = width // 2
    lanes = max_ref.shape[1]
    scale = width**-0.5 * LOG2E
    cosine, sine = cos_ref[...], sin_ref[...]
    for h in range(heads):
        front = pre_ref[:, h * width : h * width + half]
        back = pre_ref[:, h * width + half : (h + 1) * width]
        rows = slice(h * tokens, (h + 1) * tokens)
        query_ref[rows, :half] = (front * cosine - back * sine).astype(BF)
        query_ref[rows, half:] = (front * sine + back * cosine).astype(BF)
        start_ref[rows, :] = first_ref[...]
        index_ref[rows, :] = info_ref[0] + lax.broadcasted_iota(I32, (tokens, lanes), 0)
    for copy in copies:
        copy.wait()
    pieces = [slice(n * lanes, (n + 1) * lanes) for n in range(size // lanes)]
    for i in range(heads * tokens // tile):
        r = slice(i * tile, (i + 1) * tile)
        max_ref[...] = jnp.full(max_ref.shape, NEG, F32)
        sum_ref[...] = jnp.zeros(sum_ref.shape, F32)
        acc_ref[...] = jnp.zeros(acc_ref.shape, F32)

        def score(j, masked, r=r):
            base = pl.multiple_of(j * size, size)
            scores = dense_nt(query_ref[r, :], kv_ref[pl.ds(base, size), :width])
            most = max_ref[...]
            lane = lax.broadcasted_iota(I32, max_ref.shape, 1)
            for n, piece in enumerate(pieces):
                part = scores[:, piece]
                if masked:
                    at = lane + (base + n * lanes)
                    allowed = (at >= start_ref[r, :]) & (at <= index_ref[r, :])
                    part = jnp.where(allowed, part, NEG)
                scores_ref[j, :, piece] = part
                most = jnp.maximum(most, part)
            max_ref[...] = most
            return None

        over_key_blocks(info_ref, size, tokens, score)
        most = jnp.max(max_ref[...], 1, keepdims=True) * scale
        max_ref[...] = jnp.broadcast_to(most, max_ref.shape)

        def mix(j, carry):
            base = pl.multiple_of(j * size, size)
            most, total = max_ref[...], sum_ref[...]
            probs = []
            for piece in pieces:
                prob = jnp.exp2(scores_ref[j, :, piece] * scale - most)
                total = total + prob
                probs.append(prob.astype(BF))
            sum_ref[...] = total
            acc_ref[...] += dense(jnp.concatenate(probs, 1), kv_ref[pl.ds(base, size), width:])
            return carry

        end = (info_ref[0] + tokens + size - 1) // size
        lax.fori_loop(info_ref[1] // size, end, mix, None)
        total = jnp.sum(sum_ref[...], 1, keepdims=True)
        log_ref[:, r] = jnp.broadcast_to(most + jnp.log2(total), max_ref.shape).T[0:1, :]
        out = acc_ref[...] * (1.0 / total)
        at = i * tile
        while at < (i + 1) * tile:
            h = at // tokens
            stop = min((i + 1) * tile, (h + 1) * tokens)
            rows, cols = slice(at - h * tokens, stop - h * tokens), slice(h * width, (h + 1) * width)
            part = out[at - i * tile : stop - i * tile, :]
            out_ref[rows, cols] = part
            low_ref[rows, cols] = part.astype(BF)
            at = stop


def in_vmem(count):
    return [pl.BlockSpec(memory_space=pltpu.VMEM) for _ in range(count)]


def attend(info, query_pre, cosine, sine, start, pieces):
    tokens, all_heads = query_pre.shape
    width = pieces[0][0].shape[1] // 2
    keys = sum(piece[0].shape[0] for piece in pieces)
    rows = tokens * (all_heads // width)
    size, tile = key_block(keys, 1536), row_tile(rows)
    start = jnp.broadcast_to(start[:, None], (tokens, LANES))
    return pl.pallas_call(
        functools.partial(
            attend_kernel, size, tile, all_heads // width, [piece[1:] for piece in pieces]
        ),
        out_shape=(
            jax.ShapeDtypeStruct((rows, width), BF),
            jax.ShapeDtypeStruct((tokens, all_heads), F32),
            jax.ShapeDtypeStruct((tokens, all_heads), BF),
            jax.ShapeDtypeStruct((1, rows), F32),
            jax.ShapeDtypeStruct((keys, 2 * width), BF),
        ),
        in_specs=[pl.BlockSpec(memory_space=pltpu.SMEM)]
        + in_vmem(4)
        + [pl.BlockSpec(memory_space=pl.ANY)] * len(pieces),
        out_specs=tuple(in_vmem(5)),
        scratch_shapes=[
            pltpu.VMEM((tile, LANES), F32),
            pltpu.VMEM((tile, LANES), F32),
            pltpu.VMEM((tile, width), F32),
            pltpu.VMEM((keys // size, tile, size), F32),
            pltpu.VMEM((rows, LANES), I32),
            pltpu.VMEM((rows, LANES), I32),
            pltpu.SemaphoreType.DMA((len(pieces),)),
        ],
        compiler_params=pltpu.CompilerParams(vmem_limit_bytes=56 * 2**20),
        cost_estimate=brief(0),
        name="attend",
    )(info, query_pre, cosine, sine, start, *[piece[0] for piece in pieces])


def attend_back_kernel(
    size, tile, heads, by_axis, info_ref, query_ref, grad_ref, out_ref, log_ref, cos_ref, sin_ref, kv_ref, start_ref, index_ref,
    gq_ref, near_ref, far_ref, gout_ref, gk_ref, gv_ref, gqt_ref, dots_ref,
):
    tokens = grad_ref.shape[0]
    width = kv_ref.shape[1] // 2
    half = width // 2
    scale = width**-0.5
    for h in range(heads):
        gout = grad_ref[:, h * width : (h + 1) * width]
        gout_ref[h * tokens : (h + 1) * tokens, :] = gout
        dots = gout.astype(F32) * out_ref[:, h * width : (h + 1) * width]
        dots_ref[h * tokens : (h + 1) * tokens, :] = dots[:, :half] + dots[:, half:]
    delta = jnp.sum(dots_ref[...].T, 0, keepdims=True)
    gk_ref[...] = jnp.zeros(gk_ref.shape, F32)
    gv_ref[...] = jnp.zeros(gv_ref.shape, F32)
    gqt_ref[...] = jnp.zeros(gqt_ref.shape, F32)

    def run(j, masked):
        base = pl.multiple_of(j * size, size)
        at_keys = pl.ds(base, size)
        keys = kv_ref[at_keys, :width]
        values = kv_ref[at_keys, width:]
        for i in range(heads * tokens // tile):
            r = slice(i * tile, (i + 1) * tile)
            query, gout = query_ref[r, :], gout_ref[r, :]
            probs = jnp.exp2(dense_nt(keys, query) * (scale * LOG2E) - log_ref[:, r])
            if masked:
                at = base + lax.broadcasted_iota(I32, (size, tile), 0)
                allowed = (at >= start_ref[:, r]) & (at <= index_ref[:, r])
                probs = jnp.where(allowed, probs, 0.0)
            gscores = (probs * (dense_nt(values, gout) - delta[:, r])).astype(BF)
            gv_ref[at_keys, :] += dense(probs.astype(BF), gout)
            gk_ref[at_keys, :] += dense(gscores, query)
            gqt_ref[:, r] += dense_tn(keys, gscores)
        return None

    over_key_blocks(info_ref, size, tokens, run)
    mine = info_ref[3]
    part = tokens // 2
    for s in range(kv_ref.shape[0] // part):
        rows = slice(s * part, (s + 1) * part)
        chip = s // 4
        if by_axis and s % 2 == 0:
            chip = chip % 2 * 2 + chip // 2
        gk = (gk_ref[rows, :] * scale).astype(BF)
        gv = gv_ref[rows, :].astype(BF)

        @pl.when(mine == s // 2 % 2)
        def _(s=s, chip=chip, gk=gk, gv=gv):
            near_ref[s % 2, chip, :, :width] = gk
            near_ref[s % 2, chip, :, width:] = gv

        @pl.when(mine != s // 2 % 2)
        def _(s=s, chip=chip, gk=gk, gv=gv):
            far_ref[s % 2, chip, :, :width] = gk
            far_ref[s % 2, chip, :, width:] = gv

    gq = (gqt_ref[...] * scale).T.astype(BF).astype(F32)
    cosine, sine = cos_ref[...], sin_ref[...]
    for h in range(heads):
        front = gq[h * tokens : (h + 1) * tokens, :half]
        back = gq[h * tokens : (h + 1) * tokens, half:]
        gq_ref[:, h * width : h * width + half] = (front * cosine + back * sine).astype(BF)
        gq_ref[:, h * width + half : (h + 1) * width] = (back * cosine - front * sine).astype(BF)


def attend_back(info, query, grad, out, log, cosine, sine, kv, start, index, by_axis):
    tokens, all_heads = grad.shape
    keys, width = kv.shape[0], kv.shape[1] // 2
    rows = tokens * (all_heads // width)
    blocks = keys // tokens
    return pl.pallas_call(
        functools.partial(
            attend_back_kernel, key_block(keys, 512), row_tile(rows), all_heads // width, by_axis
        ),
        out_shape=(
            jax.ShapeDtypeStruct((tokens, all_heads), BF),
            jax.ShapeDtypeStruct((2, blocks // 2, tokens // 2, 2 * width), BF),
            jax.ShapeDtypeStruct((2, blocks // 2, tokens // 2, 2 * width), BF),
        ),
        in_specs=[pl.BlockSpec(memory_space=pltpu.SMEM)] + in_vmem(9),
        out_specs=tuple(in_vmem(3)),
        scratch_shapes=[
            pltpu.VMEM((rows, width), BF),
            pltpu.VMEM((keys, width), F32),
            pltpu.VMEM((keys, width), F32),
            pltpu.VMEM((width, rows), F32),
            pltpu.VMEM((rows, width // 2), F32),
        ],
        compiler_params=pltpu.CompilerParams(vmem_limit_bytes=56 * 2**20),
        cost_estimate=brief(0),
        name="attend_back",
    )(info, query, grad, out, log, cosine, sine, kv, start, index)


def feed_kernel(tile, mid_ref, grad_ref, gate_ref, up_ref, hidden_ref, both_ref, part_ref):
    width = gate_ref.shape[1]

    def run(i, carry):
        rows = pl.ds(pl.multiple_of(i * tile, tile), tile)
        mid = mid_ref[rows, :]
        gate = dense(mid, gate_ref[...])
        up = dense(mid, up_ref[...])
        grad = grad_ref[rows, :]
        sigmoid = 1.0 / (1.0 + jnp.exp(-gate))
        active = gate * sigmoid
        hidden_ref[rows, :] = (active * up).astype(BF)
        grad_gate = (grad * up * sigmoid * (1.0 + gate * (1.0 - sigmoid))).astype(BF)
        grad_up = (grad * active).astype(BF)
        both_ref[rows, :width] = grad_gate
        both_ref[rows, width:] = grad_up
        part = dense_nt(grad_gate, gate_ref[...]) + dense_nt(grad_up, up_ref[...])
        part_ref[rows, :] = part.astype(BF)
        return carry

    lax.fori_loop(0, mid_ref.shape[0] // tile, run, None)


def feed_forward(mid, grad, gate, up):
    rows, model = mid.shape
    width = gate.shape[1]
    tile = next(t for t in (288, 192, 144, 96, 64, 48, 32, 16, rows) if rows % t == 0)
    return pl.pallas_call(
        functools.partial(feed_kernel, tile),
        out_shape=(
            jax.ShapeDtypeStruct((rows, width), BF),
            jax.ShapeDtypeStruct((rows, 2 * width), BF),
            jax.ShapeDtypeStruct((rows, model), BF),
        ),
        in_specs=in_vmem(4),
        out_specs=tuple(in_vmem(3)),
        compiler_params=pltpu.CompilerParams(vmem_limit_bytes=40 * 2**20),
        cost_estimate=brief(20),
        name="feed_forward",
    )(mid, grad, gate, up)


class Order:
    last = None


def brief(micros):
    return pl.CostEstimate(flops=int(micros * 1e8), bytes_accessed=0, transcendentals=0)


def call(kernel, outs, args, name, micros=0, scratch=(), grid=None, in_specs=None, out_specs=None, prefetch=None):
    out_shape = tuple(jax.ShapeDtypeStruct(*out) for out in outs)
    prefetch = in_order(prefetch)
    params = dict(
        out_shape=out_shape,
        compiler_params=pltpu.CompilerParams(vmem_limit_bytes=56 * 2**20),
        cost_estimate=brief(micros),
        name=name,
    )
    outs = placed_call(kernel, out_shape, args, params, scratch, grid, in_specs, out_specs, prefetch)
    Order.last = outs[0]
    return outs


def in_order(info):
    return info if Order.last is None else after(info, Order.last)


def placed_call(kernel, out_shape, args, params, scratch, grid, in_specs, out_specs, prefetch):
    if grid is None:
        return pl.pallas_call(
            kernel,
            in_specs=[pl.BlockSpec(memory_space=pltpu.SMEM)] + in_vmem(len(args)),
            out_specs=tuple(in_vmem(len(out_shape))),
            scratch_shapes=list(scratch),
            **params,
        )(prefetch, *args)
    return pl.pallas_call(
        kernel,
        grid_spec=pltpu.PrefetchScalarGridSpec(
            num_scalar_prefetch=1,
            grid=grid,
            in_specs=in_specs,
            out_specs=tuple(out_specs),
            scratch_shapes=list(scratch),
        ),
        **params,
    )(prefetch, *args)


def once(shape, index):
    return pl.BlockSpec(shape, index, pipeline_mode=pl.Buffered(1))


def at_block(index, size):
    return pl.ds(pl.multiple_of(index * size, size), size)


CORE, RANK, SEQ = 3, 4, 5


def ahead(info_ref, shift, ranks):
    return lax.rem(info_ref[RANK] + shift, ranks)


def behind(info_ref, shift, ranks):
    return lax.rem(info_ref[RANK] + ranks - shift, ranks)


def chip_of(info_ref):
    return lax.div(info_ref[SEQ], 2)


def rank_blocks(info, index):
    return lambda i, info_ref: index(info_ref[RANK])


def project_kernel(
    info_ref, tokens_ref, gain_ref, down_ref, kv_weight_ref, latent_gain_ref, normed_ref, recip_ref, kv_ref, low_ref
):
    values = tokens_ref[...].astype(F32)
    normed, recip = norm_rows(values, gain_ref[...])
    normed_ref[...] = normed.astype(BF)
    recip_ref[...] = jnp.broadcast_to(recip, recip_ref.shape)
    rows = normed_ref.shape[0]
    low_ref[at_block(pl.program_id(0), rows), :] = dense(normed_ref[...], down_ref[...]).astype(BF)

    @pl.when(pl.program_id(0) == 0)
    def _():
        rest = latent_gain_ref[...]
        parts = []
        for _ in range(3):
            parts.append(rest.astype(BF))
            rest = rest - parts[-1].astype(F32)
        parts.append(jnp.zeros((EXTRA - 3, rest.shape[1]), BF))
        low_ref[low_ref.shape[0] - EXTRA :, :] = jnp.concatenate(parts, 0)

    kv_ref[...] = dense(normed_ref[...], kv_weight_ref[...])


EXTRA = 16


def project(info, tokens, gain, q_down, kv_weight, latent_gain):
    rows, model = tokens.shape
    tile = rows // 2
    widths = ((model, BF), (LANES, F32), (kv_weight.shape[1], F32))
    low = (rows + EXTRA, q_down.shape[1])
    return call(
        project_kernel,
        [((rows, width), dtype) for width, dtype in widths] + [(low, BF)],
        (tokens, gain.reshape(1, -1), q_down, kv_weight, latent_gain.reshape(1, -1)),
        "project",
        grid=(2,),
        in_specs=[
            pl.BlockSpec((tile, model), lambda i, w: (i, 0)),
            once((1, model), lambda i, w: (0, 0)),
            once(q_down.shape, lambda i, w: (0, 0)),
            once(kv_weight.shape, lambda i, w: (0, 0)),
            once((1, q_down.shape[1]), lambda i, w: (0, 0)),
        ],
        out_specs=[pl.BlockSpec((tile, width), lambda i, w: (i, 0)) for width, _ in widths]
        + [pl.BlockSpec(low, lambda i, w: (0, 0))],
        prefetch=info,
    )


def turn_kernel(info_ref, kv_ref, cos_ref, sin_ref, out_ref):
    half = cos_ref.shape[1]
    front, back = kv_ref[:, :half], kv_ref[:, half : 2 * half]
    cosine, sine = cos_ref[...], sin_ref[...]
    out_ref[:, :half] = (front * cosine - back * sine).astype(BF)
    out_ref[:, half : 2 * half] = (front * sine + back * cosine).astype(BF)
    out_ref[:, 2 * half :] = kv_ref[:, 2 * half :].astype(BF)


def turn(info, kv_pre, cosine, sine):
    return call(turn_kernel, [(kv_pre.shape, BF)], (kv_pre, cosine, sine), "turn", prefetch=info)[0]


def query_kernel(info_ref, latent_ref, own_ref, other_ref, low_ref, recip_ref, gain_ref, query_ref):
    rows = low_ref.shape[0]
    parts = latent_ref[rows:, :].astype(F32)
    gain_ref[...] = parts[0:1] + parts[1:2] + parts[2:3]
    normed, recip = norm_rows(latent_ref[:rows, :].astype(F32), gain_ref[...])
    low_ref[...] = normed.astype(BF)
    recip_ref[...] = jnp.broadcast_to(recip, recip_ref.shape)
    half = own_ref.shape[1]
    ranks = 4
    cols = latent_ref.shape[1] // ranks
    totals = [0.0, 0.0]
    for s in range(ranks):
        left = low_ref[:, at_block(behind(info_ref, s, ranks), cols)]
        for n, ref in enumerate((own_ref, other_ref)):
            totals[n] = totals[n] + dense(left, ref[s * cols : (s + 1) * cols, :])
    core = info_ref[CORE]
    query_ref[:, at_block(core, half)] = totals[0]
    query_ref[:, at_block(1 - core, half)] = totals[1]


def queries(info, latent, own, other):
    rows, width = latent.shape[0] - EXTRA, latent.shape[1]
    return call(
        query_kernel,
        [((rows, width), BF), ((rows, LANES), F32), ((1, width), F32), ((rows, 2 * own.shape[1]), F32)],
        (latent, own, other),
        "queries",
        prefetch=info,
    )


def latent_part_kernel(info_ref, grad_ref, own_ref, other_ref, *refs):
    outs, all_ref = refs[:-1], refs[-1]
    ranks, rows = len(outs), outs[0].shape[0]
    half, cols = own_ref.shape[1], own_ref.shape[0] // ranks
    core = info_ref[CORE]
    own_grad = grad_ref[:, at_block(core, half)]
    other_grad = grad_ref[:, at_block(1 - core, half)]
    for s in range(ranks):
        part = slice(s * cols, (s + 1) * cols)
        out = dense_nt(own_grad, own_ref[part, :]) + dense_nt(other_grad, other_ref[part, :])
        all_ref[:, at_block(behind(info_ref, s, ranks), cols)] = out.astype(BF)
    for s in range(ranks):
        outs[s][...] = all_ref[at_block(ahead(info_ref, s, ranks), rows), :]


def latent_parts(info, grad, own, other, ranks):
    rows, width = grad.shape[0], own.shape[0]
    return call(
        latent_part_kernel,
        [((rows // ranks, width), BF)] * ranks,
        (grad, own, other),
        "latent_parts",
        scratch=[pltpu.VMEM((rows, width), BF)],
        prefetch=info,
    )


def latent_back_kernel(info_ref, latent_ref, recip_ref, gain_ref, *refs):
    parts, (grad_ref, gain_grad_ref) = refs[:-2], refs[-2:]
    grad_in = sum(part[...].astype(F32) for part in parts)
    latent = latent_ref[...].astype(F32)
    recip = recip_ref[:, 0:1]
    gained = grad_in * gain_ref[...]
    stat = jnp.sum(latent * gained, -1, keepdims=True)
    grad = recip * gained - latent * (recip * recip * recip * stat / latent.shape[1])
    grad_ref[...] = grad.astype(BF)
    gain_grad_ref[...] = jnp.sum(grad_in * latent * recip, 0, keepdims=True)


def latent_back(info, latent, recip, gain, parts):
    rows, width = parts[0].shape
    return call(
        latent_back_kernel,
        [((rows, width), BF), ((1, width), F32)],
        (latent, recip, gain, *parts),
        "latent_back",
        grid=(1,),
        in_specs=[
            pl.BlockSpec((rows, width), lambda i, w: (w[RANK], 0)),
            pl.BlockSpec((rows, LANES), lambda i, w: (w[RANK], 0)),
            pl.BlockSpec((1, width), lambda i, w: (0, 0)),
        ]
        + [pl.BlockSpec((rows, width), lambda i, w: (0, 0)) for _ in parts],
        out_specs=[
            pl.BlockSpec((rows, width), lambda i, w: (0, 0)),
            pl.BlockSpec((1, width), lambda i, w: (0, 0)),
        ],
        prefetch=info,
    )


def kv_back_kernel(info_ref, cos_ref, sin_ref, *refs):
    parts, out_ref = refs[:-1], refs[-1]
    total = sum(part[...].astype(F32) for part in parts).astype(BF).astype(F32)
    half = cos_ref.shape[1]
    front, back = total[:, :half], total[:, half : 2 * half]
    cosine, sine = cos_ref[...], sin_ref[...]
    out_ref[:, :half] = (front * cosine + back * sine).astype(BF)
    out_ref[:, half : 2 * half] = (back * cosine - front * sine).astype(BF)
    out_ref[:, 2 * half :] = total[:, 2 * half :].astype(BF)


def kv_back(info, cosine, sine, parts):
    rows, width = parts[0].shape
    return call(
        kv_back_kernel,
        [((rows, width), BF)],
        (cosine, sine, *parts),
        "kv_back",
        grid=(1,),
        in_specs=[pl.BlockSpec((rows, cosine.shape[1]), lambda i, w: (w[RANK], 0))] * 2
        + [pl.BlockSpec((rows, width), lambda i, w: (0, 0)) for _ in parts],
        out_specs=[pl.BlockSpec((rows, width), lambda i, w: (0, 0))],
        prefetch=info,
    )[0]


def mid_kernel(info_ref, branch_ref, tokens_ref, gain_ref, residual_ref, mid_ref, recip_ref):
    residual = tokens_ref[...].astype(F32) + branch_ref[...].astype(F32)
    normed, recip = norm_rows(residual, gain_ref[...])
    residual_ref[...] = residual
    mid_ref[...] = normed.astype(BF)
    recip_ref[...] = jnp.broadcast_to(recip, recip_ref.shape)


def mid_norm(info, branch, tokens, gain):
    rows, model = branch.shape
    whole = pl.BlockSpec((rows, model), lambda i, w: (0, 0))
    return call(
        mid_kernel,
        [((rows, model), F32), ((rows, model), BF), ((rows, LANES), F32)],
        (branch, tokens, gain.reshape(1, -1)),
        "mid_norm",
        grid=(1,),
        in_specs=[
            whole,
            pl.BlockSpec((rows, model), lambda i, w: (w[RANK], 0)),
            pl.BlockSpec((1, model), lambda i, w: (0, 0)),
        ],
        out_specs=[whole, whole, pl.BlockSpec((rows, LANES), lambda i, w: (0, 0))],
        prefetch=info,
    )


def mid_back_kernel(info_ref, grad_ref, residual_ref, recip_ref, gain_ref, out_grad_ref, branch_ref, gain_grad_ref):
    grad = grad_ref[...].astype(F32)
    residual = residual_ref[...]
    recip = recip_ref[:, 0:1]
    gained = grad * gain_ref[...]
    stat = jnp.sum(residual * gained, -1, keepdims=True)
    out = out_grad_ref[...].astype(F32) + recip * gained
    out = out - residual * (recip * recip * recip * stat / residual.shape[1])
    branch_ref[...] = out.astype(BF)
    gain_grad_ref[...] = jnp.sum(grad * residual * recip, 0, keepdims=True)


def mid_back(info, grad, residual, recip, gain, out_grad):
    rows, model = grad.shape
    whole = pl.BlockSpec((rows, model), lambda i, w: (0, 0))
    return call(
        mid_back_kernel,
        [((rows, model), BF), ((1, model), F32)],
        (grad, residual, recip, gain.reshape(1, -1), out_grad),
        "mid_back",
        grid=(1,),
        in_specs=[
            whole,
            whole,
            pl.BlockSpec((rows, LANES), lambda i, w: (0, 0)),
            pl.BlockSpec((1, model), lambda i, w: (0, 0)),
            pl.BlockSpec((rows, model), lambda i, w: (w[RANK], 0)),
        ],
        out_specs=[whole, pl.BlockSpec((1, model), lambda i, w: (0, 0))],
        prefetch=info,
    )


def matmul_kernel(dims, info_ref, left_ref, right_ref, *refs):
    out = lax.dot_general(left_ref[...], right_ref[...], (dims, ((), ())), preferred_element_type=F32)
    if len(refs) == 1:
        refs[0][...] = out.astype(BF)
        return
    outs, all_ref = refs[:-1], refs[-1]
    all_ref[...] = out.astype(BF)
    for s, out_ref in enumerate(outs):
        out_ref[...] = all_ref[at_block(ahead(info_ref, s, len(outs)), out_ref.shape[0]), :]


def matmul(info, left, right, transposed=False, parts=1):
    rows, depth = left.shape
    cols = right.shape[0 if transposed else 1]
    tile = next(t for t in ((512, 256, LANES) if transposed else (1024, 512, 256, LANES)) if cols % t == 0)
    if transposed:
        dims, spec = ((1,), (1,)), pl.BlockSpec((tile, depth), lambda i, w: (i, 0))
    else:
        dims, spec = ((1,), (0,)), pl.BlockSpec((depth, tile), lambda i, w: (0, i))
    outs = call(
        functools.partial(matmul_kernel, dims),
        [((rows // parts, cols), BF)] * parts,
        (left, right),
        "matmul",
        scratch=[pltpu.VMEM((rows, tile), BF)] if parts > 1 else [],
        grid=(cols // tile,),
        in_specs=[once((rows, depth), lambda i, w: (0, 0)), spec],
        out_specs=[pl.BlockSpec((rows // parts, tile), lambda i, w: (0, i))] * parts,
        prefetch=info,
    )
    return outs if parts > 1 else outs[0]


def quarter_order(info_ref):
    bit_x = lax.rem(chip_of(info_ref), 2)
    bit_y = lax.div(chip_of(info_ref), 2)
    return 1 - bit_x, 3 - bit_y, bit_x, 2 + bit_y


def product_kernel(counts, info_ref, *refs):
    outs, all_ref = refs[4 * len(counts) : 4 * len(counts) + 4], refs[-1]
    order = quarter_order(info_ref)
    rows = outs[0].shape[0]
    first = 0
    for n, count in enumerate(counts):
        own, other, own_right, other_right = refs[4 * n : 4 * n + 4]
        step = pl.program_id(0)

        def mixed(cols):
            out = dense_tn(own[:, cols], own_right[...])
            return (out + dense_tn(other[:, cols], other_right[...])).astype(BF)

        @pl.when((step >= first) & (step < first + count))
        def _():
            if rows >= 256:
                for out_ref, at in zip(outs, order):
                    out_ref[...] = mixed(at_block(at, rows))
            else:
                all_ref[...] = mixed(slice(None))
                for out_ref, at in zip(outs, order):
                    out_ref[...] = all_ref[at_block(at, rows), :]

        first += count


def pair_products(info, terms, tile):
    tokens, rows = terms[0][0].shape[0], terms[0][0].shape[1] // 2
    counts = [term[2].shape[1] // tile for term in terms]
    specs, args, first = [], [], 0
    for term, count in zip(terms, counts):
        specs += [once((tokens, rows), lambda i, w: (0, w[CORE]))] * 2
        place = lambda i, w, first=first, count=count: (0, jnp.clip(i - first, 0, count - 1))
        specs += [pl.BlockSpec((tokens, tile), place)] * 2
        args += term
        first += count
    return call(
        functools.partial(product_kernel, counts),
        [((rows // 4, first * tile), BF)] * 4,
        args,
        "pair_products",
        scratch=[pltpu.VMEM((rows, tile) if rows < 1024 else (16, LANES), BF)],
        grid=(first,),
        in_specs=specs,
        out_specs=[pl.BlockSpec((rows // 4, tile), lambda i, w: (0, i))] * 4,
        prefetch=info,
    )


def add_low(left, right):
    return (left.astype(F32) + right.astype(F32)).astype(BF)


def fold_near_kernel(info_ref, near_ref, got_ref, *outs):
    for out_ref, at in zip(outs, quarter_order(info_ref)):
        p, bit = lax.div(at, 2), lax.rem(at, 2)
        for other in range(2):
            chip = bit * 2 + other
            out_ref[other] = add_low(near_ref[p, chip], got_ref[p, chip])


def fold_near(info, near, got):
    _, chips, rows, cols = near.shape
    tile = rows // 3
    return call(
        fold_near_kernel,
        [((2, rows, cols), BF)] * 4,
        (near, got),
        "fold_near",
        grid=(3,),
        in_specs=[pl.BlockSpec((2, chips, tile, cols), lambda i, w: (0, 0, i, 0))] * 2,
        out_specs=[pl.BlockSpec((2, tile, cols), lambda i, w: (0, i, 0))] * 4,
        prefetch=info,
    )


def fold_first_kernel(info_ref, keep_first, got_first, keep_last, got_last, *outs):
    bit_x = lax.rem(chip_of(info_ref), 2)
    bit_y = lax.div(chip_of(info_ref), 2)
    outs[0][...] = add_low(keep_first[1 - bit_y], got_first[1 - bit_y])
    outs[1][...] = add_low(keep_last[1 - bit_x], got_last[1 - bit_x])
    outs[2][...] = add_low(keep_first[bit_y], got_first[bit_y])
    outs[3][...] = add_low(keep_last[bit_x], got_last[bit_x])


def fold_first(info, arrays, steps, micros=0):
    rows, cols = arrays[0].shape[1:]
    tile = rows // steps
    return call(
        fold_first_kernel,
        [((rows, cols), BF)] * 4,
        arrays,
        "fold_first",
        micros,
        grid=(steps,),
        in_specs=[pl.BlockSpec((2, tile, cols), lambda i, w: (0, i, 0))] * 4,
        out_specs=[pl.BlockSpec((tile, cols), lambda i, w: (i, 0))] * 4,
        prefetch=info,
    )


def fold_last_kernel(info_ref, keep_first, got_first, keep_last, got_last, out_ref):
    out_ref[0] = add_low(keep_first[...], got_first[...])
    out_ref[1] = add_low(keep_last[...], got_last[...])


def fold_last(info, arrays, steps):
    rows, cols = arrays[0].shape
    tile = rows // steps
    return call(
        fold_last_kernel,
        [((2, rows, cols), BF)],
        arrays,
        "fold_last",
        grid=(steps,),
        in_specs=[pl.BlockSpec((tile, cols), lambda i, w: (i, 0))] * 4,
        out_specs=[pl.BlockSpec((2, tile, cols), lambda i, w: (0, i, 0))],
        prefetch=info,
    )[0]


def fold_kv_kernel(info_ref, keep_first, got_first, keep_last, got_last, *refs):
    outs, all_ref = refs[:-1], refs[-1]
    half = keep_first.shape[0]
    all_ref[:half, :] = add_low(keep_first[...], got_first[...])
    all_ref[half:, :] = add_low(keep_last[...], got_last[...])
    for s, out_ref in enumerate(outs):
        out_ref[...] = all_ref[at_block(ahead(info_ref, s, len(outs)), out_ref.shape[0]), :]


def fold_kv(info, arrays, ranks):
    rows, cols = arrays[0].shape
    return call(
        fold_kv_kernel,
        [((2 * rows // ranks, cols), BF)] * ranks,
        arrays,
        "fold_kv",
        scratch=[pltpu.VMEM((2 * rows, cols), BF)],
        prefetch=info,
    )


def fold_heads_kernel(info_ref, keep_first, got_first, keep_last, got_last, out_ref, *refs):
    ups, all_ref = refs[:-1], refs[-1]
    width = out_ref.shape[2]
    all_ref[0] = add_low(keep_first[...], got_first[...])
    all_ref[1] = add_low(keep_last[...], got_last[...])
    out_ref[...] = all_ref[:, :, :width]
    for s, up_ref in enumerate(ups):
        up_ref[...] = all_ref[:, at_block(ahead(info_ref, s, len(ups)), up_ref.shape[1]), width:]


def fold_heads(info, arrays, width, ranks):
    rows, cols = arrays[0].shape
    return call(
        fold_heads_kernel,
        [((2, rows, width), BF)] + [((2, rows // ranks, cols - width), BF)] * ranks,
        arrays,
        "fold_heads",
        scratch=[pltpu.VMEM((2, rows, cols), BF)],
        prefetch=info,
    )


def pack_heads_kernel(info_ref, out_ref, *refs):
    ups, all_ref = refs[:-1], refs[-1]
    width = out_ref.shape[2]
    all_ref[:, :, :width] = out_ref[...]
    for s, up_ref in enumerate(ups):
        all_ref[:, at_block(behind(info_ref, s, len(ups)), up_ref.shape[1]), width:] = up_ref[...]


def pack_heads(info, out, ups):
    shape = out.shape[:2] + (out.shape[2] + ups[0].shape[2],)
    return call(pack_heads_kernel, [(shape, BF)], (out, *ups), "pack_heads", prefetch=info)[0]


def layer_kernel(info_ref, residual_ref, *refs):
    parts, out_ref = refs[:-1], refs[-1]
    out_ref[...] = (residual_ref[...] + sum(part[...].astype(F32) for part in parts)).astype(BF)


def place_kernel(info_ref, *refs):
    parts, out_ref = refs[:-1], refs[-1]
    for s, part in enumerate(parts):
        pl.when(pl.program_id(0) == s)(lambda part=part: out_ref.__setitem__(..., part[...]))


def place(info, parts):
    rows, cols = parts[0].shape
    ranks = len(parts)
    return call(
        place_kernel,
        [((ranks * rows, cols), BF)],
        parts,
        "place",
        grid=(ranks,),
        in_specs=[once((rows, cols), lambda i, w: (0, 0))] * ranks,
        out_specs=[pl.BlockSpec((rows, cols), lambda i, w: (behind(w, i, ranks), 0))],
        prefetch=info,
    )[0]


def input_back_kernel(
    ranks, info_ref, tokens_ref, branch_ref, gain_ref, kv_weight_ref, recip_ref, latent_ref, kv_pre_ref, *refs
):
    latents, kvs, downs = refs[:ranks], refs[ranks : 2 * ranks], refs[2 * ranks : 3 * ranks]
    grad_in_ref, norm_ref, own_ref, kv_ref, all_ref = refs[3 * ranks :]
    rows = latents[0].shape[0]
    cols = own_ref.shape[1]
    for s in range(ranks):
        at = at_block(behind(info_ref, s, ranks), rows)
        all_ref[at, :] = latents[s][...]
        kv_ref[at, :] = kvs[s][...]
    grad = dense_nt(kv_ref[...], kv_weight_ref[...])
    for s in range(ranks):
        at = at_block(behind(info_ref, s, ranks), cols)
        grad = grad + dense_nt(all_ref[:, at], downs[s][...])
    own_ref[...] = all_ref[:, at_block(info_ref[RANK], cols)]
    recip = recip_ref[:, 0:1]
    latent = latent_ref[: all_ref.shape[0], :].astype(F32)
    stat = jnp.sum(all_ref[...].astype(F32) * latent, -1, keepdims=True)
    stat = stat + jnp.sum(kv_ref[...].astype(F32) * kv_pre_ref[...], -1, keepdims=True)
    tokens = tokens_ref[...].astype(F32)
    model = tokens.shape[1] * ranks
    out = branch_ref[...].astype(F32) + recip * gain_ref[...] * grad
    grad_in_ref[...] = out - tokens * (recip * recip * stat / model)
    norm_ref[...] = jnp.sum(grad * tokens * recip, 0, keepdims=True)


def input_back(info, tokens, branch, gain, kv_weight, recip, latent, kv_pre, latents, kvs, downs):
    ranks = len(latents)
    rows, model = tokens.shape
    cols = model // ranks
    width, down = kv_weight.shape[1], downs[0].shape[1]
    whole = lambda array: pl.BlockSpec(array.shape, lambda i, w: (0, 0))
    wide = pl.BlockSpec((rows, cols), lambda i, w: (0, w[RANK]))
    outs = [((rows, cols), F32), ((1, cols), F32), ((rows, down), BF), ((rows, width), BF)]
    return call(
        functools.partial(input_back_kernel, ranks),
        outs,
        (tokens, branch, gain.reshape(1, -1), kv_weight, recip, latent, kv_pre, *latents, *kvs, *downs),
        "input_back",
        scratch=[pltpu.VMEM((rows, latent.shape[1]), BF)],
        grid=(1,),
        in_specs=[
            wide,
            wide,
            pl.BlockSpec((1, cols), lambda i, w: (0, w[RANK])),
            pl.BlockSpec((cols, width), lambda i, w: (w[RANK], 0)),
        ]
        + [whole(array) for array in (recip, latent, kv_pre, *latents, *kvs, *downs)],
        out_specs=[pl.BlockSpec(shape, lambda i, w: (0, 0)) for shape, _ in outs],
        prefetch=info,
    )


def last_products_kernel(info_ref, normed_ref, latent_ref, kv_ref, near_ref, far_ref, down_ref, wide_ref):
    down_ref[...] = dense_tn(normed_ref[...], latent_ref[...]).astype(BF)
    cols = wide_ref.shape[0]
    wide_ref[...] = dense_tn(normed_ref[:, at_block(info_ref[RANK], cols)], kv_ref[...]).astype(BF)
    chips, width = near_ref.shape[0], near_ref.shape[2]
    for out_ref, core in ((near_ref, info_ref[CORE]), (far_ref, 1 - info_ref[CORE])):
        for chip in range(chips):
            rows = down_ref.shape[0] // (2 * chips)
            out_ref[chip, :rows, :] = down_ref[at_block(core * chips + chip, rows), :]
            more = wide_ref.shape[0] // (2 * chips)
            part = wide_ref[at_block(core * chips + chip, more), :]
            out_ref[chip, rows : rows + more, :] = part[:, :width]
            out_ref[chip, rows + more :, :] = part[:, width:]


def last_products(info, normed, latent, kv, ranks):
    model, down, width = normed.shape[1], latent.shape[1], kv.shape[1]
    cols = model // ranks
    rows = (model + cols * width // down) // 8
    return call(
        last_products_kernel,
        [((4, rows, down), BF)] * 2,
        (normed, latent, kv),
        "last_products",
        scratch=[pltpu.VMEM((model, down), BF), pltpu.VMEM((cols, width), BF)],
        prefetch=info,
    )


def fold_direct_kernel(info_ref, near_ref, got_ref, *outs):
    for mask, out_ref in enumerate(outs):
        chip = lax.bitwise_xor(chip_of(info_ref), mask)
        out_ref[...] = add_low(near_ref[chip], got_ref[chip])


def fold_direct(info, near, got):
    return call(fold_direct_kernel, [(near.shape[1:], BF)] * 4, (near, got), "fold_direct", prefetch=info)


def sum_kernel(info_ref, *refs):
    refs[-1][...] = sum(part[...].astype(F32) for part in refs[:-1]).astype(BF)


def sum_parts(info, parts):
    return call(sum_kernel, [(parts[0].shape, BF)], parts, "sum_parts", prefetch=info)[0]


def stack_kernel(info_ref, *refs):
    for mask, part in enumerate(refs[:-1]):
        refs[-1][lax.bitwise_xor(chip_of(info_ref), mask)] = part[...]


def stack_chips(info, parts):
    return call(stack_kernel, [((4,) + parts[0].shape, BF)], parts, "stack_chips", prefetch=info)[0]


def last_kernel(info_ref, own_ref, other_ref, down_ref, kv_ref):
    chips, width = own_ref.shape[0], own_ref.shape[2]
    rows, more = down_ref.shape[0] // (2 * chips), kv_ref.shape[0] // (2 * chips)
    for in_ref, core in ((own_ref, info_ref[CORE]), (other_ref, 1 - info_ref[CORE])):
        for chip in range(chips):
            part = in_ref[chip].astype(F32)
            down_ref[at_block(core * chips + chip, rows), :] = part[:rows]
            kv_ref[at_block(core * chips + chip, more), :width] = part[rows : rows + more]
            kv_ref[at_block(core * chips + chip, more), width:] = part[rows + more :]


def store_feed(part, gate_ref, up_ref, down_ref):
    width = gate_ref.shape[1]
    gate_ref[...] = part[:, :width].astype(F32)
    up_ref[...] = part[:, width : 2 * width].astype(F32)
    down_ref[...] = part[:, 2 * width :].astype(F32).T


def store_heads(part, out_ref, up_ref):
    width = out_ref.shape[1]
    rows, cols = up_ref.shape[0], part.shape[1] - width
    out_ref[...] = part[:, :width].astype(F32)
    for r in range(part.shape[0] // rows):
        up_ref[:, r * cols : (r + 1) * cols] = part[r * rows : (r + 1) * rows, width:].astype(F32)


def unpack_kernel(store, info_ref, in_ref, *out_refs):
    store(in_ref[...], *out_refs)


def unpack(info, whole, store, shapes, along):
    def where(i):
        source, p = i // 2, i % 2
        chip = source // 2
        return source % 2 * 8 + p * 4 + jnp.where(p == 0, chip % 2 * 2 + chip // 2, chip)

    out_specs = []
    for (rows, cols), dim in zip(shapes, along):
        if dim == 0:
            out_specs.append(pl.BlockSpec((rows // 16, cols), lambda i, w: (where(i), 0)))
        else:
            out_specs.append(pl.BlockSpec((rows, cols // 16), lambda i, w: (0, where(i))))
    return call(
        functools.partial(unpack_kernel, store),
        [(shape, F32) for shape in shapes],
        (whole,),
        "unpack",
        grid=(16,),
        in_specs=[pl.BlockSpec((None, None) + whole.shape[2:], lambda i, w: (i // 2, i % 2, 0, 0))],
        out_specs=out_specs,
        prefetch=info,
    )


def bit_of(index, bit):
    return (index >> bit) & 1


def exchange(value, mask):
    count = lax.axis_size("seq")
    return lax.ppermute(value, "seq", [(i, i ^ mask) for i in range(count)])


def swap(value, bit):
    return exchange(value, 1 << bit)


def ring(value, shift):
    if not shift:
        return value
    ranks = lax.axis_size("rank")
    return lax.ppermute(value, "rank", [(i, (i + shift) % ranks) for i in range(ranks)])


def rings(values):
    return [ring(value, s) for s, value in enumerate(values)]


def sum_over(value, axis):
    count = lax.axis_size(axis)
    mask = 1
    while mask < count:
        value = value + lax.ppermute(value, axis, [(i, i ^ mask) for i in range(count)])
        mask *= 2
    return value


def after(value, *others):
    return lax.optimization_barrier((value, others))[0]


def per_device_fast(
    tokens_in,
    norm1_gain,
    q_down,
    latent_gain,
    q_up,
    kv_weight,
    out_weight,
    norm2_gain,
    gate_weight,
    up_weight,
    down_weight,
    doc_ids,
    out_grad,
):
    Order.last = None
    row_count, model_width = tokens_in.shape
    ranks = lax.axis_size("rank")
    rank_ix = lax.axis_index("rank")
    seq_ix = lax.axis_index("seq")
    head_dim = kv_weight.shape[1] // 2
    local_heads = out_weight.shape[0] // head_dim
    first_row = seq_ix * row_count
    core = bit_of(seq_ix, 0)
    rank_cols = q_down.shape[1]
    rank_width = rank_cols * ranks
    col_count = model_width // ranks

    up_cols = q_up.shape[1] // ranks
    half_cols = up_cols // 2
    blocks = [
        lax.dynamic_slice_in_dim(
            q_up, lax.rem(rank_ix + s, ranks) * up_cols + core * half_cols, half_cols, 1
        )
        for s in range(ranks)
    ]
    tokens_late = after(tokens_in, blocks)
    up_own = jnp.concatenate(rings(blocks), 0)
    up_other = swap(up_own, 0)

    ids_local = lax.dynamic_slice_in_dim(doc_ids, first_row, row_count, 0)
    start = jnp.sum((doc_ids[None, :] < ids_local[:, None]).astype(I32), 1)
    query_index = first_row + jnp.arange(row_count, dtype=I32)
    position = (query_index - start).astype(F32)
    half_dim = head_dim // 2
    freqs = BASE ** (-jnp.arange(half_dim, dtype=F32) / half_dim)
    angle = position[:, None] * freqs[None, :]
    cosine, sine = jnp.cos(angle), jnp.sin(angle)
    start_rows = jnp.tile(start, local_heads)[None]
    index_rows = jnp.tile(query_index, local_heads)[None]
    place_info = jnp.stack([first_row, first_row, first_row, core, rank_ix, seq_ix]).astype(I32)
    info = jnp.stack([first_row, start[0], start[-1], core, rank_ix, seq_ix]).astype(I32)

    normed_low, recip1, kv_pre, latent = project(
        place_info, tokens_late, norm1_gain, q_down, kv_weight, latent_gain
    )
    latent_all = lax.all_gather(latent, "rank", axis=1, tiled=True)

    kv_local = turn(place_info, kv_pre, cosine, sine)
    half_rows = row_count // 2
    by_x, by_y = swap(kv_local, 1), swap(kv_local, 2)
    top, bottom = swap(by_x[:half_rows], 2), swap(by_y[half_rows:], 1)
    pieces = [(kv_local, 0, 0), (by_x, 2, 0), (by_y, 4, 0), (top, 6, 0), (bottom, 6, half_rows)]
    pieces += [(swap(array, 0), mask ^ 1, offset) for array, mask, offset in pieces]

    latent_low, recip_c, gain_all, query_pre = queries(place_info, latent_all, up_own, up_other)
    query, attn_vals, attn_low, log_total, kv_all = attend(
        in_order(info), query_pre, cosine, sine, start, pieces
    )
    Order.last = attn_low

    branch_part = matmul(info, attn_low, out_weight)
    branch = lax.psum_scatter(branch_part, "rank", scatter_dimension=0, tiled=True)
    grad_hidden = dense_nt(after(out_grad, branch_part), down_weight)
    out_grad_pair = swap(after(out_grad, branch_part), 0)
    attn_pair = swap(attn_low, 0)
    piece_cols = rank_cols // 16
    latent_cut = jnp.transpose(
        after(latent_low, branch_part).reshape(row_count, ranks, 16, piece_cols), (0, 2, 1, 3)
    ).reshape(row_count, rank_width)
    latent_pair = swap(latent_cut, 0)
    down_blocks = [
        lax.dynamic_slice_in_dim(
            after(q_down, branch_part), lax.rem(rank_ix + s, ranks) * col_count, col_count, 0
        )
        for s in range(ranks)
    ]
    branch = after(
        branch, grad_hidden, out_grad_pair, attn_pair, latent_pair, latent_cut, down_blocks
    )
    residual, mid_own, recip2 = mid_norm(info, branch, tokens_in, norm2_gain)
    mid_low = lax.all_gather(mid_own, "rank", axis=0, tiled=True)

    downs = rings(after(down_blocks, mid_low))
    mid_pair = swap(mid_low, 0)
    hidden_low, grad_both, grad_mid_part = feed_forward(
        mid_low, grad_hidden, gate_weight, up_weight
    )
    Order.last = hidden_low
    hidden_low, grad_both, grad_mid_part = after((hidden_low, grad_both, grad_mid_part), downs)
    grad_mid = lax.psum_scatter(grad_mid_part, "rank", scatter_dimension=0, tiled=True)
    both_pair, hidden_pair = swap(grad_both, 0), swap(hidden_low, 0)
    feed_parts = matmul(info, hidden_low, down_weight, parts=ranks)
    feed_width = gate_weight.shape[1]
    send_first, send_last, keep_first, keep_last = pair_products(
        info,
        [
            (mid_low, mid_pair, grad_both, both_pair),
            (out_grad, out_grad_pair, hidden_low, hidden_pair),
        ],
        feed_width,
    )
    grad_mid = after(grad_mid, send_first)
    branch_own, norm2_part = mid_back(info, grad_mid, residual, recip2, norm2_gain, out_grad)
    grad_branch = lax.all_gather(branch_own, "rank", axis=0, tiled=True)

    two = lambda array: array.reshape((2, -1) + array.shape[1:])
    arrays = (keep_first, swap(send_first, 1), keep_last, swap(send_last, 2))
    arrays = fold_first(info, [two(array) for array in arrays], 4, 10000)
    arrays = (arrays[2], swap(arrays[0], 2), arrays[3], swap(arrays[1], 1))
    feed_piece = fold_last(info, arrays, 4)
    branch_pair = swap(grad_branch, 0)
    grad_attn = matmul(info, grad_branch, out_weight, True)
    feed_whole = lax.all_gather(feed_piece, "seq", axis=0, tiled=False)
    feed_sums = rings(after(feed_parts, grad_branch))
    grad_query, near, far = attend_back(
        in_order(info), query, grad_attn, attn_vals, log_total, cosine, sine, kv_all,
        start_rows, index_rows, True,
    )
    grad_query, near, far = after((grad_query, near, far), feed_sums, branch_pair)
    Order.last = grad_query

    latent_grads = rings(latent_parts(info, grad_query, up_own, up_other, ranks))
    query_pair = swap(grad_query, 0)
    arrays = fold_near(info, near, swap(far, 0))
    heads = pair_products(
        info,
        [
            (attn_low, attn_pair, grad_branch, branch_pair),
            (latent_cut, latent_pair, grad_query, query_pair),
        ],
        up_cols,
    )
    arrays = (arrays[2], swap(arrays[0], 1), arrays[3], swap(arrays[1], 2))
    arrays = fold_first(info, after(arrays, latent_grads), 1)
    arrays = (arrays[2], swap(arrays[0], 2), arrays[3], swap(arrays[1], 1))
    latent_own, gain_part = latent_back(info, latent_all, recip_c, gain_all, latent_grads)
    latent_blocks = rings([latent_own] * ranks)
    kv_sums = rings(fold_kv(info, arrays, ranks))
    arrays = (heads[2], swap(heads[0], 1), heads[3], swap(heads[1], 2))
    arrays = fold_first(info, [two(array) for array in arrays], 1)
    kv_own = kv_back(info, cosine, sine, kv_sums)
    kv_blocks = rings([kv_own] * ranks)
    arrays = (arrays[2], swap(arrays[0], 2), arrays[3], swap(arrays[1], 1))
    arrays = after(arrays, latent_blocks)
    out_piece, *up_pieces = fold_heads(info, arrays, model_width, ranks)
    heads_piece = pack_heads(info, out_piece, rings(up_pieces))
    heads_whole = lax.all_gather(heads_piece, "seq", axis=0, tiled=False)
    layer_own = call(
        layer_kernel, [(residual.shape, BF)], (residual, *feed_sums), "layer", prefetch=info
    )[0]
    shape = gate_weight.shape
    grad_gate, grad_up, grad_down = unpack(
        info, after(feed_whole, kv_blocks), store_feed, (shape, shape, shape[::-1]), (0, 0, 1)
    )
    gains = jnp.concatenate([norm2_part[0], gain_part[0]])
    gains = sum_over(sum_over(gains, "rank"), "seq")
    layer_blocks = rings([after(layer_own, kv_blocks, latent_blocks, gains)] * ranks)

    grad_in, norm1_part, latent_cols, grad_kv = input_back(
        info, tokens_in, grad_branch, norm1_gain, kv_weight, recip1, latent_all, kv_pre,
        latent_blocks, kv_blocks, downs,
    )
    near, far = last_products(info, normed_low, latent_cols, grad_kv, ranks)
    own, *others = fold_direct(info, near, swap(far, 0))
    norm1 = sum_over(norm1_part[0], "seq")
    piece = sum_parts(info, [own] + [exchange(part, 2 * m) for m, part in enumerate(others, 1)])
    last = stack_chips(info, after([piece] + [exchange(piece, 2 * m) for m in (1, 2, 3)], norm1))
    grad_q_down, grad_kv_weight = call(
        last_kernel,
        [(q_down.shape, F32), ((col_count, 2 * head_dim), F32)],
        (last, swap(last, 0)),
        "last",
        prefetch=info,
    )
    grad_out, grad_q_up = unpack(
        info, heads_whole, store_heads, (out_weight.shape, q_up.shape), (0, 0)
    )
    layer_out = place(info, after(layer_blocks, grad_out))

    grad_norm2 = gains[:model_width]
    grad_latent_gain = lax.dynamic_slice_in_dim(gains, model_width + rank_ix * rank_cols, rank_cols, 0)
    return (
        layer_out,
        grad_in,
        norm1,
        grad_q_down,
        grad_latent_gain,
        grad_q_up,
        grad_kv_weight,
        grad_out,
        grad_norm2,
        grad_gate,
        grad_up,
        grad_down,
    )


def add_low(left, right):
    return (left.astype(F32) + right.astype(F32)).astype(BF)


def halve(value, axis, bit, seq_ix):
    own = bit_of(seq_ix, bit)
    keep = lax.dynamic_index_in_dim(value, own, axis, keepdims=False)
    send = lax.dynamic_index_in_dim(value, 1 - own, axis, keepdims=False)
    return add_low(keep, swap(send, bit))


def scatter_chips(value, seq_ix):
    bits = value.shape[0].bit_length() - 1
    shape = (2,) * bits + value.shape[2:]
    first, last = value[:, 0].reshape(shape), value[:, 1].reshape(shape)
    first_axes = list(range(bits))
    last_axes = list(range(bits))
    for step in range(bits):
        bit = step + 1
        axis = first_axes.index(bits - bit)
        first = halve(first, axis, bit, seq_ix)
        del first_axes[axis]
        bit = bits - step
        axis = last_axes.index(bits - bit)
        last = halve(last, axis, bit, seq_ix)
        del last_axes[axis]
    return jnp.stack([first, last])


def scatter_rows(near, far, seq_ix):
    return scatter_chips(add_low(near, swap(far, 0)), seq_ix)


def split_product(left, right, seq_ix):
    chips = lax.axis_size("seq") // 2
    rows = left.shape[1] // 2
    own = bit_of(seq_ix, 0)
    parts = []
    for core in (own, 1 - own):
        piece = lax.dynamic_slice_in_dim(left, core * rows, rows, 1)
        parts.append(dense_tn(piece, right).astype(BF))
    shape = (2, chips, rows // (2 * chips), right.shape[1])
    return [jnp.swapaxes(part.reshape(shape), 0, 1) for part in parts]


def gather_rows(piece):
    seq = lax.axis_size("seq")
    whole = lax.all_gather(piece, "seq", axis=0, tiled=False)
    whole = whole.reshape((seq // 2, 2) + piece.shape)
    whole = jnp.transpose(whole, (1, 2, 0, 3, 4))
    return whole.reshape(seq * piece.shape[0] * piece.shape[1], piece.shape[2])


def reduce_product(left, right, seq_ix):
    near, far = split_product(left, right, seq_ix)
    return gather_rows(scatter_rows(near, far, seq_ix)).astype(F32)


def high_low(values):
    high = values.astype(BF)
    return [high, (values - high.astype(F32)).astype(BF)]


def per_device_general(
    tokens_in,
    norm1_gain,
    q_down,
    latent_gain,
    q_up,
    kv_weight,
    out_weight,
    norm2_gain,
    gate_weight,
    up_weight,
    down_weight,
    doc_ids,
    out_grad,
):
    row_count, model_width = tokens_in.shape
    rank_count = lax.axis_size("rank")
    seq_count = lax.axis_size("seq")
    rank_ix = lax.axis_index("rank")
    seq_ix = lax.axis_index("seq")
    head_dim = kv_weight.shape[1] // 2
    local_heads = out_weight.shape[0] // head_dim
    first_row = seq_ix * row_count
    core = bit_of(seq_ix, 0)
    own_rows = row_count // rank_count
    rank_cols = q_down.shape[1]
    rank_width = rank_cols * rank_count

    half_rows = q_up.shape[0] // 2
    up_half = lax.dynamic_slice_in_dim(q_up, core * half_rows, half_rows, 0)
    up_half = lax.all_to_all(up_half, "rank", 1, 0, tiled=True)
    up_other = swap(up_half, 0)
    up_half = up_half.reshape(rank_count, 1, half_rows, -1)
    up_other = up_other.reshape(rank_count, 1, half_rows, -1)
    q_up_own = jnp.concatenate(
        [jnp.where(core == 0, up_half, up_other), jnp.where(core == 0, up_other, up_half)], 1
    ).reshape(rank_width, -1)

    ids_local = lax.dynamic_slice_in_dim(doc_ids, first_row, row_count, 0)
    start = jnp.sum((doc_ids[None, :] < ids_local[:, None]).astype(I32), 1)
    query_index = first_row + jnp.arange(row_count, dtype=I32)
    position = (query_index - start).astype(F32)
    half_dim = head_dim // 2
    freqs = BASE ** (-jnp.arange(half_dim, dtype=F32) / half_dim)
    angle = position[:, None] * freqs[None, :]
    cosine_rows, sine_rows = jnp.cos(angle), jnp.sin(angle)
    start_rows = jnp.tile(start, local_heads)[None]
    index_rows = jnp.tile(query_index, local_heads)[None]
    info = jnp.stack([first_row, start[0], start[-1], core]).astype(I32)

    tokens = tokens_in.astype(F32)
    normed_in, recip1 = norm_rows(tokens, norm1_gain)
    normed_low = normed_in.astype(BF)
    kv_pre = dense(normed_low, kv_weight)
    key_local = rotate(kv_pre[:, :head_dim], cosine_rows, sine_rows)
    kv_local = jnp.concatenate([key_local, kv_pre[:, head_dim:]], -1).astype(BF)
    kv_all = lax.all_gather(kv_local, "seq", axis=0, tiled=True)

    latent = dense(normed_low, q_down)
    high, rest = high_low(latent_gain)
    low = (latent_gain - high.astype(F32) - rest.astype(F32)).astype(BF)
    gain_rows = jnp.stack([high, rest, low] + [jnp.zeros_like(high)] * 13)
    gathered = lax.all_gather(
        jnp.concatenate([latent.astype(BF), gain_rows], 0), "rank", axis=1, tiled=True
    ).astype(F32)
    latent_all = gathered[:row_count]
    gain_all = gathered[row_count] + gathered[row_count + 1] + gathered[row_count + 2]
    recip_c = lax.rsqrt(jnp.mean(latent_all * latent_all, -1, keepdims=True) + EPS)
    latent_low = (latent_all * recip_c * gain_all).astype(BF)
    query_pre = dense(latent_low, q_up_own)

    query, attn_vals, attn_low, log_total, kv_all = attend(
        info, query_pre, cosine_rows, sine_rows, start, [(kv_all, None, 0)]
    )
    branch = lax.psum_scatter(
        dense(attn_low, out_weight).astype(BF), "rank", scatter_dimension=0, tiled=True
    )
    tokens_rows = lax.dynamic_slice_in_dim(tokens_in, rank_ix * own_rows, own_rows, 0)
    residual = tokens_rows.astype(F32) + branch.astype(F32)
    normed_mid, recip2 = norm_rows(residual, norm2_gain)
    mid_low = lax.all_gather(normed_mid.astype(BF), "rank", axis=0, tiled=True)

    grad_hidden = dense_nt(out_grad, down_weight)
    gate_pre = dense(mid_low, gate_weight)
    up_pre = dense(mid_low, up_weight)
    sigmoid_gate = jax.nn.sigmoid(gate_pre)
    activated = gate_pre * sigmoid_gate
    hidden_low = (activated * up_pre).astype(BF)
    grad_gate_pre = (
        grad_hidden * up_pre * sigmoid_gate * (1.0 + gate_pre * (1.0 - sigmoid_gate))
    ).astype(BF)
    grad_up_pre = (grad_hidden * activated).astype(BF)
    grad_mid = lax.psum_scatter(
        (dense_nt(grad_gate_pre, gate_weight) + dense_nt(grad_up_pre, up_weight)).astype(BF),
        "rank",
        scatter_dimension=0,
        tiled=True,
    ).astype(F32)
    feed_out = lax.psum_scatter(
        dense(hidden_low, down_weight).astype(BF), "rank", scatter_dimension=0, tiled=True
    )
    layer_out = lax.all_gather(
        (residual + feed_out.astype(F32)).astype(BF), "rank", axis=0, tiled=True
    )
    grad_gate = reduce_product(mid_low, grad_gate_pre, seq_ix)
    grad_up = reduce_product(mid_low, grad_up_pre, seq_ix)
    grad_down = reduce_product(hidden_low, out_grad, seq_ix)

    gained_mid = grad_mid * norm2_gain
    stat_mid = jnp.sum(residual * gained_mid, -1, keepdims=True)
    out_grad_rows = lax.dynamic_slice_in_dim(out_grad, rank_ix * own_rows, own_rows, 0)
    grad_residual = (
        out_grad_rows.astype(F32)
        + recip2 * gained_mid
        - residual * recip2**3 * stat_mid / model_width
    )
    grad_norm2 = jnp.sum(grad_mid * residual * recip2, 0)
    grad_branch = lax.all_gather(grad_residual.astype(BF), "rank", axis=0, tiled=True)
    grad_attn = dense_nt(grad_branch, out_weight).astype(BF)
    grad_out = reduce_product(attn_low, grad_branch, seq_ix)
    grad_query, near, far = attend_back(
        info, query, grad_attn, attn_vals, log_total, cosine_rows, sine_rows, kv_all,
        start_rows, index_rows, False,
    )

    chips = seq_count // 2
    summed = scatter_rows(jnp.swapaxes(near, 0, 1), jnp.swapaxes(far, 0, 1), seq_ix)
    summed = lax.psum(summed.reshape(row_count, 2 * head_dim), "rank").astype(F32)
    key_back = rotate(summed[:, :head_dim], cosine_rows, -sine_rows)
    grad_kv = jnp.concatenate([key_back, summed[:, head_dim:]], -1).astype(BF)

    grad_latent_part = dense_nt(grad_query, q_up_own).astype(BF)
    norm2_rows = jnp.concatenate(high_low(grad_norm2)).reshape(-1, rank_width)
    extra = norm2_rows.shape[0]
    norm2_rows = jnp.pad(norm2_rows, ((0, -extra % 16), (0, 0)))
    over_ranks = lax.psum(jnp.concatenate([grad_latent_part, norm2_rows], 0), "rank").astype(F32)
    grad_latent_in = over_ranks[:row_count]
    grad_norm2 = jnp.sum(
        over_ranks[row_count : row_count + extra].reshape(2, model_width), 0
    )
    gained_latent = grad_latent_in * gain_all
    stat_latent = jnp.sum(latent_all * gained_latent, -1, keepdims=True)
    grad_latent = (
        recip_c * gained_latent - latent_all * recip_c**3 * stat_latent / rank_width
    ).astype(BF)
    own_latent = lambda v: lax.dynamic_slice_in_dim(v, rank_ix * rank_cols, rank_cols, 1)
    grad_latent_gain = jnp.sum(own_latent(grad_latent_in) * latent * recip_c, 0)

    near, far = split_product(grad_query, latent_low, seq_ix)
    piece = scatter_rows(near, far, seq_ix)
    piece = lax.all_to_all(piece, "rank", 2, 0, tiled=True)
    piece = piece.reshape(rank_count * 2, piece.shape[1], rank_cols)
    whole = lax.all_gather(piece, "seq", axis=0, tiled=False)
    whole = whole.reshape(chips, 2, rank_count, 2, piece.shape[1], rank_cols)
    grad_q_up = jnp.transpose(whole, (5, 2, 1, 3, 0, 4)).reshape(rank_cols, -1).astype(F32)

    col_count = model_width // rank_count
    col_start = rank_ix * col_count
    cols = lambda v: lax.dynamic_slice_in_dim(v, col_start, col_count, v.ndim - 1)
    q_down_rows = lax.all_to_all(q_down, "rank", 0, 1, tiled=True)
    kv_rows = lax.dynamic_slice_in_dim(kv_weight, col_start, col_count, 0)
    grad_normed = dense_nt(grad_latent, q_down_rows) + dense_nt(grad_kv, kv_rows)
    norm1_stat = (
        jnp.sum(grad_latent.astype(F32) * latent_all, -1, keepdims=True)
        + jnp.sum(grad_kv.astype(F32) * kv_pre, -1, keepdims=True)
    ) / recip1
    tokens_own = cols(tokens_in).astype(F32)
    grad_in = (
        cols(grad_branch).astype(F32)
        + recip1 * cols(norm1_gain) * grad_normed
        - tokens_own * recip1**3 * norm1_stat / model_width
    )
    grad_norm1 = jnp.sum(grad_normed * tokens_own * recip1, 0)

    grad_q_down = lax.psum(
        dense_tn(normed_low, own_latent(grad_latent)).astype(BF), "seq"
    ).astype(F32)
    grad_kv_weight = dense_tn(cols(normed_low), grad_kv).astype(BF)
    small = jnp.concatenate([grad_norm1, grad_latent_gain, grad_norm2])
    small = jnp.concatenate(high_low(small)).reshape(2, -1)
    count = small.shape[1]
    kv_cols = grad_kv_weight.shape[1]
    small_rows = jnp.pad(small.reshape(-1), (0, -2 * count % (16 * kv_cols))).reshape(-1, kv_cols)
    last = lax.psum(jnp.concatenate([grad_kv_weight, small_rows], 0), "seq").astype(F32)
    grad_kv_weight = last[:col_count]
    small = jnp.sum(last[col_count:].reshape(-1)[: 2 * count].reshape(2, count), 0)
    grad_norm1 = small[:col_count]
    grad_latent_gain = small[col_count : col_count + rank_cols]
    grad_norm2 = small[col_count + rank_cols :]
    return (
        layer_out,
        grad_in,
        grad_norm1,
        grad_q_down,
        grad_latent_gain,
        grad_q_up,
        grad_kv_weight,
        grad_out,
        grad_norm2,
        grad_gate,
        grad_up,
        grad_down,
    )


def per_device(*args):
    tokens, out_weight = args[0], args[6]
    fits = (
        lax.axis_size("seq") == 8
        and lax.axis_size("rank") == 4
        and tokens.shape[0] % 64 == 0
        and tokens.shape[1] % 2048 == 0
        and args[2].shape[1] % 256 == 0
        and out_weight.shape[0] % 1024 == 0
        and args[8].shape[1] % LANES == 0
        and args[11].shape[0] % 512 == 0
    )
    return (per_device_fast if fits else per_device_general)(*args)


def solution(mesh):
    return jax.shard_map(
        per_device,
        mesh=mesh,
        in_specs=(
            P("seq", None),
            P(),
            P(None, "rank"),
            P("rank"),
            P("rank", None),
            P(),
            P("rank", None),
            P(),
            P(None, "rank"),
            P(None, "rank"),
            P("rank", None),
            P(),
            P("seq", None),
        ),
        out_specs=(
            P("seq", None),
            P("seq", "rank"),
            P("rank"),
            P(None, "rank"),
            P("rank"),
            P("rank", None),
            P("rank", None),
            P("rank", None),
            P(),
            P(None, "rank"),
            P(None, "rank"),
            P("rank", None),
        ),
        check_vma=False,
    )
```

```python
import functools

import jax
import jax.numpy as jnp
from jax import lax
from jax.experimental import pallas as pl
from jax.experimental.pallas import tpu as pltpu
from jax.sharding import PartitionSpec as P

EPS = 1e-05
BASE = 10000.0
NEG = -1e30
LOG2E = 1.4426950408889634
BF = jnp.bfloat16
F32 = jnp.float32
I32 = jnp.int32
LANES = 128

def norm_rows(values, gain):
    recip = lax.rsqrt(jnp.mean(values * values, -1, keepdims=True) + EPS)
    return (values * recip * gain, recip)


def rotate(values, cosine_rows, sine_rows):
    half_dim = values.shape[-1] // 2
    front_half = values[..., :half_dim]
    back_half = values[..., half_dim:]
    return jnp.concatenate(
        [
            front_half * cosine_rows - back_half * sine_rows,
            front_half * sine_rows + back_half * cosine_rows,
        ],
        -1,
    )


def dense(left, right):
    return jnp.dot(left, right, preferred_element_type=F32)


def dense_tn(left, right):
    return lax.dot_general(left, right, (((0,), (0,)), ((), ())), preferred_element_type=F32)


def dense_nt(left, right):
    return lax.dot_general(left, right, (((1,), (1,)), ((), ())), preferred_element_type=F32)


def key_block(key_count, most):
    for size in (1536, 1024, 512, 256, 128):
        if size <= most and key_count % size == 0:
            return size
    return key_count


def row_tile(rows):
    for parts in (3, 2):
        if rows % (parts * 128) == 0:
            return rows // parts
    return rows


def over_key_blocks(info_ref, size, tokens, run):
    first, low, high = info_ref[0], info_ref[1], info_ref[2]
    begin = low // size
    whole_end = jnp.maximum(first // size, begin)
    whole_begin = jnp.clip((high + size - 1) // size, begin, whole_end)
    end = (first + tokens + size - 1) // size
    lax.fori_loop(begin, whole_begin, lambda j, c: run(j, True), None)
    lax.fori_loop(whole_begin, whole_end, lambda j, c: run(j, False), None)
    lax.fori_loop(whole_end, end, lambda j, c: run(j, True), None)


def attend_kernel(
    size, tile, heads, places, info_ref, pre_ref, cos_ref, sin_ref, first_ref, *refs
):
    pieces_in = refs[: len(places)]
    query_ref, out_ref, low_ref, log_ref, kv_ref = refs[len(places) : len(places) + 5]
    max_ref, sum_ref, acc_ref, scores_ref, start_ref, index_ref, sems = refs[len(places) + 5 :]
    tokens = pre_ref.shape[0]
    copies = []
    for n, (mask, offset) in enumerate(places):
        at = lax.bitwise_xor(info_ref[5], mask) * tokens + offset if mask is not None else 0
        rows = pl.ds(pl.multiple_of(at, 16), pieces_in[n].shape[0])
        copies.append(pltpu.make_async_copy(pieces_in[n], kv_ref.at[rows, :], sems.at[n]))
    for copy in copies:
        copy.start()
    width = kv_ref.shape[1] // 2
    half = width // 2
    lanes = max_ref.shape[1]
    scale = width**-0.5 * LOG2E
    cosine, sine = cos_ref[...], sin_ref[...]
    for h in range(heads):
        front = pre_ref[:, h * width : h * width + half]
        back = pre_ref[:, h * width + half : (h + 1) * width]
        rows = slice(h * tokens, (h + 1) * tokens)
        query_ref[rows, :half] = (front * cosine - back * sine).astype(BF)
        query_ref[rows, half:] = (front * sine + back * cosine).astype(BF)
        start_ref[rows, :] = first_ref[...]
        index_ref[rows, :] = info_ref[0] + lax.broadcasted_iota(I32, (tokens, lanes), 0)
    for copy in copies:
        copy.wait()
    pieces = [slice(n * lanes, (n + 1) * lanes) for n in range(size // lanes)]
    for i in range(heads * tokens // tile):
        r = slice(i * tile, (i + 1) * tile)
        max_ref[...] = jnp.full(max_ref.shape, NEG, F32)
        sum_ref[...] = jnp.zeros(sum_ref.shape, F32)
        acc_ref[...] = jnp.zeros(acc_ref.shape, F32)

        def score(j, masked, r=r):
            base = pl.multiple_of(j * size, size)
            scores = dense_nt(query_ref[r, :], kv_ref[pl.ds(base, size), :width])
            most = max_ref[...]
            lane = lax.broadcasted_iota(I32, max_ref.shape, 1)
            for n, piece in enumerate(pieces):
                part = scores[:, piece]
                if masked:
                    at = lane + (base + n * lanes)
                    allowed = (at >= start_ref[r, :]) & (at <= index_ref[r, :])
                    part = jnp.where(allowed, part, NEG)
                scores_ref[j, :, piece] = part
                most = jnp.maximum(most, part)
            max_ref[...] = most
            return None

        over_key_blocks(info_ref, size, tokens, score)
        most = jnp.max(max_ref[...], 1, keepdims=True) * scale
        max_ref[...] = jnp.broadcast_to(most, max_ref.shape)

        def mix(j, carry):
            base = pl.multiple_of(j * size, size)
            most, total = max_ref[...], sum_ref[...]
            probs = []
            for piece in pieces:
                prob = jnp.exp2(scores_ref[j, :, piece] * scale - most)
                total = total + prob
                probs.append(prob.astype(BF))
            sum_ref[...] = total
            acc_ref[...] += dense(jnp.concatenate(probs, 1), kv_ref[pl.ds(base, size), width:])
            return carry

        end = (info_ref[0] + tokens + size - 1) // size
        lax.fori_loop(info_ref[1] // size, end, mix, None)
        total = jnp.sum(sum_ref[...], 1, keepdims=True)
        log_ref[:, r] = jnp.broadcast_to(most + jnp.log2(total), max_ref.shape).T[0:1, :]
        out = acc_ref[...] * (1.0 / total)
        at = i * tile
        while at < (i + 1) * tile:
            h = at // tokens
            stop = min((i + 1) * tile, (h + 1) * tokens)
            rows, cols = slice(at - h * tokens, stop - h * tokens), slice(h * width, (h + 1) * width)
            part = out[at - i * tile : stop - i * tile, :]
            out_ref[rows, cols] = part
            low_ref[rows, cols] = part.astype(BF)
            at = stop


def in_vmem(count):
    return [pl.BlockSpec(memory_space=pltpu.VMEM) for _ in range(count)]


def attend(info, query_pre, cosine, sine, start, pieces):
    tokens, all_heads = query_pre.shape
    width = pieces[0][0].shape[1] // 2
    keys = sum(piece[0].shape[0] for piece in pieces)
    rows = tokens * (all_heads // width)
    size, tile = key_block(keys, 1536), row_tile(rows)
    start = jnp.broadcast_to(start[:, None], (tokens, LANES))
    return pl.pallas_call(
        functools.partial(
            attend_kernel, size, tile, all_heads // width, [piece[1:] for piece in pieces]
        ),
        out_shape=(
            jax.ShapeDtypeStruct((rows, width), BF),
            jax.ShapeDtypeStruct((tokens, all_heads), F32),
            jax.ShapeDtypeStruct((tokens, all_heads), BF),
            jax.ShapeDtypeStruct((1, rows), F32),
            jax.ShapeDtypeStruct((keys, 2 * width), BF),
        ),
        in_specs=[pl.BlockSpec(memory_space=pltpu.SMEM)]
        + in_vmem(4)
        + [pl.BlockSpec(memory_space=pl.ANY)] * len(pieces),
        out_specs=tuple(in_vmem(5)),
        scratch_shapes=[
            pltpu.VMEM((tile, LANES), F32),
            pltpu.VMEM((tile, LANES), F32),
            pltpu.VMEM((tile, width), F32),
            pltpu.VMEM((keys // size, tile, size), F32),
            pltpu.VMEM((rows, LANES), I32),
            pltpu.VMEM((rows, LANES), I32),
            pltpu.SemaphoreType.DMA((len(pieces),)),
        ],
        compiler_params=pltpu.CompilerParams(vmem_limit_bytes=56 * 2**20),
        cost_estimate=brief(0),
        name="attend",
    )(info, query_pre, cosine, sine, start, *[piece[0] for piece in pieces])


def attend_back_kernel(
    size, tile, heads, by_axis, info_ref, query_ref, grad_ref, out_ref, log_ref, cos_ref, sin_ref, kv_ref, start_ref, index_ref,
    gq_ref, near_ref, far_ref, gout_ref, gk_ref, gv_ref, gqt_ref, dots_ref,
):
    tokens = grad_ref.shape[0]
    width = kv_ref.shape[1] // 2
    half = width // 2
    scale = width**-0.5
    for h in range(heads):
        gout = grad_ref[:, h * width : (h + 1) * width]
        gout_ref[h * tokens : (h + 1) * tokens, :] = gout
        dots = gout.astype(F32) * out_ref[:, h * width : (h + 1) * width]
        dots_ref[h * tokens : (h + 1) * tokens, :] = dots[:, :half] + dots[:, half:]
    delta = jnp.sum(dots_ref[...].T, 0, keepdims=True)
    gk_ref[...] = jnp.zeros(gk_ref.shape, F32)
    gv_ref[...] = jnp.zeros(gv_ref.shape, F32)
    gqt_ref[...] = jnp.zeros(gqt_ref.shape, F32)

    def run(j, masked):
        base = pl.multiple_of(j * size, size)
        at_keys = pl.ds(base, size)
        keys = kv_ref[at_keys, :width]
        values = kv_ref[at_keys, width:]
        for i in range(heads * tokens // tile):
            r = slice(i * tile, (i + 1) * tile)
            query, gout = query_ref[r, :], gout_ref[r, :]
            probs = jnp.exp2(dense_nt(keys, query) * (scale * LOG2E) - log_ref[:, r])
            if masked:
                at = base + lax.broadcasted_iota(I32, (size, tile), 0)
                allowed = (at >= start_ref[:, r]) & (at <= index_ref[:, r])
                probs = jnp.where(allowed, probs, 0.0)
            gscores = (probs * (dense_nt(values, gout) - delta[:, r])).astype(BF)
            gv_ref[at_keys, :] += dense(probs.astype(BF), gout)
            gk_ref[at_keys, :] += dense(gscores, query)
            gqt_ref[:, r] += dense_tn(keys, gscores)
        return None

    over_key_blocks(info_ref, size, tokens, run)
    mine = info_ref[3]
    part = tokens // 2
    for s in range(kv_ref.shape[0] // part):
        rows = slice(s * part, (s + 1) * part)
        chip = s // 4
        if by_axis and s % 2 == 0:
            chip = chip % 2 * 2 + chip // 2
        gk = (gk_ref[rows, :] * scale).astype(BF)
        gv = gv_ref[rows, :].astype(BF)

        @pl.when(mine == s // 2 % 2)
        def _(s=s, chip=chip, gk=gk, gv=gv):
            near_ref[s % 2, chip, :, :width] = gk
            near_ref[s % 2, chip, :, width:] = gv

        @pl.when(mine != s // 2 % 2)
        def _(s=s, chip=chip, gk=gk, gv=gv):
            far_ref[s % 2, chip, :, :width] = gk
            far_ref[s % 2, chip, :, width:] = gv

    gq = (gqt_ref[...] * scale).T.astype(BF).astype(F32)
    cosine, sine = cos_ref[...], sin_ref[...]
    for h in range(heads):
        front = gq[h * tokens : (h + 1) * tokens, :half]
        back = gq[h * tokens : (h + 1) * tokens, half:]
        gq_ref[:, h * width : h * width + half] = (front * cosine + back * sine).astype(BF)
        gq_ref[:, h * width + half : (h + 1) * width] = (back * cosine - front * sine).astype(BF)


def attend_back(info, query, grad, out, log, cosine, sine, kv, start, index, by_axis):
    tokens, all_heads = grad.shape
    keys, width = kv.shape[0], kv.shape[1] // 2
    rows = tokens * (all_heads // width)
    blocks = keys // tokens
    return pl.pallas_call(
        functools.partial(
            attend_back_kernel, key_block(keys, 512), row_tile(rows), all_heads // width, by_axis
        ),
        out_shape=(
            jax.ShapeDtypeStruct((tokens, all_heads), BF),
            jax.ShapeDtypeStruct((2, blocks // 2, tokens // 2, 2 * width), BF),
            jax.ShapeDtypeStruct((2, blocks // 2, tokens // 2, 2 * width), BF),
        ),
        in_specs=[pl.BlockSpec(memory_space=pltpu.SMEM)] + in_vmem(9),
        out_specs=tuple(in_vmem(3)),
        scratch_shapes=[
            pltpu.VMEM((rows, width), BF),
            pltpu.VMEM((keys, width), F32),
            pltpu.VMEM((keys, width), F32),
            pltpu.VMEM((width, rows), F32),
            pltpu.VMEM((rows, width // 2), F32),
        ],
        compiler_params=pltpu.CompilerParams(vmem_limit_bytes=56 * 2**20),
        cost_estimate=brief(0),
        name="attend_back",
    )(info, query, grad, out, log, cosine, sine, kv, start, index)


def feed_kernel(tile, mid_ref, grad_ref, gate_ref, up_ref, hidden_ref, both_ref, part_ref):
    width = gate_ref.shape[1]

    def run(i, carry):
        rows = pl.ds(pl.multiple_of(i * tile, tile), tile)
        mid = mid_ref[rows, :]
        gate = dense(mid, gate_ref[...])
        up = dense(mid, up_ref[...])
        grad = grad_ref[rows, :]
        sigmoid = 1.0 / (1.0 + jnp.exp(-gate))
        active = gate * sigmoid
        hidden_ref[rows, :] = (active * up).astype(BF)
        grad_gate = (grad * up * sigmoid * (1.0 + gate * (1.0 - sigmoid))).astype(BF)
        grad_up = (grad * active).astype(BF)
        both_ref[rows, :width] = grad_gate
        both_ref[rows, width:] = grad_up
        part = dense_nt(grad_gate, gate_ref[...]) + dense_nt(grad_up, up_ref[...])
        part_ref[rows, :] = part.astype(BF)
        return carry

    lax.fori_loop(0, mid_ref.shape[0] // tile, run, None)


def feed_forward(mid, grad, gate, up):
    rows, model = mid.shape
    width = gate.shape[1]
    tile = next(t for t in (288, 192, 144, 96, 64, 48, 32, 16, rows) if rows % t == 0)
    return pl.pallas_call(
        functools.partial(feed_kernel, tile),
        out_shape=(
            jax.ShapeDtypeStruct((rows, width), BF),
            jax.ShapeDtypeStruct((rows, 2 * width), BF),
            jax.ShapeDtypeStruct((rows, model), BF),
        ),
        in_specs=in_vmem(4),
        out_specs=tuple(in_vmem(3)),
        compiler_params=pltpu.CompilerParams(vmem_limit_bytes=40 * 2**20),
        cost_estimate=brief(20),
        name="feed_forward",
    )(mid, grad, gate, up)


class Order:
    last = None


def brief(micros):
    return pl.CostEstimate(flops=int(micros * 1e8), bytes_accessed=0, transcendentals=0)


def call(kernel, outs, args, name, micros=0, scratch=(), grid=None, in_specs=None, out_specs=None, prefetch=None):
    out_shape = tuple(jax.ShapeDtypeStruct(*out) for out in outs)
    prefetch = in_order(prefetch)
    params = dict(
        out_shape=out_shape,
        compiler_params=pltpu.CompilerParams(vmem_limit_bytes=56 * 2**20),
        cost_estimate=brief(micros),
        name=name,
    )
    outs = placed_call(kernel, out_shape, args, params, scratch, grid, in_specs, out_specs, prefetch)
    Order.last = outs[0]
    return outs


def in_order(value):
    return value if Order.last is None else after(value, Order.last)


def wait(*values):
    Order.last = (Order.last, values)


def placed_call(kernel, out_shape, args, params, scratch, grid, in_specs, out_specs, prefetch):
    if grid is None:
        return pl.pallas_call(
            kernel,
            in_specs=[pl.BlockSpec(memory_space=pltpu.SMEM)] + in_vmem(len(args)),
            out_specs=tuple(in_vmem(len(out_shape))),
            scratch_shapes=list(scratch),
            **params,
        )(prefetch, *args)
    return pl.pallas_call(
        kernel,
        grid_spec=pltpu.PrefetchScalarGridSpec(
            num_scalar_prefetch=1,
            grid=grid,
            in_specs=in_specs,
            out_specs=tuple(out_specs),
            scratch_shapes=list(scratch),
        ),
        **params,
    )(prefetch, *args)


def once(shape, index):
    return pl.BlockSpec(shape, index, pipeline_mode=pl.Buffered(1))


def at_block(index, size):
    return pl.ds(pl.multiple_of(index * size, size), size)


CORE, RANK, SEQ = 3, 4, 5


def ahead(info_ref, shift, ranks):
    return lax.rem(info_ref[RANK] + shift, ranks)


def behind(info_ref, shift, ranks):
    return lax.rem(info_ref[RANK] + ranks - shift, ranks)


def chip_of(info_ref):
    return lax.div(info_ref[SEQ], 2)


def rank_blocks(info, index):
    return lambda i, info_ref: index(info_ref[RANK])


def project_kernel(
    info_ref, tokens_ref, gain_ref, down_ref, kv_weight_ref, latent_gain_ref, normed_ref, recip_ref, kv_ref, low_ref
):
    values = tokens_ref[...].astype(F32)
    normed, recip = norm_rows(values, gain_ref[...])
    normed_ref[...] = normed.astype(BF)
    recip_ref[...] = jnp.broadcast_to(recip, recip_ref.shape)
    rows = normed_ref.shape[0]
    low_ref[at_block(pl.program_id(0), rows), :] = dense(normed_ref[...], down_ref[...]).astype(BF)

    @pl.when(pl.program_id(0) == 0)
    def _():
        rest = latent_gain_ref[...]
        parts = []
        for _ in range(3):
            parts.append(rest.astype(BF))
            rest = rest - parts[-1].astype(F32)
        parts.append(jnp.zeros((EXTRA - 3, rest.shape[1]), BF))
        low_ref[low_ref.shape[0] - EXTRA :, :] = jnp.concatenate(parts, 0)

    kv_ref[...] = dense(normed_ref[...], kv_weight_ref[...])


EXTRA = 16


def project(info, tokens, gain, q_down, kv_weight, latent_gain):
    rows, model = tokens.shape
    tile = rows // 2
    widths = ((model, BF), (LANES, F32), (kv_weight.shape[1], F32))
    low = (rows + EXTRA, q_down.shape[1])
    return call(
        project_kernel,
        [((rows, width), dtype) for width, dtype in widths] + [(low, BF)],
        (tokens, gain.reshape(1, -1), q_down, kv_weight, latent_gain.reshape(1, -1)),
        "project",
        grid=(2,),
        in_specs=[
            pl.BlockSpec((tile, model), lambda i, w: (i, 0)),
            once((1, model), lambda i, w: (0, 0)),
            once(q_down.shape, lambda i, w: (0, 0)),
            once(kv_weight.shape, lambda i, w: (0, 0)),
            once((1, q_down.shape[1]), lambda i, w: (0, 0)),
        ],
        out_specs=[pl.BlockSpec((tile, width), lambda i, w: (i, 0)) for width, _ in widths]
        + [pl.BlockSpec(low, lambda i, w: (0, 0))],
        prefetch=info,
    )


def turn_kernel(info_ref, kv_ref, cos_ref, sin_ref, out_ref):
    half = cos_ref.shape[1]
    front, back = kv_ref[:, :half], kv_ref[:, half : 2 * half]
    cosine, sine = cos_ref[...], sin_ref[...]
    out_ref[:, :half] = (front * cosine - back * sine).astype(BF)
    out_ref[:, half : 2 * half] = (front * sine + back * cosine).astype(BF)
    out_ref[:, 2 * half :] = kv_ref[:, 2 * half :].astype(BF)


def turn(info, kv_pre, cosine, sine):
    return call(turn_kernel, [(kv_pre.shape, BF)], (kv_pre, cosine, sine), "turn", prefetch=info)[0]


def query_kernel(info_ref, latent_ref, own_ref, other_ref, low_ref, recip_ref, gain_ref, query_ref):
    rows = low_ref.shape[0]
    parts = latent_ref[rows:, :].astype(F32)
    gain_ref[...] = parts[0:1] + parts[1:2] + parts[2:3]
    normed, recip = norm_rows(latent_ref[:rows, :].astype(F32), gain_ref[...])
    low_ref[...] = normed.astype(BF)
    recip_ref[...] = jnp.broadcast_to(recip, recip_ref.shape)
    half = own_ref.shape[1]
    ranks = 4
    cols = latent_ref.shape[1] // ranks
    totals = [0.0, 0.0]
    for s in range(ranks):
        left = low_ref[:, at_block(behind(info_ref, s, ranks), cols)]
        for n, ref in enumerate((own_ref, other_ref)):
            totals[n] = totals[n] + dense(left, ref[s * cols : (s + 1) * cols, :])
    core = info_ref[CORE]
    query_ref[:, at_block(core, half)] = totals[0]
    query_ref[:, at_block(1 - core, half)] = totals[1]


def queries(info, latent, own, other):
    rows, width = latent.shape[0] - EXTRA, latent.shape[1]
    return call(
        query_kernel,
        [((rows, width), BF), ((rows, LANES), F32), ((1, width), F32), ((rows, 2 * own.shape[1]), F32)],
        (latent, own, other),
        "queries",
        prefetch=info,
    )


def latent_part_kernel(info_ref, grad_ref, own_ref, other_ref, *refs):
    outs, all_ref = refs[:-1], refs[-1]
    ranks, rows = len(outs), outs[0].shape[0]
    half, cols = own_ref.shape[1], own_ref.shape[0] // ranks
    core = info_ref[CORE]
    own_grad = grad_ref[:, at_block(core, half)]
    other_grad = grad_ref[:, at_block(1 - core, half)]
    for s in range(ranks):
        part = slice(s * cols, (s + 1) * cols)
        out = dense_nt(own_grad, own_ref[part, :]) + dense_nt(other_grad, other_ref[part, :])
        all_ref[:, at_block(behind(info_ref, s, ranks), cols)] = out.astype(BF)
    for s in range(ranks):
        outs[s][...] = all_ref[at_block(ahead(info_ref, s, ranks), rows), :]


def latent_parts(info, grad, own, other, ranks):
    rows, width = grad.shape[0], own.shape[0]
    return call(
        latent_part_kernel,
        [((rows // ranks, width), BF)] * ranks,
        (grad, own, other),
        "latent_parts",
        scratch=[pltpu.VMEM((rows, width), BF)],
        prefetch=info,
    )


def latent_back_kernel(info_ref, latent_ref, recip_ref, gain_ref, norm2_ref, *refs):
    parts, grad_ref = refs[:-1], refs[-1]
    grad_in = sum(part[...].astype(F32) for part in parts)
    latent = latent_ref[...].astype(F32)
    recip = recip_ref[:, 0:1]
    gained = grad_in * gain_ref[...]
    stat = jnp.sum(latent * gained, -1, keepdims=True)
    grad = recip * gained - latent * (recip * recip * recip * stat / latent.shape[1])
    rows, width = grad.shape
    grad_ref[:rows, :] = grad.astype(BF)
    sums = [norm2_ref[:, i * width : (i + 1) * width] for i in range(norm2_ref.shape[1] // width)]
    sums = jnp.concatenate(sums + [jnp.sum(grad_in * latent * recip, 0, keepdims=True)], 0)
    high = sums.astype(BF)
    low = (sums - high.astype(F32)).astype(BF)
    fill = jnp.zeros((EXTRA - 2 * sums.shape[0], width), BF)
    grad_ref[rows:, :] = jnp.concatenate([high, low, fill], 0)


def latent_back(info, latent, recip, gain, norm2, parts):
    rows, width = parts[0].shape
    return call(
        latent_back_kernel,
        [((rows + EXTRA, width), BF)],
        (latent, recip, gain, norm2, *parts),
        "latent_back",
        grid=(1,),
        in_specs=[
            pl.BlockSpec((rows, width), lambda i, w: (w[RANK], 0)),
            pl.BlockSpec((rows, LANES), lambda i, w: (w[RANK], 0)),
            pl.BlockSpec((1, width), lambda i, w: (0, 0)),
            pl.BlockSpec(norm2.shape, lambda i, w: (0, 0)),
        ]
        + [pl.BlockSpec((rows, width), lambda i, w: (0, 0)) for _ in parts],
        out_specs=[pl.BlockSpec((rows + EXTRA, width), lambda i, w: (0, 0))],
        prefetch=info,
    )[0]


def kv_back_kernel(info_ref, cos_ref, sin_ref, *refs):
    parts, out_ref = refs[:-1], refs[-1]
    total = sum(part[...].astype(F32) for part in parts).astype(BF).astype(F32)
    half = cos_ref.shape[1]
    front, back = total[:, :half], total[:, half : 2 * half]
    cosine, sine = cos_ref[...], sin_ref[...]
    out_ref[:, :half] = (front * cosine + back * sine).astype(BF)
    out_ref[:, half : 2 * half] = (back * cosine - front * sine).astype(BF)
    out_ref[:, 2 * half :] = total[:, 2 * half :].astype(BF)


def kv_back(info, cosine, sine, parts):
    rows, width = parts[0].shape
    return call(
        kv_back_kernel,
        [((rows, width), BF)],
        (cosine, sine, *parts),
        "kv_back",
        grid=(1,),
        in_specs=[pl.BlockSpec((rows, cosine.shape[1]), lambda i, w: (w[RANK], 0))] * 2
        + [pl.BlockSpec((rows, width), lambda i, w: (0, 0)) for _ in parts],
        out_specs=[pl.BlockSpec((rows, width), lambda i, w: (0, 0))],
        prefetch=info,
    )[0]


def mid_kernel(info_ref, branch_ref, tokens_ref, gain_ref, residual_ref, mid_ref, recip_ref):
    residual = tokens_ref[...].astype(F32) + branch_ref[...].astype(F32)
    normed, recip = norm_rows(residual, gain_ref[...])
    residual_ref[...] = residual
    mid_ref[...] = normed.astype(BF)
    recip_ref[...] = jnp.broadcast_to(recip, recip_ref.shape)


def mid_norm(info, branch, tokens, gain):
    rows, model = branch.shape
    whole = pl.BlockSpec((rows, model), lambda i, w: (0, 0))
    return call(
        mid_kernel,
        [((rows, model), F32), ((rows, model), BF), ((rows, LANES), F32)],
        (branch, tokens, gain.reshape(1, -1)),
        "mid_norm",
        grid=(1,),
        in_specs=[
            whole,
            pl.BlockSpec((rows, model), lambda i, w: (w[RANK], 0)),
            pl.BlockSpec((1, model), lambda i, w: (0, 0)),
        ],
        out_specs=[whole, whole, pl.BlockSpec((rows, LANES), lambda i, w: (0, 0))],
        prefetch=info,
    )


def mid_back_kernel(info_ref, grad_ref, residual_ref, recip_ref, gain_ref, out_grad_ref, branch_ref, gain_grad_ref):
    grad = grad_ref[...].astype(F32)
    residual = residual_ref[...]
    recip = recip_ref[:, 0:1]
    gained = grad * gain_ref[...]
    stat = jnp.sum(residual * gained, -1, keepdims=True)
    out = out_grad_ref[...].astype(F32) + recip * gained
    out = out - residual * (recip * recip * recip * stat / residual.shape[1])
    branch_ref[...] = out.astype(BF)
    gain_grad_ref[...] = jnp.sum(grad * residual * recip, 0, keepdims=True)


def mid_back(info, grad, residual, recip, gain, out_grad):
    rows, model = grad.shape
    whole = pl.BlockSpec((rows, model), lambda i, w: (0, 0))
    return call(
        mid_back_kernel,
        [((rows, model), BF), ((1, model), F32)],
        (grad, residual, recip, gain.reshape(1, -1), out_grad),
        "mid_back",
        grid=(1,),
        in_specs=[
            whole,
            whole,
            pl.BlockSpec((rows, LANES), lambda i, w: (0, 0)),
            pl.BlockSpec((1, model), lambda i, w: (0, 0)),
            pl.BlockSpec((rows, model), lambda i, w: (w[RANK], 0)),
        ],
        out_specs=[whole, pl.BlockSpec((1, model), lambda i, w: (0, 0))],
        prefetch=info,
    )


def matmul_kernel(dims, info_ref, left_ref, right_ref, *refs):
    out = lax.dot_general(left_ref[...], right_ref[...], (dims, ((), ())), preferred_element_type=F32)
    if len(refs) == 1:
        refs[0][...] = out.astype(BF)
        return
    outs, all_ref = refs[:-1], refs[-1]
    all_ref[...] = out.astype(BF)
    for s, out_ref in enumerate(outs):
        out_ref[...] = all_ref[at_block(ahead(info_ref, s, len(outs)), out_ref.shape[0]), :]


def matmul(info, left, right, transposed=False, parts=1):
    rows, depth = left.shape
    cols = right.shape[0 if transposed else 1]
    tile = next(t for t in ((512, 256, LANES) if transposed else (1024, 512, 256, LANES)) if cols % t == 0)
    if transposed:
        dims, spec = ((1,), (1,)), pl.BlockSpec((tile, depth), lambda i, w: (i, 0))
    else:
        dims, spec = ((1,), (0,)), pl.BlockSpec((depth, tile), lambda i, w: (0, i))
    outs = call(
        functools.partial(matmul_kernel, dims),
        [((rows // parts, cols), BF)] * parts,
        (left, right),
        "matmul",
        scratch=[pltpu.VMEM((rows, tile), BF)] if parts > 1 else [],
        grid=(cols // tile,),
        in_specs=[once((rows, depth), lambda i, w: (0, 0)), spec],
        out_specs=[pl.BlockSpec((rows // parts, tile), lambda i, w: (0, i))] * parts,
        prefetch=info,
    )
    return outs if parts > 1 else outs[0]


def quarter_order(info_ref):
    bit_x = lax.rem(chip_of(info_ref), 2)
    bit_y = lax.div(chip_of(info_ref), 2)
    return 1 - bit_x, 3 - bit_y, bit_x, 2 + bit_y


def product_kernel(counts, info_ref, *refs):
    outs, all_ref = refs[4 * len(counts) : 4 * len(counts) + 4], refs[-1]
    order = quarter_order(info_ref)
    rows = outs[0].shape[0]
    first = 0
    for n, count in enumerate(counts):
        own, other, own_right, other_right = refs[4 * n : 4 * n + 4]
        step = pl.program_id(0)

        def mixed(cols):
            out = dense_tn(own[:, cols], own_right[...])
            return (out + dense_tn(other[:, cols], other_right[...])).astype(BF)

        @pl.when((step >= first) & (step < first + count))
        def _():
            if rows >= 256:
                for out_ref, at in zip(outs, order):
                    out_ref[...] = mixed(at_block(at, rows))
            else:
                all_ref[...] = mixed(slice(None))
                for out_ref, at in zip(outs, order):
                    out_ref[...] = all_ref[at_block(at, rows), :]

        first += count


def pair_products(info, terms, tile):
    tokens, rows = terms[0][0].shape[0], terms[0][0].shape[1] // 2
    counts = [term[2].shape[1] // tile for term in terms]
    specs, args, first = [], [], 0
    for term, count in zip(terms, counts):
        specs += [once((tokens, rows), lambda i, w: (0, w[CORE]))] * 2
        place = lambda i, w, first=first, count=count: (0, jnp.clip(i - first, 0, count - 1))
        specs += [pl.BlockSpec((tokens, tile), place)] * 2
        args += term
        first += count
    return call(
        functools.partial(product_kernel, counts),
        [((rows // 4, first * tile), BF)] * 4,
        args,
        "pair_products",
        scratch=[pltpu.VMEM((rows, tile) if rows < 1024 else (16, LANES), BF)],
        grid=(first,),
        in_specs=specs,
        out_specs=[pl.BlockSpec((rows // 4, tile), lambda i, w: (0, i))] * 4,
        prefetch=info,
    )


def add_low(left, right):
    return (left.astype(F32) + right.astype(F32)).astype(BF)


def fold_near_kernel(info_ref, near_ref, got_ref, *outs):
    for out_ref, at in zip(outs, quarter_order(info_ref)):
        p, bit = lax.div(at, 2), lax.rem(at, 2)
        for other in range(2):
            chip = bit * 2 + other
            out_ref[other] = add_low(near_ref[p, chip], got_ref[p, chip])


def fold_near(info, near, got):
    _, chips, rows, cols = near.shape
    tile = rows // 3
    return call(
        fold_near_kernel,
        [((2, rows, cols), BF)] * 4,
        (near, got),
        "fold_near",
        grid=(3,),
        in_specs=[pl.BlockSpec((2, chips, tile, cols), lambda i, w: (0, 0, i, 0))] * 2,
        out_specs=[pl.BlockSpec((2, tile, cols), lambda i, w: (0, i, 0))] * 4,
        prefetch=info,
    )


def fold_first_kernel(info_ref, keep_first, got_first, keep_last, got_last, *outs):
    bit_x = lax.rem(chip_of(info_ref), 2)
    bit_y = lax.div(chip_of(info_ref), 2)
    outs[0][...] = add_low(keep_first[1 - bit_y], got_first[1 - bit_y])
    outs[1][...] = add_low(keep_last[1 - bit_x], got_last[1 - bit_x])
    outs[2][...] = add_low(keep_first[bit_y], got_first[bit_y])
    outs[3][...] = add_low(keep_last[bit_x], got_last[bit_x])


def fold_first(info, arrays, steps, micros=0):
    rows, cols = arrays[0].shape[1:]
    tile = rows // steps
    return call(
        fold_first_kernel,
        [((rows, cols), BF)] * 4,
        arrays,
        "fold_first",
        micros,
        grid=(steps,),
        in_specs=[pl.BlockSpec((2, tile, cols), lambda i, w: (0, i, 0))] * 4,
        out_specs=[pl.BlockSpec((tile, cols), lambda i, w: (i, 0))] * 4,
        prefetch=info,
    )


def fold_last_kernel(info_ref, keep_first, got_first, keep_last, got_last, out_ref):
    out_ref[0] = add_low(keep_first[...], got_first[...])
    out_ref[1] = add_low(keep_last[...], got_last[...])


def fold_last(info, arrays, steps):
    rows, cols = arrays[0].shape
    tile = rows // steps
    return call(
        fold_last_kernel,
        [((2, rows, cols), BF)],
        arrays,
        "fold_last",
        grid=(steps,),
        in_specs=[pl.BlockSpec((tile, cols), lambda i, w: (i, 0))] * 4,
        out_specs=[pl.BlockSpec((2, tile, cols), lambda i, w: (0, i, 0))],
        prefetch=info,
    )[0]


def fold_kv_kernel(info_ref, keep_first, got_first, keep_last, got_last, *refs):
    outs, all_ref = refs[:-1], refs[-1]
    half = keep_first.shape[0]
    all_ref[:half, :] = add_low(keep_first[...], got_first[...])
    all_ref[half:, :] = add_low(keep_last[...], got_last[...])
    for s, out_ref in enumerate(outs):
        out_ref[...] = all_ref[at_block(ahead(info_ref, s, len(outs)), out_ref.shape[0]), :]


def fold_kv(info, arrays, ranks):
    rows, cols = arrays[0].shape
    return call(
        fold_kv_kernel,
        [((2 * rows // ranks, cols), BF)] * ranks,
        arrays,
        "fold_kv",
        scratch=[pltpu.VMEM((2 * rows, cols), BF)],
        prefetch=info,
    )


def fold_up_kernel(info_ref, keep_first, got_first, keep_last, got_last, *refs):
    ups, all_ref = refs[:-1], refs[-1]
    all_ref[0] = add_low(keep_first[...], got_first[...])
    all_ref[1] = add_low(keep_last[...], got_last[...])
    for s, up_ref in enumerate(ups):
        up_ref[...] = all_ref[:, at_block(ahead(info_ref, s, len(ups)), up_ref.shape[1]), :]


def fold_up(info, arrays, ranks):
    rows, cols = arrays[0].shape
    return call(
        fold_up_kernel,
        [((2, rows // ranks, cols), BF)] * ranks,
        arrays,
        "fold_up",
        scratch=[pltpu.VMEM((2, rows, cols), BF)],
        prefetch=info,
    )


def pack_up_kernel(info_ref, *refs):
    ups, all_ref = refs[:-1], refs[-1]
    for s, up_ref in enumerate(ups):
        all_ref[:, at_block(behind(info_ref, s, len(ups)), up_ref.shape[1]), :] = up_ref[...]


def pack_up(info, ups):
    _, rows, cols = ups[0].shape
    return call(pack_up_kernel, [((2, rows * len(ups), cols), BF)], ups, "pack_up", prefetch=info)[0]


def layer_kernel(info_ref, residual_ref, *refs):
    parts, out_ref = refs[:-1], refs[-1]
    out_ref[...] = (residual_ref[...] + sum(part[...].astype(F32) for part in parts)).astype(BF)


def place_kernel(info_ref, *refs):
    parts, out_ref = refs[:-1], refs[-1]
    for s, part in enumerate(parts):
        pl.when(pl.program_id(0) == s)(lambda part=part: out_ref.__setitem__(..., part[...]))


def place(info, parts):
    rows, cols = parts[0].shape
    ranks = len(parts)
    return call(
        place_kernel,
        [((ranks * rows, cols), BF)],
        parts,
        "place",
        grid=(ranks,),
        in_specs=[once((rows, cols), lambda i, w: (0, 0))] * ranks,
        out_specs=[pl.BlockSpec((rows, cols), lambda i, w: (behind(w, i, ranks), 0))],
        prefetch=info,
    )[0]


def input_back_kernel(
    ranks, info_ref, tokens_ref, branch_ref, gain_ref, kv_weight_ref, recip_ref, latent_ref, kv_pre_ref, *refs
):
    latents, kvs, downs = refs[:ranks], refs[ranks : 2 * ranks], refs[2 * ranks : 3 * ranks]
    grad_in_ref, small_ref, own_ref, kv_ref, all_ref, sums_ref = refs[3 * ranks :]
    rows = kvs[0].shape[0]
    cols = own_ref.shape[1]
    sums = 0.0
    for s in range(ranks):
        at = at_block(behind(info_ref, s, ranks), rows)
        all_ref[at, :] = latents[s][:rows, :]
        sums = sums + latents[s][rows:, :].astype(F32)
        kv_ref[at, :] = kvs[s][...]
    grad = dense_nt(kv_ref[...], kv_weight_ref[...])
    for s in range(ranks):
        at = at_block(behind(info_ref, s, ranks), cols)
        grad = grad + dense_nt(all_ref[:, at], downs[s][...])
    own_ref[...] = all_ref[:, at_block(info_ref[RANK], cols)]
    recip = recip_ref[:, 0:1]
    latent = latent_ref[: all_ref.shape[0], :].astype(F32)
    stat = jnp.sum(all_ref[...].astype(F32) * latent, -1, keepdims=True)
    stat = stat + jnp.sum(kv_ref[...].astype(F32) * kv_pre_ref[...], -1, keepdims=True)
    tokens = tokens_ref[...].astype(F32)
    model = tokens.shape[1] * ranks
    out = branch_ref[...].astype(F32) + recip * gain_ref[...] * grad
    grad_in_ref[...] = out - tokens * (recip * recip * stat / model)
    count = sums.shape[0] // 16 * 3
    sums = sums[:count] + sums[count : 2 * count]
    sums_ref[...] = sums[count - 1 :]
    norm1 = jnp.sum(grad * tokens * recip, 0, keepdims=True)
    lines = [sums[r : r + 1, i * cols : (i + 1) * cols] for r in range(count - 1) for i in range(sums.shape[1] // cols)]
    lines += [norm1[:, i * cols : (i + 1) * cols] for i in range(norm1.shape[1] // cols)]
    lines.append(sums_ref[:, at_block(info_ref[RANK], cols)])
    lines += [jnp.zeros_like(lines[0])] * (small_ref.shape[0] - len(lines))
    small_ref[...] = jnp.concatenate(lines, 0).astype(BF)


def input_back(info, tokens, branch, gain, kv_weight, recip, latent, kv_pre, latents, kvs, downs):
    ranks = len(latents)
    rows, model = tokens.shape
    cols = model // ranks
    width, down = kv_weight.shape[1], downs[0].shape[1]
    whole = lambda array: pl.BlockSpec(array.shape, lambda i, w: (0, 0))
    wide = pl.BlockSpec((rows, cols), lambda i, w: (0, w[RANK]))
    outs = [((rows, cols), F32), ((16, down), BF), ((rows, down), BF), ((rows, width), BF)]
    return call(
        functools.partial(input_back_kernel, ranks),
        outs,
        (tokens, branch, gain.reshape(1, -1), kv_weight, recip, latent, kv_pre, *latents, *kvs, *downs),
        "input_back",
        scratch=[pltpu.VMEM((rows, latent.shape[1]), BF), pltpu.VMEM((1, latent.shape[1]), F32)],
        grid=(1,),
        in_specs=[
            wide,
            wide,
            pl.BlockSpec((1, cols), lambda i, w: (0, w[RANK])),
            pl.BlockSpec((cols, width), lambda i, w: (w[RANK], 0)),
        ]
        + [whole(array) for array in (recip, latent, kv_pre, *latents, *kvs, *downs)],
        out_specs=[pl.BlockSpec(shape, lambda i, w: (0, 0)) for shape, _ in outs],
        prefetch=info,
    )


def last_products_kernel(info_ref, normed_ref, latent_ref, kv_ref, small_ref, out_ref):
    rows, width = normed_ref.shape[1], latent_ref.shape[1]
    out_ref[:rows, :] = dense_tn(normed_ref[...], latent_ref[...]).astype(BF)
    count = (out_ref.shape[0] - rows - small_ref.shape[0]) // 2
    wide = dense_tn(normed_ref[:, at_block(info_ref[RANK], count)], kv_ref[...]).astype(BF)
    out_ref[rows : rows + count, :] = wide[:, :width]
    out_ref[rows + count : rows + 2 * count, :] = wide[:, width:]
    out_ref[rows + 2 * count :, :] = small_ref[...]


def last_products(info, normed, latent, kv, small, ranks):
    model, width = normed.shape[1], latent.shape[1]
    shape = (model + 2 * model // ranks + small.shape[0], width)
    return call(
        last_products_kernel, [(shape, BF)], (normed, latent, kv, small), "last_products", prefetch=info
    )[0]


def last_kernel(info_ref, in_ref, down_ref, kv_ref, small_ref):
    rows, width = down_ref.shape
    count = kv_ref.shape[0]
    down_ref[...] = in_ref[:rows, :].astype(F32)
    kv_ref[:, :width] = in_ref[rows : rows + count, :].astype(F32)
    kv_ref[:, width:] = in_ref[rows + count : rows + 2 * count, :].astype(F32)
    small_ref[...] = in_ref[rows + 2 * count :, :].astype(F32)


def store_feed(part, at, gate_ref, up_ref, down_ref):
    rows, width = part.shape[0], gate_ref.shape[1]
    block = slice(at * rows, (at + 1) * rows)
    gate_ref[block, :] = part[:, :width].astype(F32)
    up_ref[block, :] = part[:, width : 2 * width].astype(F32)
    down_ref[:, block] = part[:, 2 * width :].astype(F32).T


def store_same(part, at, out_ref):
    rows = part.shape[0]
    out_ref[at * rows : (at + 1) * rows, :] = part.astype(F32)


def unpack_up_kernel(info_ref, *refs):
    out_ref = refs[-1]
    for mask, ref in enumerate(refs[:-1]):
        source = lax.bitwise_xor(info_ref[SEQ], mask)
        core, chip = lax.rem(source, 2), lax.div(source, 2)
        _, rows, cols = ref.shape
        rows = rows // (out_ref.shape[1] // cols)
        for p in range(2):
            place = lax.rem(chip, 2) * 2 + lax.div(chip, 2) if p == 0 else chip
            at = at_block(core * 8 + p * 4 + place, rows)
            for r in range(out_ref.shape[1] // cols):
                block = ref[p, r * rows : (r + 1) * rows, :].astype(F32)
                out_ref[at, r * cols : (r + 1) * cols] = block


def unpack_up(info, pieces, shape):
    return call(unpack_up_kernel, [(shape, F32)], pieces, "unpack_up", prefetch=info)[0]


def unpack_kernel(store, info_ref, in_ref, *out_refs):
    part = lax.rem(pl.program_id(0), 2)
    for chip in range(4):
        turned = chip % 2 * 2 + chip // 2
        pl.when(part == 0)(lambda chip=chip, at=turned: store(in_ref[chip], at, *out_refs))
        pl.when(part == 1)(lambda chip=chip: store(in_ref[chip], chip, *out_refs))


def unpack(info, whole, store, shapes, along):
    _, _, rows, cols = whole.shape
    whole = whole.reshape(4, 2, 2, rows, cols)
    out_specs = []
    for (height, width), dim in zip(shapes, along):
        if dim == 0:
            out_specs.append(pl.BlockSpec((height // 4, width), lambda i, w: (i, 0)))
        else:
            out_specs.append(pl.BlockSpec((height, width // 4), lambda i, w: (0, i)))
    return call(
        functools.partial(unpack_kernel, store),
        [(shape, F32) for shape in shapes],
        (whole,),
        "unpack",
        grid=(4,),
        in_specs=[
            pl.BlockSpec((4, None, None, rows, cols), lambda i, w: (0, i // 2, i % 2, 0, 0))
        ],
        out_specs=out_specs,
        prefetch=info,
    )


def bit_of(index, bit):
    return (index >> bit) & 1


def exchange(value, mask):
    count = lax.axis_size("seq")
    return lax.ppermute(value, "seq", [(i, i ^ mask) for i in range(count)])


def swap(value, bit):
    return exchange(value, 1 << bit)


def ring(value, shift):
    if not shift:
        return value
    ranks = lax.axis_size("rank")
    return lax.ppermute(value, "rank", [(i, (i + shift) % ranks) for i in range(ranks)])


def rings(values):
    return [ring(value, s) for s, value in enumerate(values)]


def both(first, last):
    return swap(first, 1), swap(last, 2)


def sum_over(value, axis):
    count = lax.axis_size(axis)
    mask = 1
    while mask < count:
        value = value + lax.ppermute(value, axis, [(i, i ^ mask) for i in range(count)])
        mask *= 2
    return value


def after(value, *others):
    return lax.optimization_barrier((value, others))[0]


def per_device_fast(
    tokens_in,
    norm1_gain,
    q_down,
    latent_gain,
    q_up,
    kv_weight,
    out_weight,
    norm2_gain,
    gate_weight,
    up_weight,
    down_weight,
    doc_ids,
    out_grad,
):
    Order.last = None
    row_count, model_width = tokens_in.shape
    ranks = lax.axis_size("rank")
    rank_ix = lax.axis_index("rank")
    seq_ix = lax.axis_index("seq")
    head_dim = kv_weight.shape[1] // 2
    local_heads = out_weight.shape[0] // head_dim
    first_row = seq_ix * row_count
    core = bit_of(seq_ix, 0)
    rank_cols = q_down.shape[1]
    rank_width = rank_cols * ranks
    col_count = model_width // ranks

    up_cols = q_up.shape[1] // ranks
    half_cols = up_cols // 2
    blocks = [
        lax.dynamic_slice_in_dim(
            q_up, lax.rem(rank_ix + s, ranks) * up_cols + core * half_cols, half_cols, 1
        )
        for s in range(ranks)
    ]
    tokens_late = after(tokens_in, blocks)
    up_own = jnp.concatenate(rings(blocks), 0)
    up_other = swap(up_own, 0)

    ids_local = lax.dynamic_slice_in_dim(doc_ids, first_row, row_count, 0)
    start = jnp.sum((doc_ids[None, :] < ids_local[:, None]).astype(I32), 1)
    query_index = first_row + jnp.arange(row_count, dtype=I32)
    position = (query_index - start).astype(F32)
    half_dim = head_dim // 2
    freqs = BASE ** (-jnp.arange(half_dim, dtype=F32) / half_dim)
    angle = position[:, None] * freqs[None, :]
    cosine, sine = jnp.cos(angle), jnp.sin(angle)
    start_rows = jnp.tile(start, local_heads)[None]
    index_rows = jnp.tile(query_index, local_heads)[None]
    place_info = jnp.stack([first_row, first_row, first_row, core, rank_ix, seq_ix]).astype(I32)
    info = jnp.stack([first_row, start[0], start[-1], core, rank_ix, seq_ix]).astype(I32)

    normed_low, recip1, kv_pre, latent = project(
        place_info, tokens_late, norm1_gain, q_down, kv_weight, latent_gain
    )
    latent_all = lax.all_gather(latent, "rank", axis=1, tiled=True)

    kv_local = turn(place_info, kv_pre, cosine, sine)
    half_rows = row_count // 2
    by_x, by_y = lax.optimization_barrier(both(kv_local, kv_local))
    top, bottom = swap(by_x[:half_rows], 2), swap(by_y[half_rows:], 1)
    pieces = [(kv_local, 0, 0), (by_x, 2, 0), (by_y, 4, 0), (top, 6, 0), (bottom, 6, half_rows)]
    pieces += [(swap(array, 0), mask ^ 1, offset) for array, mask, offset in pieces]

    latent_low, recip_c, gain_all, query_pre = queries(place_info, latent_all, up_own, up_other)
    query, attn_vals, attn_low, log_total, kv_all = attend(
        in_order(info), query_pre, cosine, sine, start, pieces
    )
    Order.last = attn_low

    branch_part = matmul(info, attn_low, out_weight)
    branch = lax.psum_scatter(branch_part, "rank", scatter_dimension=0, tiled=True)
    grad_hidden = dense_nt(after(out_grad, branch_part), down_weight)
    out_grad_pair = swap(after(out_grad, branch_part), 0)
    attn_pair = swap(attn_low, 0)
    piece_cols = rank_cols // 16
    latent_cut = jnp.transpose(
        after(latent_low, branch_part).reshape(row_count, ranks, 16, piece_cols), (0, 2, 1, 3)
    ).reshape(row_count, rank_width)
    latent_pair = swap(latent_cut, 0)
    down_blocks = [
        lax.dynamic_slice_in_dim(
            after(q_down, branch_part), lax.rem(rank_ix + s, ranks) * col_count, col_count, 0
        )
        for s in range(ranks)
    ]
    branch = after(
        branch, grad_hidden, out_grad_pair, attn_pair, latent_pair, latent_cut, down_blocks
    )
    residual, mid_own, recip2 = mid_norm(info, branch, tokens_in, norm2_gain)
    mid_low = lax.all_gather(mid_own, "rank", axis=0, tiled=True)

    downs = rings(after(down_blocks, mid_low))
    mid_pair = swap(mid_low, 0)
    hidden_low, grad_both, grad_mid_part = feed_forward(
        mid_low, grad_hidden, gate_weight, up_weight
    )
    Order.last = hidden_low
    hidden_low, grad_both, grad_mid_part = after((hidden_low, grad_both, grad_mid_part), downs)
    grad_mid = lax.psum_scatter(grad_mid_part, "rank", scatter_dimension=0, tiled=True)
    both_pair, hidden_pair = swap(grad_both, 0), swap(hidden_low, 0)
    feed_parts = matmul(info, hidden_low, down_weight, parts=ranks)
    feed_width = gate_weight.shape[1]
    send_first, send_last, keep_first, keep_last = pair_products(
        info,
        [
            (mid_low, mid_pair, grad_both, both_pair),
            (out_grad, out_grad_pair, hidden_low, hidden_pair),
        ],
        feed_width,
    )
    grad_mid = after(grad_mid, send_first)
    branch_own, norm2_part = mid_back(info, grad_mid, residual, recip2, norm2_gain, out_grad)
    grad_branch = lax.all_gather(branch_own, "rank", axis=0, tiled=True)

    two = lambda array: array.reshape((2, -1) + array.shape[1:])
    first, last = both(send_first, send_last)
    arrays = [two(array) for array in (keep_first, first, keep_last, last)]
    arrays = fold_first(info, arrays, 4, 10000)
    last, first = both(arrays[1], arrays[0])
    grad_branch = after(grad_branch, arrays[0])
    grad_attn = matmul(info, grad_branch, out_weight, True)
    branch_pair = swap(grad_branch, 0)
    outs = pair_products(info, [(attn_low, attn_pair, grad_branch, branch_pair)], up_cols)
    feed_piece = fold_last(info, (arrays[2], first, arrays[3], last), 4)
    feed_whole = lax.all_gather(feed_piece, "seq", axis=0, tiled=False)
    feed_sums = rings(after(feed_parts, grad_branch))
    first, last = both(outs[0], outs[1])
    grad_query, near, far = attend_back(
        in_order(info), query, grad_attn, attn_vals, log_total, cosine, sine, kv_all,
        start_rows, index_rows, True,
    )
    grad_query, near, far = after((grad_query, near, far), feed_sums, first, last)
    Order.last = grad_query

    latent_grads = rings(latent_parts(info, grad_query, up_own, up_other, ranks))
    query_pair = swap(grad_query, 0)
    arrays = fold_near(info, near, swap(far, 0))
    kv_first, kv_last = both(arrays[0], arrays[1])
    outs = [two(array) for array in (outs[2], first, outs[3], last)]
    outs = fold_first(info, outs, 1)
    ups = pair_products(info, [(latent_cut, latent_pair, grad_query, query_pair)], up_cols)
    wait(latent_grads, kv_first, kv_last)

    latent_own = latent_back(info, latent_all, recip_c, gain_all, norm2_part, latent_grads)
    latent_blocks = rings([latent_own] * ranks)
    arrays = fold_first(info, (arrays[2], kv_first, arrays[3], kv_last), 1)
    kv_last, kv_first = both(arrays[1], arrays[0])
    last, first = both(*in_order((outs[1], outs[0])))
    kv_sums = rings(fold_kv(info, (arrays[2], kv_first, arrays[3], kv_last), ranks))
    ups_first, ups_last = both(*in_order(ups[:2]))
    ups = fold_first(info, [two(array) for array in (ups[2], ups_first, ups[3], ups_last)], 1)
    ups_last, ups_first = both(ups[1], ups[0])
    layer_own = call(
        layer_kernel, [(residual.shape, BF)], (residual, *feed_sums), "layer", prefetch=info
    )[0]
    joined, *latent_blocks = lax.optimization_barrier((info, *latent_blocks))

    ups = rings(fold_up(joined, (ups[2], ups_first, ups[3], ups_last), ranks))
    kv_own = kv_back(info, cosine, sine, kv_sums)
    kv_blocks = rings([kv_own] * ranks)
    out_piece = fold_last(info, (outs[2], first, outs[3], last), 1)
    out_whole = lax.all_gather(out_piece, "seq", axis=0, tiled=False)
    wait(kv_blocks)

    grad_in, small, latent_cols, grad_kv = input_back(
        info, tokens_in, grad_branch, norm1_gain, kv_weight, recip1, latent_all, kv_pre,
        latent_blocks, kv_blocks, downs,
    )
    last = last_products(info, normed_low, latent_cols, grad_kv, small, ranks)
    last = lax.psum(last, "seq")
    up_piece = pack_up(info, ups)
    layer_blocks = rings([in_order(layer_own)] * ranks)
    up_pieces = [up_piece] + [exchange(in_order(up_piece), mask) for mask in (1, 2)]
    shape = gate_weight.shape
    grad_gate, grad_up, grad_down = unpack(
        info, feed_whole, store_feed, (shape, shape, shape[::-1]), (0, 0, 1)
    )
    up_pieces += [exchange(in_order(up_piece), mask) for mask in range(3, 8)]
    grad_out = unpack(info, out_whole, store_same, [out_weight.shape], [0])[0]
    layer_out = place(info, layer_blocks)
    grad_q_up = unpack_up(info, up_pieces, q_up.shape)
    grad_q_down, grad_kv_weight, small = call(
        last_kernel,
        [(q_down.shape, F32), ((col_count, 2 * head_dim), F32), (small.shape, F32)],
        (last,),
        "last",
        prefetch=info,
    )

    small = small.reshape(-1)
    norm1 = small[model_width : model_width + col_count]
    grad_latent_gain = small[model_width + col_count : model_width + col_count + rank_cols]
    grad_norm2 = small[:model_width]
    return (
        layer_out,
        grad_in,
        norm1,
        grad_q_down,
        grad_latent_gain,
        grad_q_up,
        grad_kv_weight,
        grad_out,
        grad_norm2,
        grad_gate,
        grad_up,
        grad_down,
    )


def add_low(left, right):
    return (left.astype(F32) + right.astype(F32)).astype(BF)


def halve(value, axis, bit, seq_ix):
    own = bit_of(seq_ix, bit)
    keep = lax.dynamic_index_in_dim(value, own, axis, keepdims=False)
    send = lax.dynamic_index_in_dim(value, 1 - own, axis, keepdims=False)
    return add_low(keep, swap(send, bit))


def scatter_chips(value, seq_ix):
    bits = value.shape[0].bit_length() - 1
    shape = (2,) * bits + value.shape[2:]
    first, last = value[:, 0].reshape(shape), value[:, 1].reshape(shape)
    first_axes = list(range(bits))
    last_axes = list(range(bits))
    for step in range(bits):
        bit = step + 1
        axis = first_axes.index(bits - bit)
        first = halve(first, axis, bit, seq_ix)
        del first_axes[axis]
        bit = bits - step
        axis = last_axes.index(bits - bit)
        last = halve(last, axis, bit, seq_ix)
        del last_axes[axis]
    return jnp.stack([first, last])


def scatter_rows(near, far, seq_ix):
    return scatter_chips(add_low(near, swap(far, 0)), seq_ix)


def split_product(left, right, seq_ix):
    chips = lax.axis_size("seq") // 2
    rows = left.shape[1] // 2
    own = bit_of(seq_ix, 0)
    parts = []
    for core in (own, 1 - own):
        piece = lax.dynamic_slice_in_dim(left, core * rows, rows, 1)
        parts.append(dense_tn(piece, right).astype(BF))
    shape = (2, chips, rows // (2 * chips), right.shape[1])
    return [jnp.swapaxes(part.reshape(shape), 0, 1) for part in parts]


def gather_rows(piece):
    seq = lax.axis_size("seq")
    whole = lax.all_gather(piece, "seq", axis=0, tiled=False)
    whole = whole.reshape((seq // 2, 2) + piece.shape)
    whole = jnp.transpose(whole, (1, 2, 0, 3, 4))
    return whole.reshape(seq * piece.shape[0] * piece.shape[1], piece.shape[2])


def reduce_product(left, right, seq_ix):
    near, far = split_product(left, right, seq_ix)
    return gather_rows(scatter_rows(near, far, seq_ix)).astype(F32)


def high_low(values):
    high = values.astype(BF)
    return [high, (values - high.astype(F32)).astype(BF)]


def per_device_general(
    tokens_in,
    norm1_gain,
    q_down,
    latent_gain,
    q_up,
    kv_weight,
    out_weight,
    norm2_gain,
    gate_weight,
    up_weight,
    down_weight,
    doc_ids,
    out_grad,
):
    row_count, model_width = tokens_in.shape
    rank_count = lax.axis_size("rank")
    seq_count = lax.axis_size("seq")
    rank_ix = lax.axis_index("rank")
    seq_ix = lax.axis_index("seq")
    head_dim = kv_weight.shape[1] // 2
    local_heads = out_weight.shape[0] // head_dim
    first_row = seq_ix * row_count
    core = bit_of(seq_ix, 0)
    own_rows = row_count // rank_count
    rank_cols = q_down.shape[1]
    rank_width = rank_cols * rank_count

    half_rows = q_up.shape[0] // 2
    up_half = lax.dynamic_slice_in_dim(q_up, core * half_rows, half_rows, 0)
    up_half = lax.all_to_all(up_half, "rank", 1, 0, tiled=True)
    up_other = swap(up_half, 0)
    up_half = up_half.reshape(rank_count, 1, half_rows, -1)
    up_other = up_other.reshape(rank_count, 1, half_rows, -1)
    q_up_own = jnp.concatenate(
        [jnp.where(core == 0, up_half, up_other), jnp.where(core == 0, up_other, up_half)], 1
    ).reshape(rank_width, -1)

    ids_local = lax.dynamic_slice_in_dim(doc_ids, first_row, row_count, 0)
    start = jnp.sum((doc_ids[None, :] < ids_local[:, None]).astype(I32), 1)
    query_index = first_row + jnp.arange(row_count, dtype=I32)
    position = (query_index - start).astype(F32)
    half_dim = head_dim // 2
    freqs = BASE ** (-jnp.arange(half_dim, dtype=F32) / half_dim)
    angle = position[:, None] * freqs[None, :]
    cosine_rows, sine_rows = jnp.cos(angle), jnp.sin(angle)
    start_rows = jnp.tile(start, local_heads)[None]
    index_rows = jnp.tile(query_index, local_heads)[None]
    info = jnp.stack([first_row, start[0], start[-1], core]).astype(I32)

    tokens = tokens_in.astype(F32)
    normed_in, recip1 = norm_rows(tokens, norm1_gain)
    normed_low = normed_in.astype(BF)
    kv_pre = dense(normed_low, kv_weight)
    key_local = rotate(kv_pre[:, :head_dim], cosine_rows, sine_rows)
    kv_local = jnp.concatenate([key_local, kv_pre[:, head_dim:]], -1).astype(BF)
    kv_all = lax.all_gather(kv_local, "seq", axis=0, tiled=True)

    latent = dense(normed_low, q_down)
    high, rest = high_low(latent_gain)
    low = (latent_gain - high.astype(F32) - rest.astype(F32)).astype(BF)
    gain_rows = jnp.stack([high, rest, low] + [jnp.zeros_like(high)] * 13)
    gathered = lax.all_gather(
        jnp.concatenate([latent.astype(BF), gain_rows], 0), "rank", axis=1, tiled=True
    ).astype(F32)
    latent_all = gathered[:row_count]
    gain_all = gathered[row_count] + gathered[row_count + 1] + gathered[row_count + 2]
    recip_c = lax.rsqrt(jnp.mean(latent_all * latent_all, -1, keepdims=True) + EPS)
    latent_low = (latent_all * recip_c * gain_all).astype(BF)
    query_pre = dense(latent_low, q_up_own)

    query, attn_vals, attn_low, log_total, kv_all = attend(
        info, query_pre, cosine_rows, sine_rows, start, [(kv_all, None, 0)]
    )
    branch = lax.psum_scatter(
        dense(attn_low, out_weight).astype(BF), "rank", scatter_dimension=0, tiled=True
    )
    tokens_rows = lax.dynamic_slice_in_dim(tokens_in, rank_ix * own_rows, own_rows, 0)
    residual = tokens_rows.astype(F32) + branch.astype(F32)
    normed_mid, recip2 = norm_rows(residual, norm2_gain)
    mid_low = lax.all_gather(normed_mid.astype(BF), "rank", axis=0, tiled=True)

    grad_hidden = dense_nt(out_grad, down_weight)
    gate_pre = dense(mid_low, gate_weight)
    up_pre = dense(mid_low, up_weight)
    sigmoid_gate = jax.nn.sigmoid(gate_pre)
    activated = gate_pre * sigmoid_gate
    hidden_low = (activated * up_pre).astype(BF)
    grad_gate_pre = (
        grad_hidden * up_pre * sigmoid_gate * (1.0 + gate_pre * (1.0 - sigmoid_gate))
    ).astype(BF)
    grad_up_pre = (grad_hidden * activated).astype(BF)
    grad_mid = lax.psum_scatter(
        (dense_nt(grad_gate_pre, gate_weight) + dense_nt(grad_up_pre, up_weight)).astype(BF),
        "rank",
        scatter_dimension=0,
        tiled=True,
    ).astype(F32)
    feed_out = lax.psum_scatter(
        dense(hidden_low, down_weight).astype(BF), "rank", scatter_dimension=0, tiled=True
    )
    layer_out = lax.all_gather(
        (residual + feed_out.astype(F32)).astype(BF), "rank", axis=0, tiled=True
    )
    grad_gate = reduce_product(mid_low, grad_gate_pre, seq_ix)
    grad_up = reduce_product(mid_low, grad_up_pre, seq_ix)
    grad_down = reduce_product(hidden_low, out_grad, seq_ix)

    gained_mid = grad_mid * norm2_gain
    stat_mid = jnp.sum(residual * gained_mid, -1, keepdims=True)
    out_grad_rows = lax.dynamic_slice_in_dim(out_grad, rank_ix * own_rows, own_rows, 0)
    grad_residual = (
        out_grad_rows.astype(F32)
        + recip2 * gained_mid
        - residual * recip2**3 * stat_mid / model_width
    )
    grad_norm2 = jnp.sum(grad_mid * residual * recip2, 0)
    grad_branch = lax.all_gather(grad_residual.astype(BF), "rank", axis=0, tiled=True)
    grad_attn = dense_nt(grad_branch, out_weight).astype(BF)
    grad_out = reduce_product(attn_low, grad_branch, seq_ix)
    grad_query, near, far = attend_back(
        info, query, grad_attn, attn_vals, log_total, cosine_rows, sine_rows, kv_all,
        start_rows, index_rows, False,
    )

    chips = seq_count // 2
    summed = scatter_rows(jnp.swapaxes(near, 0, 1), jnp.swapaxes(far, 0, 1), seq_ix)
    summed = lax.psum(summed.reshape(row_count, 2 * head_dim), "rank").astype(F32)
    key_back = rotate(summed[:, :head_dim], cosine_rows, -sine_rows)
    grad_kv = jnp.concatenate([key_back, summed[:, head_dim:]], -1).astype(BF)

    grad_latent_part = dense_nt(grad_query, q_up_own).astype(BF)
    norm2_rows = jnp.concatenate(high_low(grad_norm2)).reshape(-1, rank_width)
    extra = norm2_rows.shape[0]
    norm2_rows = jnp.pad(norm2_rows, ((0, -extra % 16), (0, 0)))
    over_ranks = lax.psum(jnp.concatenate([grad_latent_part, norm2_rows], 0), "rank").astype(F32)
    grad_latent_in = over_ranks[:row_count]
    grad_norm2 = jnp.sum(
        over_ranks[row_count : row_count + extra].reshape(2, model_width), 0
    )
    gained_latent = grad_latent_in * gain_all
    stat_latent = jnp.sum(latent_all * gained_latent, -1, keepdims=True)
    grad_latent = (
        recip_c * gained_latent - latent_all * recip_c**3 * stat_latent / rank_width
    ).astype(BF)
    own_latent = lambda v: lax.dynamic_slice_in_dim(v, rank_ix * rank_cols, rank_cols, 1)
    grad_latent_gain = jnp.sum(own_latent(grad_latent_in) * latent * recip_c, 0)

    near, far = split_product(grad_query, latent_low, seq_ix)
    piece = scatter_rows(near, far, seq_ix)
    piece = lax.all_to_all(piece, "rank", 2, 0, tiled=True)
    piece = piece.reshape(rank_count * 2, piece.shape[1], rank_cols)
    whole = lax.all_gather(piece, "seq", axis=0, tiled=False)
    whole = whole.reshape(chips, 2, rank_count, 2, piece.shape[1], rank_cols)
    grad_q_up = jnp.transpose(whole, (5, 2, 1, 3, 0, 4)).reshape(rank_cols, -1).astype(F32)

    col_count = model_width // rank_count
    col_start = rank_ix * col_count
    cols = lambda v: lax.dynamic_slice_in_dim(v, col_start, col_count, v.ndim - 1)
    q_down_rows = lax.all_to_all(q_down, "rank", 0, 1, tiled=True)
    kv_rows = lax.dynamic_slice_in_dim(kv_weight, col_start, col_count, 0)
    grad_normed = dense_nt(grad_latent, q_down_rows) + dense_nt(grad_kv, kv_rows)
    norm1_stat = (
        jnp.sum(grad_latent.astype(F32) * latent_all, -1, keepdims=True)
        + jnp.sum(grad_kv.astype(F32) * kv_pre, -1, keepdims=True)
    ) / recip1
    tokens_own = cols(tokens_in).astype(F32)
    grad_in = (
        cols(grad_branch).astype(F32)
        + recip1 * cols(norm1_gain) * grad_normed
        - tokens_own * recip1**3 * norm1_stat / model_width
    )
    grad_norm1 = jnp.sum(grad_normed * tokens_own * recip1, 0)

    grad_q_down = lax.psum(
        dense_tn(normed_low, own_latent(grad_latent)).astype(BF), "seq"
    ).astype(F32)
    grad_kv_weight = dense_tn(cols(normed_low), grad_kv).astype(BF)
    small = jnp.concatenate([grad_norm1, grad_latent_gain, grad_norm2])
    small = jnp.concatenate(high_low(small)).reshape(2, -1)
    count = small.shape[1]
    kv_cols = grad_kv_weight.shape[1]
    small_rows = jnp.pad(small.reshape(-1), (0, -2 * count % (16 * kv_cols))).reshape(-1, kv_cols)
    last = lax.psum(jnp.concatenate([grad_kv_weight, small_rows], 0), "seq").astype(F32)
    grad_kv_weight = last[:col_count]
    small = jnp.sum(last[col_count:].reshape(-1)[: 2 * count].reshape(2, count), 0)
    grad_norm1 = small[:col_count]
    grad_latent_gain = small[col_count : col_count + rank_cols]
    grad_norm2 = small[col_count + rank_cols :]
    return (
        layer_out,
        grad_in,
        grad_norm1,
        grad_q_down,
        grad_latent_gain,
        grad_q_up,
        grad_kv_weight,
        grad_out,
        grad_norm2,
        grad_gate,
        grad_up,
        grad_down,
    )


def per_device(*args):
    tokens, out_weight = args[0], args[6]
    fits = (
        lax.axis_size("seq") == 8
        and lax.axis_size("rank") == 4
        and tokens.shape[0] % 64 == 0
        and tokens.shape[1] % 2048 == 0
        and args[2].shape[1] % 256 == 0
        and out_weight.shape[0] % 1024 == 0
        and args[8].shape[1] % LANES == 0
        and args[11].shape[0] % 512 == 0
    )
    return (per_device_fast if fits else per_device_general)(*args)


def solution(mesh):
    return jax.shard_map(
        per_device,
        mesh=mesh,
        in_specs=(
            P("seq", None),
            P(),
            P(None, "rank"),
            P("rank"),
            P("rank", None),
            P(),
            P("rank", None),
            P(),
            P(None, "rank"),
            P(None, "rank"),
            P("rank", None),
            P(),
            P("seq", None),
        ),
        out_specs=(
            P("seq", None),
            P("seq", "rank"),
            P("rank"),
            P(None, "rank"),
            P("rank"),
            P("rank", None),
            P("rank", None),
            P("rank", None),
            P(),
            P(None, "rank"),
            P(None, "rank"),
            P("rank", None),
        ),
        check_vma=False,
    )
```

```python
import functools

import jax
import jax.numpy as jnp
from jax import lax
from jax.experimental import pallas as pl
from jax.experimental.pallas import tpu as pltpu
from jax.sharding import PartitionSpec as P

EPS = 1e-05
BASE = 10000.0
NEG = -1e30
LOG2E = 1.4426950408889634
BF = jnp.bfloat16
F32 = jnp.float32
I32 = jnp.int32
LANES = 128

def norm_rows(values, gain):
    recip = lax.rsqrt(jnp.mean(values * values, -1, keepdims=True) + EPS)
    return (values * recip * gain, recip)


def rotate(values, cosine_rows, sine_rows):
    half_dim = values.shape[-1] // 2
    front_half = values[..., :half_dim]
    back_half = values[..., half_dim:]
    return jnp.concatenate(
        [
            front_half * cosine_rows - back_half * sine_rows,
            front_half * sine_rows + back_half * cosine_rows,
        ],
        -1,
    )


def dense(left, right):
    return jnp.dot(left, right, preferred_element_type=F32)


def dense_tn(left, right):
    return lax.dot_general(left, right, (((0,), (0,)), ((), ())), preferred_element_type=F32)


def dense_nt(left, right):
    return lax.dot_general(left, right, (((1,), (1,)), ((), ())), preferred_element_type=F32)


def key_block(key_count, most):
    for size in (1536, 1024, 512, 256, 128):
        if size <= most and key_count % size == 0:
            return size
    return key_count


def row_tile(rows):
    for parts in (3, 2):
        if rows % (parts * 128) == 0:
            return rows // parts
    return rows


def over_key_blocks(info_ref, size, tokens, run):
    first, low, high = info_ref[0], info_ref[1], info_ref[2]
    begin = low // size
    whole_end = jnp.maximum(first // size, begin)
    whole_begin = jnp.clip((high + size - 1) // size, begin, whole_end)
    end = (first + tokens + size - 1) // size
    lax.fori_loop(begin, whole_begin, lambda j, c: run(j, True), None)
    lax.fori_loop(whole_begin, whole_end, lambda j, c: run(j, False), None)
    lax.fori_loop(whole_end, end, lambda j, c: run(j, True), None)


def attend_kernel(
    size, tile, heads, places, info_ref, pre_ref, cos_ref, sin_ref, first_ref, *refs
):
    pieces_in = refs[: len(places)]
    query_ref, out_ref, low_ref, log_ref, kv_ref = refs[len(places) : len(places) + 5]
    max_ref, sum_ref, acc_ref, scores_ref, start_ref, index_ref, sems = refs[len(places) + 5 :]
    tokens = pre_ref.shape[0]
    copies = []
    for n, (mask, offset) in enumerate(places):
        at = lax.bitwise_xor(info_ref[5], mask) * tokens + offset if mask is not None else 0
        rows = pl.ds(pl.multiple_of(at, 16), pieces_in[n].shape[0])
        copies.append(pltpu.make_async_copy(pieces_in[n], kv_ref.at[rows, :], sems.at[n]))
    for copy in copies:
        copy.start()
    width = kv_ref.shape[1] // 2
    half = width // 2
    lanes = max_ref.shape[1]
    scale = width**-0.5 * LOG2E
    cosine, sine = cos_ref[...], sin_ref[...]
    for h in range(heads):
        front = pre_ref[:, h * width : h * width + half]
        back = pre_ref[:, h * width + half : (h + 1) * width]
        rows = slice(h * tokens, (h + 1) * tokens)
        query_ref[rows, :half] = (front * cosine - back * sine).astype(BF)
        query_ref[rows, half:] = (front * sine + back * cosine).astype(BF)
        start_ref[rows, :] = first_ref[...]
        index_ref[rows, :] = info_ref[0] + lax.broadcasted_iota(I32, (tokens, lanes), 0)
    for copy in copies:
        copy.wait()
    pieces = [slice(n * lanes, (n + 1) * lanes) for n in range(size // lanes)]
    for i in range(heads * tokens // tile):
        r = slice(i * tile, (i + 1) * tile)
        max_ref[...] = jnp.full(max_ref.shape, NEG, F32)
        sum_ref[...] = jnp.zeros(sum_ref.shape, F32)
        acc_ref[...] = jnp.zeros(acc_ref.shape, F32)

        def score(j, masked, r=r):
            base = pl.multiple_of(j * size, size)
            scores = dense_nt(query_ref[r, :], kv_ref[pl.ds(base, size), :width])
            most = max_ref[...]
            lane = lax.broadcasted_iota(I32, max_ref.shape, 1)
            for n, piece in enumerate(pieces):
                part = scores[:, piece]
                if masked:
                    at = lane + (base + n * lanes)
                    allowed = (at >= start_ref[r, :]) & (at <= index_ref[r, :])
                    part = jnp.where(allowed, part, NEG)
                scores_ref[j, :, piece] = part
                most = jnp.maximum(most, part)
            max_ref[...] = most
            return None

        over_key_blocks(info_ref, size, tokens, score)
        most = jnp.max(max_ref[...], 1, keepdims=True) * scale
        max_ref[...] = jnp.broadcast_to(most, max_ref.shape)

        def mix(j, carry):
            base = pl.multiple_of(j * size, size)
            most, total = max_ref[...], sum_ref[...]
            probs = []
            for piece in pieces:
                prob = jnp.exp2(scores_ref[j, :, piece] * scale - most)
                total = total + prob
                probs.append(prob.astype(BF))
            sum_ref[...] = total
            acc_ref[...] += dense(jnp.concatenate(probs, 1), kv_ref[pl.ds(base, size), width:])
            return carry

        end = (info_ref[0] + tokens + size - 1) // size
        lax.fori_loop(info_ref[1] // size, end, mix, None)
        total = jnp.sum(sum_ref[...], 1, keepdims=True)
        log_ref[:, r] = jnp.broadcast_to(most + jnp.log2(total), max_ref.shape).T[0:1, :]
        out = acc_ref[...] * (1.0 / total)
        at = i * tile
        while at < (i + 1) * tile:
            h = at // tokens
            stop = min((i + 1) * tile, (h + 1) * tokens)
            rows, cols = slice(at - h * tokens, stop - h * tokens), slice(h * width, (h + 1) * width)
            part = out[at - i * tile : stop - i * tile, :]
            out_ref[rows, cols] = part
            low_ref[rows, cols] = part.astype(BF)
            at = stop


def in_vmem(count):
    return [pl.BlockSpec(memory_space=pltpu.VMEM) for _ in range(count)]


def attend(info, query_pre, cosine, sine, start, pieces):
    tokens, all_heads = query_pre.shape
    width = pieces[0][0].shape[1] // 2
    keys = sum(piece[0].shape[0] for piece in pieces)
    rows = tokens * (all_heads // width)
    size, tile = key_block(keys, 1536), row_tile(rows)
    start = jnp.broadcast_to(start[:, None], (tokens, LANES))
    return pl.pallas_call(
        functools.partial(
            attend_kernel, size, tile, all_heads // width, [piece[1:] for piece in pieces]
        ),
        out_shape=(
            jax.ShapeDtypeStruct((rows, width), BF),
            jax.ShapeDtypeStruct((tokens, all_heads), F32),
            jax.ShapeDtypeStruct((tokens, all_heads), BF),
            jax.ShapeDtypeStruct((1, rows), F32),
            jax.ShapeDtypeStruct((keys, 2 * width), BF),
        ),
        in_specs=[pl.BlockSpec(memory_space=pltpu.SMEM)]
        + in_vmem(4)
        + [pl.BlockSpec(memory_space=pl.ANY)] * len(pieces),
        out_specs=tuple(in_vmem(5)),
        scratch_shapes=[
            pltpu.VMEM((tile, LANES), F32),
            pltpu.VMEM((tile, LANES), F32),
            pltpu.VMEM((tile, width), F32),
            pltpu.VMEM((keys // size, tile, size), F32),
            pltpu.VMEM((rows, LANES), I32),
            pltpu.VMEM((rows, LANES), I32),
            pltpu.SemaphoreType.DMA((len(pieces),)),
        ],
        compiler_params=pltpu.CompilerParams(vmem_limit_bytes=56 * 2**20),
        cost_estimate=brief(0),
        name="attend",
    )(info, query_pre, cosine, sine, start, *[piece[0] for piece in pieces])


def attend_back_kernel(
    size, tile, heads, by_axis, info_ref, query_ref, grad_ref, out_ref, log_ref, cos_ref, sin_ref, kv_ref, start_ref, index_ref,
    gq_ref, near_ref, far_ref, gout_ref, gk_ref, gv_ref, gqt_ref, dots_ref,
):
    tokens = grad_ref.shape[0]
    width = kv_ref.shape[1] // 2
    half = width // 2
    scale = width**-0.5
    for h in range(heads):
        gout = grad_ref[:, h * width : (h + 1) * width]
        gout_ref[h * tokens : (h + 1) * tokens, :] = gout
        dots = gout.astype(F32) * out_ref[:, h * width : (h + 1) * width]
        dots_ref[h * tokens : (h + 1) * tokens, :] = dots[:, :half] + dots[:, half:]
    delta = jnp.sum(dots_ref[...].T, 0, keepdims=True)
    gk_ref[...] = jnp.zeros(gk_ref.shape, F32)
    gv_ref[...] = jnp.zeros(gv_ref.shape, F32)
    gqt_ref[...] = jnp.zeros(gqt_ref.shape, F32)

    def run(j, masked):
        base = pl.multiple_of(j * size, size)
        at_keys = pl.ds(base, size)
        keys = kv_ref[at_keys, :width]
        values = kv_ref[at_keys, width:]
        for i in range(heads * tokens // tile):
            r = slice(i * tile, (i + 1) * tile)
            query, gout = query_ref[r, :], gout_ref[r, :]
            probs = jnp.exp2(dense_nt(keys, query) * (scale * LOG2E) - log_ref[:, r])
            if masked:
                at = base + lax.broadcasted_iota(I32, (size, tile), 0)
                allowed = (at >= start_ref[:, r]) & (at <= index_ref[:, r])
                probs = jnp.where(allowed, probs, 0.0)
            gscores = (probs * (dense_nt(values, gout) - delta[:, r])).astype(BF)
            gv_ref[at_keys, :] += dense(probs.astype(BF), gout)
            gk_ref[at_keys, :] += dense(gscores, query)
            gqt_ref[:, r] += dense_tn(keys, gscores)
        return None

    over_key_blocks(info_ref, size, tokens, run)
    mine = info_ref[3]
    part = tokens // 2
    for s in range(kv_ref.shape[0] // part):
        rows = slice(s * part, (s + 1) * part)
        chip = s // 4
        if by_axis and s % 2 == 0:
            chip = chip % 2 * 2 + chip // 2
        gk = (gk_ref[rows, :] * scale).astype(BF)
        gv = gv_ref[rows, :].astype(BF)

        @pl.when(mine == s // 2 % 2)
        def _(s=s, chip=chip, gk=gk, gv=gv):
            near_ref[s % 2, chip, :, :width] = gk
            near_ref[s % 2, chip, :, width:] = gv

        @pl.when(mine != s // 2 % 2)
        def _(s=s, chip=chip, gk=gk, gv=gv):
            far_ref[s % 2, chip, :, :width] = gk
            far_ref[s % 2, chip, :, width:] = gv

    gq = (gqt_ref[...] * scale).T.astype(BF).astype(F32)
    cosine, sine = cos_ref[...], sin_ref[...]
    for h in range(heads):
        front = gq[h * tokens : (h + 1) * tokens, :half]
        back = gq[h * tokens : (h + 1) * tokens, half:]
        gq_ref[:, h * width : h * width + half] = (front * cosine + back * sine).astype(BF)
        gq_ref[:, h * width + half : (h + 1) * width] = (back * cosine - front * sine).astype(BF)


def attend_back(info, query, grad, out, log, cosine, sine, kv, start, index, by_axis):
    tokens, all_heads = grad.shape
    keys, width = kv.shape[0], kv.shape[1] // 2
    rows = tokens * (all_heads // width)
    blocks = keys // tokens
    return pl.pallas_call(
        functools.partial(
            attend_back_kernel, key_block(keys, 512), row_tile(rows), all_heads // width, by_axis
        ),
        out_shape=(
            jax.ShapeDtypeStruct((tokens, all_heads), BF),
            jax.ShapeDtypeStruct((2, blocks // 2, tokens // 2, 2 * width), BF),
            jax.ShapeDtypeStruct((2, blocks // 2, tokens // 2, 2 * width), BF),
        ),
        in_specs=[pl.BlockSpec(memory_space=pltpu.SMEM)] + in_vmem(9),
        out_specs=tuple(in_vmem(3)),
        scratch_shapes=[
            pltpu.VMEM((rows, width), BF),
            pltpu.VMEM((keys, width), F32),
            pltpu.VMEM((keys, width), F32),
            pltpu.VMEM((width, rows), F32),
            pltpu.VMEM((rows, width // 2), F32),
        ],
        compiler_params=pltpu.CompilerParams(vmem_limit_bytes=56 * 2**20),
        cost_estimate=brief(0),
        name="attend_back",
    )(info, query, grad, out, log, cosine, sine, kv, start, index)


def feed_kernel(tile, mid_ref, grad_ref, gate_ref, up_ref, hidden_ref, both_ref, part_ref):
    width = gate_ref.shape[1]

    def run(i, carry):
        rows = pl.ds(pl.multiple_of(i * tile, tile), tile)
        mid = mid_ref[rows, :]
        gate = dense(mid, gate_ref[...])
        up = dense(mid, up_ref[...])
        grad = grad_ref[rows, :]
        sigmoid = 1.0 / (1.0 + jnp.exp(-gate))
        active = gate * sigmoid
        hidden_ref[rows, :] = (active * up).astype(BF)
        grad_gate = (grad * up * sigmoid * (1.0 + gate * (1.0 - sigmoid))).astype(BF)
        grad_up = (grad * active).astype(BF)
        both_ref[rows, :width] = grad_gate
        both_ref[rows, width:] = grad_up
        part = dense_nt(grad_gate, gate_ref[...]) + dense_nt(grad_up, up_ref[...])
        part_ref[rows, :] = part.astype(BF)
        return carry

    lax.fori_loop(0, mid_ref.shape[0] // tile, run, None)


def feed_forward(mid, grad, gate, up):
    rows, model = mid.shape
    width = gate.shape[1]
    tile = next(t for t in (288, 192, 144, 96, 64, 48, 32, 16, rows) if rows % t == 0)
    return pl.pallas_call(
        functools.partial(feed_kernel, tile),
        out_shape=(
            jax.ShapeDtypeStruct((rows, width), BF),
            jax.ShapeDtypeStruct((rows, 2 * width), BF),
            jax.ShapeDtypeStruct((rows, model), BF),
        ),
        in_specs=in_vmem(4),
        out_specs=tuple(in_vmem(3)),
        compiler_params=pltpu.CompilerParams(vmem_limit_bytes=40 * 2**20),
        cost_estimate=brief(20),
        name="feed_forward",
    )(mid, grad, gate, up)


class Order:
    last = None


def brief(micros):
    return pl.CostEstimate(flops=int(micros * 1e8), bytes_accessed=0, transcendentals=0)


def call(kernel, outs, args, name, micros=0, scratch=(), grid=None, in_specs=None, out_specs=None, prefetch=None):
    out_shape = tuple(jax.ShapeDtypeStruct(*out) for out in outs)
    prefetch = in_order(prefetch)
    params = dict(
        out_shape=out_shape,
        compiler_params=pltpu.CompilerParams(vmem_limit_bytes=56 * 2**20),
        cost_estimate=brief(micros),
        name=name,
    )
    outs = placed_call(kernel, out_shape, args, params, scratch, grid, in_specs, out_specs, prefetch)
    Order.last = outs[0]
    return outs


def in_order(value):
    return value if Order.last is None else after(value, Order.last)


def wait(*values):
    Order.last = (Order.last, values)


def placed_call(kernel, out_shape, args, params, scratch, grid, in_specs, out_specs, prefetch):
    if grid is None:
        return pl.pallas_call(
            kernel,
            in_specs=[pl.BlockSpec(memory_space=pltpu.SMEM)] + in_vmem(len(args)),
            out_specs=tuple(in_vmem(len(out_shape))),
            scratch_shapes=list(scratch),
            **params,
        )(prefetch, *args)
    return pl.pallas_call(
        kernel,
        grid_spec=pltpu.PrefetchScalarGridSpec(
            num_scalar_prefetch=1,
            grid=grid,
            in_specs=in_specs,
            out_specs=tuple(out_specs),
            scratch_shapes=list(scratch),
        ),
        **params,
    )(prefetch, *args)


def once(shape, index):
    return pl.BlockSpec(shape, index, pipeline_mode=pl.Buffered(1))


def at_block(index, size):
    return pl.ds(pl.multiple_of(index * size, size), size)


CORE, RANK, SEQ = 3, 4, 5


def ahead(info_ref, shift, ranks):
    return lax.rem(info_ref[RANK] + shift, ranks)


def behind(info_ref, shift, ranks):
    return lax.rem(info_ref[RANK] + ranks - shift, ranks)


def chip_of(info_ref):
    return lax.div(info_ref[SEQ], 2)


def rank_blocks(info, index):
    return lambda i, info_ref: index(info_ref[RANK])


def project_kernel(
    info_ref, tokens_ref, gain_ref, down_ref, kv_weight_ref, latent_gain_ref, normed_ref, recip_ref, kv_ref, low_ref
):
    values = tokens_ref[...].astype(F32)
    normed, recip = norm_rows(values, gain_ref[...])
    normed_ref[...] = normed.astype(BF)
    recip_ref[...] = jnp.broadcast_to(recip, recip_ref.shape)
    rows = normed_ref.shape[0]
    low_ref[at_block(pl.program_id(0), rows), :] = dense(normed_ref[...], down_ref[...]).astype(BF)

    @pl.when(pl.program_id(0) == 0)
    def _():
        rest = latent_gain_ref[...]
        parts = []
        for _ in range(3):
            parts.append(rest.astype(BF))
            rest = rest - parts[-1].astype(F32)
        parts.append(jnp.zeros((EXTRA - 3, rest.shape[1]), BF))
        low_ref[low_ref.shape[0] - EXTRA :, :] = jnp.concatenate(parts, 0)

    kv_ref[...] = dense(normed_ref[...], kv_weight_ref[...])


EXTRA = 16


def project(info, tokens, gain, q_down, kv_weight, latent_gain):
    rows, model = tokens.shape
    tile = rows // 2
    widths = ((model, BF), (LANES, F32), (kv_weight.shape[1], F32))
    low = (rows + EXTRA, q_down.shape[1])
    return call(
        project_kernel,
        [((rows, width), dtype) for width, dtype in widths] + [(low, BF)],
        (tokens, gain.reshape(1, -1), q_down, kv_weight, latent_gain.reshape(1, -1)),
        "project",
        grid=(2,),
        in_specs=[
            pl.BlockSpec((tile, model), lambda i, w: (i, 0)),
            once((1, model), lambda i, w: (0, 0)),
            once(q_down.shape, lambda i, w: (0, 0)),
            once(kv_weight.shape, lambda i, w: (0, 0)),
            once((1, q_down.shape[1]), lambda i, w: (0, 0)),
        ],
        out_specs=[pl.BlockSpec((tile, width), lambda i, w: (i, 0)) for width, _ in widths]
        + [pl.BlockSpec(low, lambda i, w: (0, 0))],
        prefetch=info,
    )


def turn_kernel(info_ref, kv_ref, cos_ref, sin_ref, out_ref):
    half = cos_ref.shape[1]
    front, back = kv_ref[:, :half], kv_ref[:, half : 2 * half]
    cosine, sine = cos_ref[...], sin_ref[...]
    out_ref[:, :half] = (front * cosine - back * sine).astype(BF)
    out_ref[:, half : 2 * half] = (front * sine + back * cosine).astype(BF)
    out_ref[:, 2 * half :] = kv_ref[:, 2 * half :].astype(BF)


def turn(info, kv_pre, cosine, sine):
    return call(turn_kernel, [(kv_pre.shape, BF)], (kv_pre, cosine, sine), "turn", prefetch=info)[0]


def query_kernel(info_ref, latent_ref, own_ref, other_ref, low_ref, recip_ref, gain_ref, query_ref):
    rows = low_ref.shape[0]
    parts = latent_ref[rows:, :].astype(F32)
    gain_ref[...] = parts[0:1] + parts[1:2] + parts[2:3]
    normed, recip = norm_rows(latent_ref[:rows, :].astype(F32), gain_ref[...])
    low_ref[...] = normed.astype(BF)
    recip_ref[...] = jnp.broadcast_to(recip, recip_ref.shape)
    half = own_ref.shape[1]
    ranks = 4
    cols = latent_ref.shape[1] // ranks
    totals = [0.0, 0.0]
    for s in range(ranks):
        left = low_ref[:, at_block(behind(info_ref, s, ranks), cols)]
        for n, ref in enumerate((own_ref, other_ref)):
            totals[n] = totals[n] + dense(left, ref[s * cols : (s + 1) * cols, :])
    core = info_ref[CORE]
    query_ref[:, at_block(core, half)] = totals[0]
    query_ref[:, at_block(1 - core, half)] = totals[1]


def queries(info, latent, own, other):
    rows, width = latent.shape[0] - EXTRA, latent.shape[1]
    return call(
        query_kernel,
        [((rows, width), BF), ((rows, LANES), F32), ((1, width), F32), ((rows, 2 * own.shape[1]), F32)],
        (latent, own, other),
        "queries",
        prefetch=info,
    )


def latent_part_kernel(info_ref, grad_ref, own_ref, other_ref, *refs):
    outs, all_ref = refs[:-1], refs[-1]
    ranks, rows = len(outs), outs[0].shape[0]
    half, cols = own_ref.shape[1], own_ref.shape[0] // ranks
    core = info_ref[CORE]
    own_grad = grad_ref[:, at_block(core, half)]
    other_grad = grad_ref[:, at_block(1 - core, half)]
    for s in range(ranks):
        part = slice(s * cols, (s + 1) * cols)
        out = dense_nt(own_grad, own_ref[part, :]) + dense_nt(other_grad, other_ref[part, :])
        all_ref[:, at_block(behind(info_ref, s, ranks), cols)] = out.astype(BF)
    for s in range(ranks):
        outs[s][...] = all_ref[at_block(ahead(info_ref, s, ranks), rows), :]


def latent_parts(info, grad, own, other, ranks):
    rows, width = grad.shape[0], own.shape[0]
    return call(
        latent_part_kernel,
        [((rows // ranks, width), BF)] * ranks,
        (grad, own, other),
        "latent_parts",
        scratch=[pltpu.VMEM((rows, width), BF)],
        prefetch=info,
    )


def latent_back_kernel(info_ref, latent_ref, recip_ref, gain_ref, norm2_ref, *refs):
    parts, grad_ref = refs[:-1], refs[-1]
    grad_in = sum(part[...].astype(F32) for part in parts)
    latent = latent_ref[...].astype(F32)
    recip = recip_ref[:, 0:1]
    gained = grad_in * gain_ref[...]
    stat = jnp.sum(latent * gained, -1, keepdims=True)
    grad = recip * gained - latent * (recip * recip * recip * stat / latent.shape[1])
    rows, width = grad.shape
    grad_ref[:rows, :] = grad.astype(BF)
    sums = [norm2_ref[:, i * width : (i + 1) * width] for i in range(norm2_ref.shape[1] // width)]
    sums = jnp.concatenate(sums + [jnp.sum(grad_in * latent * recip, 0, keepdims=True)], 0)
    high = sums.astype(BF)
    low = (sums - high.astype(F32)).astype(BF)
    fill = jnp.zeros((EXTRA - 2 * sums.shape[0], width), BF)
    grad_ref[rows:, :] = jnp.concatenate([high, low, fill], 0)


def latent_back(info, latent, recip, gain, norm2, parts):
    rows, width = parts[0].shape
    return call(
        latent_back_kernel,
        [((rows + EXTRA, width), BF)],
        (latent, recip, gain, norm2, *parts),
        "latent_back",
        grid=(1,),
        in_specs=[
            pl.BlockSpec((rows, width), lambda i, w: (w[RANK], 0)),
            pl.BlockSpec((rows, LANES), lambda i, w: (w[RANK], 0)),
            pl.BlockSpec((1, width), lambda i, w: (0, 0)),
            pl.BlockSpec(norm2.shape, lambda i, w: (0, 0)),
        ]
        + [pl.BlockSpec((rows, width), lambda i, w: (0, 0)) for _ in parts],
        out_specs=[pl.BlockSpec((rows + EXTRA, width), lambda i, w: (0, 0))],
        prefetch=info,
    )[0]


def kv_back_kernel(info_ref, cos_ref, sin_ref, *refs):
    parts, out_ref = refs[:-1], refs[-1]
    total = sum(part[...].astype(F32) for part in parts).astype(BF).astype(F32)
    half = cos_ref.shape[1]
    front, back = total[:, :half], total[:, half : 2 * half]
    cosine, sine = cos_ref[...], sin_ref[...]
    out_ref[:, :half] = (front * cosine + back * sine).astype(BF)
    out_ref[:, half : 2 * half] = (back * cosine - front * sine).astype(BF)
    out_ref[:, 2 * half :] = total[:, 2 * half :].astype(BF)


def kv_back(info, cosine, sine, parts):
    rows, width = parts[0].shape
    return call(
        kv_back_kernel,
        [((rows, width), BF)],
        (cosine, sine, *parts),
        "kv_back",
        grid=(1,),
        in_specs=[pl.BlockSpec((rows, cosine.shape[1]), lambda i, w: (w[RANK], 0))] * 2
        + [pl.BlockSpec((rows, width), lambda i, w: (0, 0)) for _ in parts],
        out_specs=[pl.BlockSpec((rows, width), lambda i, w: (0, 0))],
        prefetch=info,
    )[0]


def mid_kernel(info_ref, branch_ref, tokens_ref, gain_ref, residual_ref, mid_ref, recip_ref):
    residual = tokens_ref[...].astype(F32) + branch_ref[...].astype(F32)
    normed, recip = norm_rows(residual, gain_ref[...])
    residual_ref[...] = residual
    mid_ref[...] = normed.astype(BF)
    recip_ref[...] = jnp.broadcast_to(recip, recip_ref.shape)


def mid_norm(info, branch, tokens, gain):
    rows, model = branch.shape
    whole = pl.BlockSpec((rows, model), lambda i, w: (0, 0))
    return call(
        mid_kernel,
        [((rows, model), F32), ((rows, model), BF), ((rows, LANES), F32)],
        (branch, tokens, gain.reshape(1, -1)),
        "mid_norm",
        grid=(1,),
        in_specs=[
            whole,
            pl.BlockSpec((rows, model), lambda i, w: (w[RANK], 0)),
            pl.BlockSpec((1, model), lambda i, w: (0, 0)),
        ],
        out_specs=[whole, whole, pl.BlockSpec((rows, LANES), lambda i, w: (0, 0))],
        prefetch=info,
    )


def mid_back_kernel(info_ref, grad_ref, residual_ref, recip_ref, gain_ref, out_grad_ref, branch_ref, gain_grad_ref):
    grad = grad_ref[...].astype(F32)
    residual = residual_ref[...]
    recip = recip_ref[:, 0:1]
    gained = grad * gain_ref[...]
    stat = jnp.sum(residual * gained, -1, keepdims=True)
    out = out_grad_ref[...].astype(F32) + recip * gained
    out = out - residual * (recip * recip * recip * stat / residual.shape[1])
    branch_ref[...] = out.astype(BF)
    gain_grad_ref[...] = jnp.sum(grad * residual * recip, 0, keepdims=True)


def mid_back(info, grad, residual, recip, gain, out_grad):
    rows, model = grad.shape
    whole = pl.BlockSpec((rows, model), lambda i, w: (0, 0))
    return call(
        mid_back_kernel,
        [((rows, model), BF), ((1, model), F32)],
        (grad, residual, recip, gain.reshape(1, -1), out_grad),
        "mid_back",
        grid=(1,),
        in_specs=[
            whole,
            whole,
            pl.BlockSpec((rows, LANES), lambda i, w: (0, 0)),
            pl.BlockSpec((1, model), lambda i, w: (0, 0)),
            pl.BlockSpec((rows, model), lambda i, w: (w[RANK], 0)),
        ],
        out_specs=[whole, pl.BlockSpec((1, model), lambda i, w: (0, 0))],
        prefetch=info,
    )


def matmul_kernel(dims, info_ref, left_ref, right_ref, *refs):
    out = lax.dot_general(left_ref[...], right_ref[...], (dims, ((), ())), preferred_element_type=F32)
    if len(refs) == 1:
        refs[0][...] = out.astype(BF)
        return
    outs, all_ref = refs[:-1], refs[-1]
    all_ref[...] = out.astype(BF)
    for s, out_ref in enumerate(outs):
        out_ref[...] = all_ref[at_block(ahead(info_ref, s, len(outs)), out_ref.shape[0]), :]


def matmul(info, left, right, transposed=False, parts=1):
    rows, depth = left.shape
    cols = right.shape[0 if transposed else 1]
    tile = next(t for t in ((512, 256, LANES) if transposed else (1024, 512, 256, LANES)) if cols % t == 0)
    if transposed:
        dims, spec = ((1,), (1,)), pl.BlockSpec((tile, depth), lambda i, w: (i, 0))
    else:
        dims, spec = ((1,), (0,)), pl.BlockSpec((depth, tile), lambda i, w: (0, i))
    outs = call(
        functools.partial(matmul_kernel, dims),
        [((rows // parts, cols), BF)] * parts,
        (left, right),
        "matmul",
        scratch=[pltpu.VMEM((rows, tile), BF)] if parts > 1 else [],
        grid=(cols // tile,),
        in_specs=[once((rows, depth), lambda i, w: (0, 0)), spec],
        out_specs=[pl.BlockSpec((rows // parts, tile), lambda i, w: (0, i))] * parts,
        prefetch=info,
    )
    return outs if parts > 1 else outs[0]


def quarter_order(info_ref):
    bit_x = lax.rem(chip_of(info_ref), 2)
    bit_y = lax.div(chip_of(info_ref), 2)
    return 1 - bit_x, 3 - bit_y, bit_x, 2 + bit_y


def product_kernel(counts, info_ref, *refs):
    outs, all_ref = refs[4 * len(counts) : 4 * len(counts) + 4], refs[-1]
    order = quarter_order(info_ref)
    rows = outs[0].shape[0]
    first = 0
    for n, count in enumerate(counts):
        own, other, own_right, other_right = refs[4 * n : 4 * n + 4]
        step = pl.program_id(0)

        def mixed(cols):
            out = dense_tn(own[:, cols], own_right[...])
            return (out + dense_tn(other[:, cols], other_right[...])).astype(BF)

        @pl.when((step >= first) & (step < first + count))
        def _():
            if rows >= 256:
                for out_ref, at in zip(outs, order):
                    out_ref[...] = mixed(at_block(at, rows))
            else:
                all_ref[...] = mixed(slice(None))
                for out_ref, at in zip(outs, order):
                    out_ref[...] = all_ref[at_block(at, rows), :]

        first += count


def pair_products(info, terms, tile):
    tokens, rows = terms[0][0].shape[0], terms[0][0].shape[1] // 2
    counts = [term[2].shape[1] // tile for term in terms]
    specs, args, first = [], [], 0
    for term, count in zip(terms, counts):
        specs += [once((tokens, rows), lambda i, w: (0, w[CORE]))] * 2
        place = lambda i, w, first=first, count=count: (0, jnp.clip(i - first, 0, count - 1))
        specs += [pl.BlockSpec((tokens, tile), place)] * 2
        args += term
        first += count
    return call(
        functools.partial(product_kernel, counts),
        [((rows // 4, first * tile), BF)] * 4,
        args,
        "pair_products",
        scratch=[pltpu.VMEM((rows, tile) if rows < 1024 else (16, LANES), BF)],
        grid=(first,),
        in_specs=specs,
        out_specs=[pl.BlockSpec((rows // 4, tile), lambda i, w: (0, i))] * 4,
        prefetch=info,
    )


def add_low(left, right):
    return (left.astype(F32) + right.astype(F32)).astype(BF)


def fold_near_kernel(info_ref, near_ref, got_ref, *outs):
    for out_ref, at in zip(outs, quarter_order(info_ref)):
        p, bit = lax.div(at, 2), lax.rem(at, 2)
        for other in range(2):
            chip = bit * 2 + other
            out_ref[other] = add_low(near_ref[p, chip], got_ref[p, chip])


def fold_near(info, near, got):
    _, chips, rows, cols = near.shape
    tile = rows // 3
    return call(
        fold_near_kernel,
        [((2, rows, cols), BF)] * 4,
        (near, got),
        "fold_near",
        grid=(3,),
        in_specs=[pl.BlockSpec((2, chips, tile, cols), lambda i, w: (0, 0, i, 0))] * 2,
        out_specs=[pl.BlockSpec((2, tile, cols), lambda i, w: (0, i, 0))] * 4,
        prefetch=info,
    )


def fold_first_kernel(info_ref, keep_first, got_first, keep_last, got_last, *outs):
    bit_x = lax.rem(chip_of(info_ref), 2)
    bit_y = lax.div(chip_of(info_ref), 2)
    outs[0][...] = add_low(keep_first[1 - bit_y], got_first[1 - bit_y])
    outs[1][...] = add_low(keep_last[1 - bit_x], got_last[1 - bit_x])
    outs[2][...] = add_low(keep_first[bit_y], got_first[bit_y])
    outs[3][...] = add_low(keep_last[bit_x], got_last[bit_x])


def fold_first(info, arrays, steps, micros=0):
    rows, cols = arrays[0].shape[1:]
    tile = rows // steps
    return call(
        fold_first_kernel,
        [((rows, cols), BF)] * 4,
        arrays,
        "fold_first",
        micros,
        grid=(steps,),
        in_specs=[pl.BlockSpec((2, tile, cols), lambda i, w: (0, i, 0))] * 4,
        out_specs=[pl.BlockSpec((tile, cols), lambda i, w: (i, 0))] * 4,
        prefetch=info,
    )


def fold_last_kernel(info_ref, keep_first, got_first, keep_last, got_last, out_ref):
    out_ref[0] = add_low(keep_first[...], got_first[...])
    out_ref[1] = add_low(keep_last[...], got_last[...])


def fold_last(info, arrays, steps):
    rows, cols = arrays[0].shape
    tile = rows // steps
    return call(
        fold_last_kernel,
        [((2, rows, cols), BF)],
        arrays,
        "fold_last",
        grid=(steps,),
        in_specs=[pl.BlockSpec((tile, cols), lambda i, w: (i, 0))] * 4,
        out_specs=[pl.BlockSpec((2, tile, cols), lambda i, w: (0, i, 0))],
        prefetch=info,
    )[0]


def fold_kv_kernel(info_ref, keep_first, got_first, keep_last, got_last, *refs):
    outs, all_ref = refs[:-1], refs[-1]
    half = keep_first.shape[0]
    all_ref[:half, :] = add_low(keep_first[...], got_first[...])
    all_ref[half:, :] = add_low(keep_last[...], got_last[...])
    for s, out_ref in enumerate(outs):
        out_ref[...] = all_ref[at_block(ahead(info_ref, s, len(outs)), out_ref.shape[0]), :]


def fold_kv(info, arrays, ranks):
    rows, cols = arrays[0].shape
    return call(
        fold_kv_kernel,
        [((2 * rows // ranks, cols), BF)] * ranks,
        arrays,
        "fold_kv",
        scratch=[pltpu.VMEM((2 * rows, cols), BF)],
        prefetch=info,
    )


def fold_up_kernel(info_ref, keep_first, got_first, keep_last, got_last, *refs):
    ups, all_ref = refs[:-1], refs[-1]
    all_ref[0] = add_low(keep_first[...], got_first[...])
    all_ref[1] = add_low(keep_last[...], got_last[...])
    for s, up_ref in enumerate(ups):
        up_ref[...] = all_ref[:, at_block(ahead(info_ref, s, len(ups)), up_ref.shape[1]), :]


def fold_up(info, arrays, ranks):
    rows, cols = arrays[0].shape
    return call(
        fold_up_kernel,
        [((2, rows // ranks, cols), BF)] * ranks,
        arrays,
        "fold_up",
        scratch=[pltpu.VMEM((2, rows, cols), BF)],
        prefetch=info,
    )


def pack_up_kernel(info_ref, *refs):
    ups, all_ref = refs[:-1], refs[-1]
    for s, up_ref in enumerate(ups):
        all_ref[:, at_block(behind(info_ref, s, len(ups)), up_ref.shape[1]), :] = up_ref[...]


def pack_up(info, ups):
    _, rows, cols = ups[0].shape
    return call(pack_up_kernel, [((2, rows * len(ups), cols), BF)], ups, "pack_up", prefetch=info)[0]


def layer_kernel(info_ref, residual_ref, feed_ref, left_ref, right_ref):
    half = left_ref.shape[1]
    out = (residual_ref[...] + feed_ref[...].astype(F32)).astype(BF)
    left_ref[...] = out[:, :half]
    right_ref[...] = out[:, half:]


def layer_halves(info, residual, feed):
    rows, model = residual.shape
    return call(
        layer_kernel, [((rows, model // 2), BF)] * 2, (residual, feed), "layer", prefetch=info
    )


def place_kernel(info_ref, *refs):
    out_ref = refs[-1]
    half = out_ref.shape[1] // 2
    for s in range(len(refs) // 2):

        @pl.when(pl.program_id(0) == s)
        def _(s=s):
            out_ref[:, :half] = refs[2 * s][...]
            out_ref[:, half:] = refs[2 * s + 1][...]


def place(info, lefts, rights):
    rows, cols = lefts[0].shape
    ranks = len(lefts)
    parts = [part for pair in zip(lefts, rights) for part in pair]
    return call(
        place_kernel,
        [((ranks * rows, 2 * cols), BF)],
        parts,
        "place",
        grid=(ranks,),
        in_specs=[once((rows, cols), lambda i, w: (0, 0))] * len(parts),
        out_specs=[pl.BlockSpec((rows, 2 * cols), lambda i, w: (behind(w, i, ranks), 0))],
        prefetch=info,
    )[0]


def input_back_kernel(
    ranks, info_ref, tokens_ref, branch_ref, gain_ref, kv_weight_ref, recip_ref, latent_ref, kv_pre_ref, *refs
):
    latents, kvs, downs = refs[:ranks], refs[ranks : 2 * ranks], refs[2 * ranks : 3 * ranks]
    grad_in_ref, small_ref, own_ref, kv_ref, all_ref, sums_ref = refs[3 * ranks :]
    rows = kvs[0].shape[0]
    cols = own_ref.shape[1]
    sums = 0.0
    for s in range(ranks):
        at = at_block(behind(info_ref, s, ranks), rows)
        all_ref[at, :] = latents[s][:rows, :]
        sums = sums + latents[s][rows:, :].astype(F32)
        kv_ref[at, :] = kvs[s][...]
    grad = dense_nt(kv_ref[...], kv_weight_ref[...])
    for s in range(ranks):
        at = at_block(behind(info_ref, s, ranks), cols)
        grad = grad + dense_nt(all_ref[:, at], downs[s][...])
    own_ref[...] = all_ref[:, at_block(info_ref[RANK], cols)]
    recip = recip_ref[:, 0:1]
    latent = latent_ref[: all_ref.shape[0], :].astype(F32)
    stat = jnp.sum(all_ref[...].astype(F32) * latent, -1, keepdims=True)
    stat = stat + jnp.sum(kv_ref[...].astype(F32) * kv_pre_ref[...], -1, keepdims=True)
    tokens = tokens_ref[...].astype(F32)
    model = tokens.shape[1] * ranks
    out = branch_ref[...].astype(F32) + recip * gain_ref[...] * grad
    grad_in_ref[...] = out - tokens * (recip * recip * stat / model)
    count = sums.shape[0] // 16 * 3
    sums = sums[:count] + sums[count : 2 * count]
    sums_ref[...] = sums[count - 1 :]
    norm1 = jnp.sum(grad * tokens * recip, 0, keepdims=True)
    lines = [sums[r : r + 1, i * cols : (i + 1) * cols] for r in range(count - 1) for i in range(sums.shape[1] // cols)]
    lines += [norm1[:, i * cols : (i + 1) * cols] for i in range(norm1.shape[1] // cols)]
    lines.append(sums_ref[:, at_block(info_ref[RANK], cols)])
    lines += [jnp.zeros_like(lines[0])] * (small_ref.shape[0] - len(lines))
    small_ref[...] = jnp.concatenate(lines, 0).astype(BF)


def input_back(info, tokens, branch, gain, kv_weight, recip, latent, kv_pre, latents, kvs, downs):
    ranks = len(latents)
    rows, model = tokens.shape
    cols = model // ranks
    width, down = kv_weight.shape[1], downs[0].shape[1]
    whole = lambda array: pl.BlockSpec(array.shape, lambda i, w: (0, 0))
    wide = pl.BlockSpec((rows, cols), lambda i, w: (0, w[RANK]))
    outs = [((rows, cols), F32), ((16, down), BF), ((rows, down), BF), ((rows, width), BF)]
    return call(
        functools.partial(input_back_kernel, ranks),
        outs,
        (tokens, branch, gain.reshape(1, -1), kv_weight, recip, latent, kv_pre, *latents, *kvs, *downs),
        "input_back",
        scratch=[pltpu.VMEM((rows, latent.shape[1]), BF), pltpu.VMEM((1, latent.shape[1]), F32)],
        grid=(1,),
        in_specs=[
            wide,
            wide,
            pl.BlockSpec((1, cols), lambda i, w: (0, w[RANK])),
            pl.BlockSpec((cols, width), lambda i, w: (w[RANK], 0)),
        ]
        + [whole(array) for array in (recip, latent, kv_pre, *latents, *kvs, *downs)],
        out_specs=[pl.BlockSpec(shape, lambda i, w: (0, 0)) for shape, _ in outs],
        prefetch=info,
    )


def last_products_kernel(info_ref, normed_ref, latent_ref, kv_ref, small_ref, out_ref):
    rows, width = normed_ref.shape[1], latent_ref.shape[1]
    out_ref[:rows, :] = dense_tn(normed_ref[...], latent_ref[...]).astype(BF)
    count = (out_ref.shape[0] - rows - small_ref.shape[0]) // 2
    wide = dense_tn(normed_ref[:, at_block(info_ref[RANK], count)], kv_ref[...]).astype(BF)
    out_ref[rows : rows + count, :] = wide[:, :width]
    out_ref[rows + count : rows + 2 * count, :] = wide[:, width:]
    out_ref[rows + 2 * count :, :] = small_ref[...]


def last_products(info, normed, latent, kv, small, ranks):
    model, width = normed.shape[1], latent.shape[1]
    shape = (model + 2 * model // ranks + small.shape[0], width)
    return call(
        last_products_kernel, [(shape, BF)], (normed, latent, kv, small), "last_products", prefetch=info
    )[0]


def last_kernel(info_ref, in_ref, down_ref, kv_ref, small_ref):
    rows, width = down_ref.shape
    count = kv_ref.shape[0]
    down_ref[...] = in_ref[:rows, :].astype(F32)
    kv_ref[:, :width] = in_ref[rows : rows + count, :].astype(F32)
    kv_ref[:, width:] = in_ref[rows + count : rows + 2 * count, :].astype(F32)
    small_ref[...] = in_ref[rows + 2 * count :, :].astype(F32)


def store_feed(part, at, gate_ref, up_ref, down_ref):
    rows, width = part.shape[0], gate_ref.shape[1]
    block = slice(at * rows, (at + 1) * rows)
    gate_ref[block, :] = part[:, :width].astype(F32)
    up_ref[block, :] = part[:, width : 2 * width].astype(F32)
    down_ref[:, block] = part[:, 2 * width :].astype(F32).T


def store_same(part, at, out_ref):
    rows = part.shape[0]
    out_ref[at * rows : (at + 1) * rows, :] = part.astype(F32)


def unpack_up_kernel(info_ref, *refs):
    out_ref = refs[-1]
    for mask, ref in enumerate(refs[:-1]):
        source = lax.bitwise_xor(info_ref[SEQ], mask)
        core, chip = lax.rem(source, 2), lax.div(source, 2)
        _, rows, cols = ref.shape
        rows = rows // (out_ref.shape[1] // cols)
        for p in range(2):
            place = lax.rem(chip, 2) * 2 + lax.div(chip, 2) if p == 0 else chip
            at = at_block(core * 8 + p * 4 + place, rows)
            for r in range(out_ref.shape[1] // cols):
                block = ref[p, r * rows : (r + 1) * rows, :].astype(F32)
                out_ref[at, r * cols : (r + 1) * cols] = block


def unpack_up(info, pieces, shape):
    return call(unpack_up_kernel, [(shape, F32)], pieces, "unpack_up", prefetch=info)[0]


def unpack_kernel(store, info_ref, in_ref, *out_refs):
    part = lax.rem(pl.program_id(0), 2)
    for chip in range(4):
        turned = chip % 2 * 2 + chip // 2
        pl.when(part == 0)(lambda chip=chip, at=turned: store(in_ref[chip], at, *out_refs))
        pl.when(part == 1)(lambda chip=chip: store(in_ref[chip], chip, *out_refs))


def unpack(info, whole, store, shapes, along):
    _, _, rows, cols = whole.shape
    whole = whole.reshape(4, 2, 2, rows, cols)
    out_specs = []
    for (height, width), dim in zip(shapes, along):
        if dim == 0:
            out_specs.append(pl.BlockSpec((height // 4, width), lambda i, w: (i, 0)))
        else:
            out_specs.append(pl.BlockSpec((height, width // 4), lambda i, w: (0, i)))
    return call(
        functools.partial(unpack_kernel, store),
        [(shape, F32) for shape in shapes],
        (whole,),
        "unpack",
        grid=(4,),
        in_specs=[
            pl.BlockSpec((4, None, None, rows, cols), lambda i, w: (0, i // 2, i % 2, 0, 0))
        ],
        out_specs=out_specs,
        prefetch=info,
    )


def bit_of(index, bit):
    return (index >> bit) & 1


def exchange(value, mask):
    count = lax.axis_size("seq")
    return lax.ppermute(value, "seq", [(i, i ^ mask) for i in range(count)])


def swap(value, bit):
    return exchange(value, 1 << bit)


def ring(value, shift):
    if not shift:
        return value
    ranks = lax.axis_size("rank")
    return lax.ppermute(value, "rank", [(i, (i + shift) % ranks) for i in range(ranks)])


def rings(values):
    return [ring(value, s) for s, value in enumerate(values)]


def both(first, last):
    return swap(first, 1), swap(last, 2)


def sum_over(value, axis):
    count = lax.axis_size(axis)
    mask = 1
    while mask < count:
        value = value + lax.ppermute(value, axis, [(i, i ^ mask) for i in range(count)])
        mask *= 2
    return value


def after(value, *others):
    return lax.optimization_barrier((value, others))[0]


def per_device_fast(
    tokens_in,
    norm1_gain,
    q_down,
    latent_gain,
    q_up,
    kv_weight,
    out_weight,
    norm2_gain,
    gate_weight,
    up_weight,
    down_weight,
    doc_ids,
    out_grad,
):
    Order.last = None
    row_count, model_width = tokens_in.shape
    ranks = lax.axis_size("rank")
    rank_ix = lax.axis_index("rank")
    seq_ix = lax.axis_index("seq")
    head_dim = kv_weight.shape[1] // 2
    local_heads = out_weight.shape[0] // head_dim
    first_row = seq_ix * row_count
    core = bit_of(seq_ix, 0)
    rank_cols = q_down.shape[1]
    rank_width = rank_cols * ranks
    col_count = model_width // ranks

    up_cols = q_up.shape[1] // ranks
    half_cols = up_cols // 2
    blocks = [
        lax.dynamic_slice_in_dim(
            q_up, lax.rem(rank_ix + s, ranks) * up_cols + core * half_cols, half_cols, 1
        )
        for s in range(ranks)
    ]
    tokens_late = after(tokens_in, blocks)
    up_own = jnp.concatenate(rings(blocks), 0)
    up_other = swap(up_own, 0)

    ids_local = lax.dynamic_slice_in_dim(doc_ids, first_row, row_count, 0)
    start = jnp.sum((doc_ids[None, :] < ids_local[:, None]).astype(I32), 1)
    query_index = first_row + jnp.arange(row_count, dtype=I32)
    position = (query_index - start).astype(F32)
    half_dim = head_dim // 2
    freqs = BASE ** (-jnp.arange(half_dim, dtype=F32) / half_dim)
    angle = position[:, None] * freqs[None, :]
    cosine, sine = jnp.cos(angle), jnp.sin(angle)
    start_rows = jnp.tile(start, local_heads)[None]
    index_rows = jnp.tile(query_index, local_heads)[None]
    place_info = jnp.stack([first_row, first_row, first_row, core, rank_ix, seq_ix]).astype(I32)
    info = jnp.stack([first_row, start[0], start[-1], core, rank_ix, seq_ix]).astype(I32)

    normed_low, recip1, kv_pre, latent = project(
        place_info, tokens_late, norm1_gain, q_down, kv_weight, latent_gain
    )
    latent_all = lax.all_gather(latent, "rank", axis=1, tiled=True)

    kv_local = turn(place_info, kv_pre, cosine, sine)
    half_rows = row_count // 2
    by_x, by_y = lax.optimization_barrier(both(kv_local, kv_local))
    top, bottom = swap(by_x[:half_rows], 2), swap(by_y[half_rows:], 1)
    pieces = [(kv_local, 0, 0), (by_x, 2, 0), (by_y, 4, 0), (top, 6, 0), (bottom, 6, half_rows)]
    pieces += [(swap(array, 0), mask ^ 1, offset) for array, mask, offset in pieces]

    latent_low, recip_c, gain_all, query_pre = queries(place_info, latent_all, up_own, up_other)
    query, attn_vals, attn_low, log_total, kv_all = attend(
        in_order(info), query_pre, cosine, sine, start, pieces
    )
    Order.last = attn_low

    branch_part = matmul(info, attn_low, out_weight)
    branch = lax.psum_scatter(branch_part, "rank", scatter_dimension=0, tiled=True)
    grad_hidden = dense_nt(after(out_grad, branch_part), down_weight)
    out_grad_pair = swap(after(out_grad, branch_part), 0)
    attn_pair = swap(attn_low, 0)
    piece_cols = rank_cols // 16
    latent_cut = jnp.transpose(
        after(latent_low, branch_part).reshape(row_count, ranks, 16, piece_cols), (0, 2, 1, 3)
    ).reshape(row_count, rank_width)
    latent_pair = swap(latent_cut, 0)
    down_blocks = [
        lax.dynamic_slice_in_dim(
            after(q_down, branch_part), lax.rem(rank_ix + s, ranks) * col_count, col_count, 0
        )
        for s in range(ranks)
    ]
    branch = after(
        branch, grad_hidden, out_grad_pair, attn_pair, latent_pair, latent_cut, down_blocks
    )
    residual, mid_own, recip2 = mid_norm(info, branch, tokens_in, norm2_gain)
    mid_low = lax.all_gather(mid_own, "rank", axis=0, tiled=True)

    downs = rings(after(down_blocks, mid_low))
    mid_pair = swap(mid_low, 0)
    hidden_low, grad_both, grad_mid_part = feed_forward(
        mid_low, grad_hidden, gate_weight, up_weight
    )
    Order.last = hidden_low
    hidden_low, grad_both, grad_mid_part = after((hidden_low, grad_both, grad_mid_part), downs)
    grad_mid = lax.psum_scatter(grad_mid_part, "rank", scatter_dimension=0, tiled=True)
    both_pair, hidden_pair = swap(grad_both, 0), swap(hidden_low, 0)
    feed_part = matmul(info, hidden_low, down_weight)
    feed_width = gate_weight.shape[1]
    send_first, send_last, keep_first, keep_last = pair_products(
        info,
        [
            (mid_low, mid_pair, grad_both, both_pair),
            (out_grad, out_grad_pair, hidden_low, hidden_pair),
        ],
        feed_width,
    )
    grad_mid = after(grad_mid, send_first)
    branch_own, norm2_part = mid_back(info, grad_mid, residual, recip2, norm2_gain, out_grad)
    grad_branch = lax.all_gather(branch_own, "rank", axis=0, tiled=True)

    two = lambda array: array.reshape((2, -1) + array.shape[1:])
    first, last = both(send_first, send_last)
    arrays = [two(array) for array in (keep_first, first, keep_last, last)]
    arrays = fold_first(info, arrays, 4, 10000)
    last, first = both(arrays[1], arrays[0])
    grad_branch = after(grad_branch, arrays[0])
    grad_attn = matmul(info, grad_branch, out_weight, True)
    third = row_count // 3
    branch_pair = jnp.concatenate(
        [swap(grad_branch[i * third : (i + 1) * third], 0) for i in range(3)], 0
    )
    outs = pair_products(info, [(attn_low, attn_pair, grad_branch, branch_pair)], up_cols)
    feed_piece = fold_last(info, (arrays[2], first, arrays[3], last), 4)
    feed_whole = lax.all_gather(feed_piece, "seq", axis=0, tiled=False)
    feed_sum = lax.psum_scatter(
        after(feed_part, arrays[0]), "rank", scatter_dimension=0, tiled=True
    )
    first, last = both(outs[0], outs[1])
    grad_query, near, far = attend_back(
        in_order(info), query, grad_attn, attn_vals, log_total, cosine, sine, kv_all,
        start_rows, index_rows, True,
    )
    (grad_query, near, far), feed_sum = lax.optimization_barrier(
        (after((grad_query, near, far), first, last), feed_sum)
    )
    Order.last = grad_query

    far, query_pair = swap(far, 0), swap(grad_query, 0)
    outs = [two(array) for array in (outs[2], first, outs[3], last)]
    outs = fold_first(info, outs, 1)
    last, first = both(outs[1], outs[0])
    latent_grads = rings(latent_parts(info, grad_query, up_own, up_other, ranks))
    arrays = fold_near(info, near, far)
    out_piece = fold_last(info, (outs[2], first, outs[3], last), 1)
    out_whole = lax.all_gather(out_piece, "seq", axis=0, tiled=False)
    kv_first, kv_last = both(*after(arrays[:2], out_piece))
    ups = pair_products(info, [(latent_cut, latent_pair, grad_query, query_pair)], up_cols)
    wait(latent_grads, kv_first, kv_last)

    latent_own = latent_back(info, latent_all, recip_c, gain_all, norm2_part, latent_grads)
    latent_blocks = rings([latent_own] * ranks)
    arrays = fold_first(info, (arrays[2], kv_first, arrays[3], kv_last), 1)
    kv_last, kv_first = both(arrays[1], arrays[0])
    kv_sums = rings(fold_kv(info, (arrays[2], kv_first, arrays[3], kv_last), ranks))
    ups_first, ups_last = both(*in_order(ups[:2]))
    ups = fold_first(info, [two(array) for array in (ups[2], ups_first, ups[3], ups_last)], 1)
    ups_last, ups_first = both(ups[1], ups[0])
    layer_left, layer_right = layer_halves(info, residual, feed_sum)
    joined, *latent_blocks = lax.optimization_barrier((info, *latent_blocks))

    ups = rings(fold_up(joined, (ups[2], ups_first, ups[3], ups_last), ranks))
    kv_own = kv_back(info, cosine, sine, kv_sums)
    kv_blocks = rings([kv_own] * ranks)
    wait(kv_blocks)

    grad_in, small, latent_cols, grad_kv = input_back(
        info, tokens_in, grad_branch, norm1_gain, kv_weight, recip1, latent_all, kv_pre,
        latent_blocks, kv_blocks, downs,
    )
    last = last_products(info, normed_low, latent_cols, grad_kv, small, ranks)
    last = lax.psum(last, "seq")
    up_piece = pack_up(info, ups)
    lefts = rings([in_order(layer_left)] * ranks)
    up_pieces = [up_piece] + [exchange(in_order(up_piece), mask) for mask in (1, 2)]
    shape = gate_weight.shape
    grad_gate, grad_up, grad_down = unpack(
        info, feed_whole, store_feed, (shape, shape, shape[::-1]), (0, 0, 1)
    )
    rights = rings([in_order(layer_right)] * ranks)
    up_pieces += [exchange(in_order(up_piece), mask) for mask in range(3, 8)]
    grad_out = unpack(info, out_whole, store_same, [out_weight.shape], [0])[0]
    layer_out = place(info, lefts, rights)
    grad_q_up = unpack_up(info, up_pieces, q_up.shape)
    grad_q_down, grad_kv_weight, small = call(
        last_kernel,
        [(q_down.shape, F32), ((col_count, 2 * head_dim), F32), (small.shape, F32)],
        (last,),
        "last",
        prefetch=info,
    )

    small = small.reshape(-1)
    norm1 = small[model_width : model_width + col_count]
    grad_latent_gain = small[model_width + col_count : model_width + col_count + rank_cols]
    grad_norm2 = small[:model_width]
    return (
        layer_out,
        grad_in,
        norm1,
        grad_q_down,
        grad_latent_gain,
        grad_q_up,
        grad_kv_weight,
        grad_out,
        grad_norm2,
        grad_gate,
        grad_up,
        grad_down,
    )


def add_low(left, right):
    return (left.astype(F32) + right.astype(F32)).astype(BF)


def halve(value, axis, bit, seq_ix):
    own = bit_of(seq_ix, bit)
    keep = lax.dynamic_index_in_dim(value, own, axis, keepdims=False)
    send = lax.dynamic_index_in_dim(value, 1 - own, axis, keepdims=False)
    return add_low(keep, swap(send, bit))


def scatter_chips(value, seq_ix):
    bits = value.shape[0].bit_length() - 1
    shape = (2,) * bits + value.shape[2:]
    first, last = value[:, 0].reshape(shape), value[:, 1].reshape(shape)
    first_axes = list(range(bits))
    last_axes = list(range(bits))
    for step in range(bits):
        bit = step + 1
        axis = first_axes.index(bits - bit)
        first = halve(first, axis, bit, seq_ix)
        del first_axes[axis]
        bit = bits - step
        axis = last_axes.index(bits - bit)
        last = halve(last, axis, bit, seq_ix)
        del last_axes[axis]
    return jnp.stack([first, last])


def scatter_rows(near, far, seq_ix):
    return scatter_chips(add_low(near, swap(far, 0)), seq_ix)


def split_product(left, right, seq_ix):
    chips = lax.axis_size("seq") // 2
    rows = left.shape[1] // 2
    own = bit_of(seq_ix, 0)
    parts = []
    for core in (own, 1 - own):
        piece = lax.dynamic_slice_in_dim(left, core * rows, rows, 1)
        parts.append(dense_tn(piece, right).astype(BF))
    shape = (2, chips, rows // (2 * chips), right.shape[1])
    return [jnp.swapaxes(part.reshape(shape), 0, 1) for part in parts]


def gather_rows(piece):
    seq = lax.axis_size("seq")
    whole = lax.all_gather(piece, "seq", axis=0, tiled=False)
    whole = whole.reshape((seq // 2, 2) + piece.shape)
    whole = jnp.transpose(whole, (1, 2, 0, 3, 4))
    return whole.reshape(seq * piece.shape[0] * piece.shape[1], piece.shape[2])


def reduce_product(left, right, seq_ix):
    near, far = split_product(left, right, seq_ix)
    return gather_rows(scatter_rows(near, far, seq_ix)).astype(F32)


def high_low(values):
    high = values.astype(BF)
    return [high, (values - high.astype(F32)).astype(BF)]


def per_device_general(
    tokens_in,
    norm1_gain,
    q_down,
    latent_gain,
    q_up,
    kv_weight,
    out_weight,
    norm2_gain,
    gate_weight,
    up_weight,
    down_weight,
    doc_ids,
    out_grad,
):
    row_count, model_width = tokens_in.shape
    rank_count = lax.axis_size("rank")
    seq_count = lax.axis_size("seq")
    rank_ix = lax.axis_index("rank")
    seq_ix = lax.axis_index("seq")
    head_dim = kv_weight.shape[1] // 2
    local_heads = out_weight.shape[0] // head_dim
    first_row = seq_ix * row_count
    core = bit_of(seq_ix, 0)
    own_rows = row_count // rank_count
    rank_cols = q_down.shape[1]
    rank_width = rank_cols * rank_count

    half_rows = q_up.shape[0] // 2
    up_half = lax.dynamic_slice_in_dim(q_up, core * half_rows, half_rows, 0)
    up_half = lax.all_to_all(up_half, "rank", 1, 0, tiled=True)
    up_other = swap(up_half, 0)
    up_half = up_half.reshape(rank_count, 1, half_rows, -1)
    up_other = up_other.reshape(rank_count, 1, half_rows, -1)
    q_up_own = jnp.concatenate(
        [jnp.where(core == 0, up_half, up_other), jnp.where(core == 0, up_other, up_half)], 1
    ).reshape(rank_width, -1)

    ids_local = lax.dynamic_slice_in_dim(doc_ids, first_row, row_count, 0)
    start = jnp.sum((doc_ids[None, :] < ids_local[:, None]).astype(I32), 1)
    query_index = first_row + jnp.arange(row_count, dtype=I32)
    position = (query_index - start).astype(F32)
    half_dim = head_dim // 2
    freqs = BASE ** (-jnp.arange(half_dim, dtype=F32) / half_dim)
    angle = position[:, None] * freqs[None, :]
    cosine_rows, sine_rows = jnp.cos(angle), jnp.sin(angle)
    start_rows = jnp.tile(start, local_heads)[None]
    index_rows = jnp.tile(query_index, local_heads)[None]
    info = jnp.stack([first_row, start[0], start[-1], core]).astype(I32)

    tokens = tokens_in.astype(F32)
    normed_in, recip1 = norm_rows(tokens, norm1_gain)
    normed_low = normed_in.astype(BF)
    kv_pre = dense(normed_low, kv_weight)
    key_local = rotate(kv_pre[:, :head_dim], cosine_rows, sine_rows)
    kv_local = jnp.concatenate([key_local, kv_pre[:, head_dim:]], -1).astype(BF)
    kv_all = lax.all_gather(kv_local, "seq", axis=0, tiled=True)

    latent = dense(normed_low, q_down)
    high, rest = high_low(latent_gain)
    low = (latent_gain - high.astype(F32) - rest.astype(F32)).astype(BF)
    gain_rows = jnp.stack([high, rest, low] + [jnp.zeros_like(high)] * 13)
    gathered = lax.all_gather(
        jnp.concatenate([latent.astype(BF), gain_rows], 0), "rank", axis=1, tiled=True
    ).astype(F32)
    latent_all = gathered[:row_count]
    gain_all = gathered[row_count] + gathered[row_count + 1] + gathered[row_count + 2]
    recip_c = lax.rsqrt(jnp.mean(latent_all * latent_all, -1, keepdims=True) + EPS)
    latent_low = (latent_all * recip_c * gain_all).astype(BF)
    query_pre = dense(latent_low, q_up_own)

    query, attn_vals, attn_low, log_total, kv_all = attend(
        info, query_pre, cosine_rows, sine_rows, start, [(kv_all, None, 0)]
    )
    branch = lax.psum_scatter(
        dense(attn_low, out_weight).astype(BF), "rank", scatter_dimension=0, tiled=True
    )
    tokens_rows = lax.dynamic_slice_in_dim(tokens_in, rank_ix * own_rows, own_rows, 0)
    residual = tokens_rows.astype(F32) + branch.astype(F32)
    normed_mid, recip2 = norm_rows(residual, norm2_gain)
    mid_low = lax.all_gather(normed_mid.astype(BF), "rank", axis=0, tiled=True)

    grad_hidden = dense_nt(out_grad, down_weight)
    gate_pre = dense(mid_low, gate_weight)
    up_pre = dense(mid_low, up_weight)
    sigmoid_gate = jax.nn.sigmoid(gate_pre)
    activated = gate_pre * sigmoid_gate
    hidden_low = (activated * up_pre).astype(BF)
    grad_gate_pre = (
        grad_hidden * up_pre * sigmoid_gate * (1.0 + gate_pre * (1.0 - sigmoid_gate))
    ).astype(BF)
    grad_up_pre = (grad_hidden * activated).astype(BF)
    grad_mid = lax.psum_scatter(
        (dense_nt(grad_gate_pre, gate_weight) + dense_nt(grad_up_pre, up_weight)).astype(BF),
        "rank",
        scatter_dimension=0,
        tiled=True,
    ).astype(F32)
    feed_out = lax.psum_scatter(
        dense(hidden_low, down_weight).astype(BF), "rank", scatter_dimension=0, tiled=True
    )
    layer_out = lax.all_gather(
        (residual + feed_out.astype(F32)).astype(BF), "rank", axis=0, tiled=True
    )
    grad_gate = reduce_product(mid_low, grad_gate_pre, seq_ix)
    grad_up = reduce_product(mid_low, grad_up_pre, seq_ix)
    grad_down = reduce_product(hidden_low, out_grad, seq_ix)

    gained_mid = grad_mid * norm2_gain
    stat_mid = jnp.sum(residual * gained_mid, -1, keepdims=True)
    out_grad_rows = lax.dynamic_slice_in_dim(out_grad, rank_ix * own_rows, own_rows, 0)
    grad_residual = (
        out_grad_rows.astype(F32)
        + recip2 * gained_mid
        - residual * recip2**3 * stat_mid / model_width
    )
    grad_norm2 = jnp.sum(grad_mid * residual * recip2, 0)
    grad_branch = lax.all_gather(grad_residual.astype(BF), "rank", axis=0, tiled=True)
    grad_attn = dense_nt(grad_branch, out_weight).astype(BF)
    grad_out = reduce_product(attn_low, grad_branch, seq_ix)
    grad_query, near, far = attend_back(
        info, query, grad_attn, attn_vals, log_total, cosine_rows, sine_rows, kv_all,
        start_rows, index_rows, False,
    )

    chips = seq_count // 2
    summed = scatter_rows(jnp.swapaxes(near, 0, 1), jnp.swapaxes(far, 0, 1), seq_ix)
    summed = lax.psum(summed.reshape(row_count, 2 * head_dim), "rank").astype(F32)
    key_back = rotate(summed[:, :head_dim], cosine_rows, -sine_rows)
    grad_kv = jnp.concatenate([key_back, summed[:, head_dim:]], -1).astype(BF)

    grad_latent_part = dense_nt(grad_query, q_up_own).astype(BF)
    norm2_rows = jnp.concatenate(high_low(grad_norm2)).reshape(-1, rank_width)
    extra = norm2_rows.shape[0]
    norm2_rows = jnp.pad(norm2_rows, ((0, -extra % 16), (0, 0)))
    over_ranks = lax.psum(jnp.concatenate([grad_latent_part, norm2_rows], 0), "rank").astype(F32)
    grad_latent_in = over_ranks[:row_count]
    grad_norm2 = jnp.sum(
        over_ranks[row_count : row_count + extra].reshape(2, model_width), 0
    )
    gained_latent = grad_latent_in * gain_all
    stat_latent = jnp.sum(latent_all * gained_latent, -1, keepdims=True)
    grad_latent = (
        recip_c * gained_latent - latent_all * recip_c**3 * stat_latent / rank_width
    ).astype(BF)
    own_latent = lambda v: lax.dynamic_slice_in_dim(v, rank_ix * rank_cols, rank_cols, 1)
    grad_latent_gain = jnp.sum(own_latent(grad_latent_in) * latent * recip_c, 0)

    near, far = split_product(grad_query, latent_low, seq_ix)
    piece = scatter_rows(near, far, seq_ix)
    piece = lax.all_to_all(piece, "rank", 2, 0, tiled=True)
    piece = piece.reshape(rank_count * 2, piece.shape[1], rank_cols)
    whole = lax.all_gather(piece, "seq", axis=0, tiled=False)
    whole = whole.reshape(chips, 2, rank_count, 2, piece.shape[1], rank_cols)
    grad_q_up = jnp.transpose(whole, (5, 2, 1, 3, 0, 4)).reshape(rank_cols, -1).astype(F32)

    col_count = model_width // rank_count
    col_start = rank_ix * col_count
    cols = lambda v: lax.dynamic_slice_in_dim(v, col_start, col_count, v.ndim - 1)
    q_down_rows = lax.all_to_all(q_down, "rank", 0, 1, tiled=True)
    kv_rows = lax.dynamic_slice_in_dim(kv_weight, col_start, col_count, 0)
    grad_normed = dense_nt(grad_latent, q_down_rows) + dense_nt(grad_kv, kv_rows)
    norm1_stat = (
        jnp.sum(grad_latent.astype(F32) * latent_all, -1, keepdims=True)
        + jnp.sum(grad_kv.astype(F32) * kv_pre, -1, keepdims=True)
    ) / recip1
    tokens_own = cols(tokens_in).astype(F32)
    grad_in = (
        cols(grad_branch).astype(F32)
        + recip1 * cols(norm1_gain) * grad_normed
        - tokens_own * recip1**3 * norm1_stat / model_width
    )
    grad_norm1 = jnp.sum(grad_normed * tokens_own * recip1, 0)

    grad_q_down = lax.psum(
        dense_tn(normed_low, own_latent(grad_latent)).astype(BF), "seq"
    ).astype(F32)
    grad_kv_weight = dense_tn(cols(normed_low), grad_kv).astype(BF)
    small = jnp.concatenate([grad_norm1, grad_latent_gain, grad_norm2])
    small = jnp.concatenate(high_low(small)).reshape(2, -1)
    count = small.shape[1]
    kv_cols = grad_kv_weight.shape[1]
    small_rows = jnp.pad(small.reshape(-1), (0, -2 * count % (16 * kv_cols))).reshape(-1, kv_cols)
    last = lax.psum(jnp.concatenate([grad_kv_weight, small_rows], 0), "seq").astype(F32)
    grad_kv_weight = last[:col_count]
    small = jnp.sum(last[col_count:].reshape(-1)[: 2 * count].reshape(2, count), 0)
    grad_norm1 = small[:col_count]
    grad_latent_gain = small[col_count : col_count + rank_cols]
    grad_norm2 = small[col_count + rank_cols :]
    return (
        layer_out,
        grad_in,
        grad_norm1,
        grad_q_down,
        grad_latent_gain,
        grad_q_up,
        grad_kv_weight,
        grad_out,
        grad_norm2,
        grad_gate,
        grad_up,
        grad_down,
    )


def per_device(*args):
    tokens, out_weight = args[0], args[6]
    fits = (
        lax.axis_size("seq") == 8
        and lax.axis_size("rank") == 4
        and tokens.shape[0] % 64 == 0
        and tokens.shape[1] % 2048 == 0
        and args[2].shape[1] % 256 == 0
        and out_weight.shape[0] % 1024 == 0
        and args[8].shape[1] % LANES == 0
        and args[11].shape[0] % 512 == 0
    )
    return (per_device_fast if fits else per_device_general)(*args)


def solution(mesh):
    return jax.shard_map(
        per_device,
        mesh=mesh,
        in_specs=(
            P("seq", None),
            P(),
            P(None, "rank"),
            P("rank"),
            P("rank", None),
            P(),
            P("rank", None),
            P(),
            P(None, "rank"),
            P(None, "rank"),
            P("rank", None),
            P(),
            P("seq", None),
        ),
        out_specs=(
            P("seq", None),
            P("seq", "rank"),
            P("rank"),
            P(None, "rank"),
            P("rank"),
            P("rank", None),
            P("rank", None),
            P("rank", None),
            P(),
            P(None, "rank"),
            P(None, "rank"),
            P("rank", None),
        ),
        check_vma=False,
    )
```

```python
import functools

import jax
import jax.numpy as jnp
from jax import lax
from jax.experimental import pallas as pl
from jax.experimental.pallas import tpu as pltpu
from jax.sharding import PartitionSpec as P

EPS = 1e-05
BASE = 10000.0
NEG = -1e30
LOG2E = 1.4426950408889634
BF = jnp.bfloat16
F32 = jnp.float32
I32 = jnp.int32
LANES = 128

def norm_rows(values, gain):
    recip = lax.rsqrt(jnp.mean(values * values, -1, keepdims=True) + EPS)
    return (values * recip * gain, recip)


def rotate(values, cosine_rows, sine_rows):
    half_dim = values.shape[-1] // 2
    front_half = values[..., :half_dim]
    back_half = values[..., half_dim:]
    return jnp.concatenate(
        [
            front_half * cosine_rows - back_half * sine_rows,
            front_half * sine_rows + back_half * cosine_rows,
        ],
        -1,
    )


def dense(left, right):
    return jnp.dot(left, right, preferred_element_type=F32)


def dense_tn(left, right):
    return lax.dot_general(left, right, (((0,), (0,)), ((), ())), preferred_element_type=F32)


def dense_nt(left, right):
    return lax.dot_general(left, right, (((1,), (1,)), ((), ())), preferred_element_type=F32)


def key_block(key_count, most):
    for size in (1536, 1024, 512, 256, 128):
        if size <= most and key_count % size == 0:
            return size
    return key_count


def row_tile(rows):
    for parts in (3, 2):
        if rows % (parts * 128) == 0:
            return rows // parts
    return rows


def over_key_blocks(info_ref, size, tokens, run):
    first, low, high = info_ref[0], info_ref[1], info_ref[2]
    begin = low // size
    whole_end = jnp.maximum(first // size, begin)
    whole_begin = jnp.clip((high + size - 1) // size, begin, whole_end)
    end = (first + tokens + size - 1) // size
    lax.fori_loop(begin, whole_begin, lambda j, c: run(j, True), None)
    lax.fori_loop(whole_begin, whole_end, lambda j, c: run(j, False), None)
    lax.fori_loop(whole_end, end, lambda j, c: run(j, True), None)


def attend_kernel(
    size, tile, heads, places, wide, info_ref, pre_ref, cos_ref, sin_ref, first_ref, *refs
):
    pieces_in, refs = refs[: len(places)], refs[len(places) :]
    if wide:
        weight_in, refs = refs[0], refs[1:]
    query_ref, out_ref, low_ref, log_ref, kv_ref = refs[:5]
    max_ref, sum_ref, acc_ref, scores_ref, start_ref, index_ref, sems = refs[5 + wide : 12 + wide]
    tokens = pre_ref.shape[0]
    copies = []
    for n, (mask, offset) in enumerate(places):
        at = lax.bitwise_xor(info_ref[5], mask) * tokens + offset if mask is not None else 0
        rows = pl.ds(pl.multiple_of(at, 16), pieces_in[n].shape[0])
        copies.append(pltpu.make_async_copy(pieces_in[n], kv_ref.at[rows, :], sems.at[n]))
    for copy in copies:
        copy.start()
    if wide:
        branch_ref, weight_ref, weight_sem = refs[5], refs[13], refs[14]
        weight_copy = pltpu.make_async_copy(weight_in, weight_ref, weight_sem)
        weight_copy.start()
    width = kv_ref.shape[1] // 2
    half = width // 2
    lanes = max_ref.shape[1]
    scale = width**-0.5 * LOG2E
    cosine, sine = cos_ref[...], sin_ref[...]
    for h in range(heads):
        front = pre_ref[:, h * width : h * width + half]
        back = pre_ref[:, h * width + half : (h + 1) * width]
        rows = slice(h * tokens, (h + 1) * tokens)
        query_ref[rows, :half] = (front * cosine - back * sine).astype(BF)
        query_ref[rows, half:] = (front * sine + back * cosine).astype(BF)
        start_ref[rows, :] = first_ref[...]
        index_ref[rows, :] = info_ref[0] + lax.broadcasted_iota(I32, (tokens, lanes), 0)
    for copy in copies:
        copy.wait()
    pieces = [slice(n * lanes, (n + 1) * lanes) for n in range(size // lanes)]
    for i in range(heads * tokens // tile):
        r = slice(i * tile, (i + 1) * tile)
        max_ref[...] = jnp.full(max_ref.shape, NEG, F32)
        sum_ref[...] = jnp.zeros(sum_ref.shape, F32)
        acc_ref[...] = jnp.zeros(acc_ref.shape, F32)

        def score(j, masked, r=r):
            base = pl.multiple_of(j * size, size)
            scores = dense_nt(query_ref[r, :], kv_ref[pl.ds(base, size), :width])
            most = max_ref[...]
            lane = lax.broadcasted_iota(I32, max_ref.shape, 1)
            for n, piece in enumerate(pieces):
                part = scores[:, piece]
                if masked:
                    at = lane + (base + n * lanes)
                    allowed = (at >= start_ref[r, :]) & (at <= index_ref[r, :])
                    part = jnp.where(allowed, part, NEG)
                scores_ref[j, :, piece] = part
                most = jnp.maximum(most, part)
            max_ref[...] = most
            return None

        over_key_blocks(info_ref, size, tokens, score)
        most = jnp.max(max_ref[...], 1, keepdims=True) * scale
        max_ref[...] = jnp.broadcast_to(most, max_ref.shape)

        def mix(j, carry):
            base = pl.multiple_of(j * size, size)
            most, total = max_ref[...], sum_ref[...]
            probs = []
            for piece in pieces:
                prob = jnp.exp2(scores_ref[j, :, piece] * scale - most)
                total = total + prob
                probs.append(prob.astype(BF))
            sum_ref[...] = total
            acc_ref[...] += dense(jnp.concatenate(probs, 1), kv_ref[pl.ds(base, size), width:])
            return carry

        end = (info_ref[0] + tokens + size - 1) // size
        lax.fori_loop(info_ref[1] // size, end, mix, None)
        total = jnp.sum(sum_ref[...], 1, keepdims=True)
        log_ref[:, r] = jnp.broadcast_to(most + jnp.log2(total), max_ref.shape).T[0:1, :]
        out = acc_ref[...] * (1.0 / total)
        at = i * tile
        while at < (i + 1) * tile:
            h = at // tokens
            stop = min((i + 1) * tile, (h + 1) * tokens)
            rows, cols = slice(at - h * tokens, stop - h * tokens), slice(h * width, (h + 1) * width)
            part = out[at - i * tile : stop - i * tile, :]
            out_ref[rows, cols] = part
            low_ref[rows, cols] = part.astype(BF)
            at = stop

    if wide:
        weight_copy.wait()

        def branch(i, carry):
            cols = pl.ds(pl.multiple_of(i * 512, 512), 512)
            branch_ref[:, cols] = dense(low_ref[...], weight_ref[:, cols]).astype(BF)
            return carry

        lax.fori_loop(0, branch_ref.shape[1] // 512, branch, None)


def in_vmem(count):
    return [pl.BlockSpec(memory_space=pltpu.VMEM) for _ in range(count)]


def attend(info, query_pre, cosine, sine, start, pieces, weight=None):
    tokens, all_heads = query_pre.shape
    width = pieces[0][0].shape[1] // 2
    keys = sum(piece[0].shape[0] for piece in pieces)
    rows = tokens * (all_heads // width)
    size = key_block(keys, 1536)
    tile = rows // 2 if rows % 256 == 0 else row_tile(rows)
    wide = weight is not None
    branch = [((tokens, weight.shape[1]), BF)] if wide else []
    start = jnp.broadcast_to(start[:, None], (tokens, LANES))
    return pl.pallas_call(
        functools.partial(
            attend_kernel, size, tile, all_heads // width, [piece[1:] for piece in pieces], wide
        ),
        out_shape=(
            jax.ShapeDtypeStruct((rows, width), BF),
            jax.ShapeDtypeStruct((tokens, all_heads), F32),
            jax.ShapeDtypeStruct((tokens, all_heads), BF),
            jax.ShapeDtypeStruct((1, rows), F32),
            jax.ShapeDtypeStruct((keys, 2 * width), BF),
            *[jax.ShapeDtypeStruct(*out) for out in branch],
        ),
        in_specs=[pl.BlockSpec(memory_space=pltpu.SMEM)]
        + in_vmem(4)
        + [pl.BlockSpec(memory_space=pl.ANY)] * (len(pieces) + wide),
        out_specs=tuple(in_vmem(5 + wide)),
        scratch_shapes=[
            pltpu.VMEM((tile, LANES), F32),
            pltpu.VMEM((tile, LANES), F32),
            pltpu.VMEM((tile, width), F32),
            pltpu.VMEM((keys // size, tile, size), F32),
            pltpu.VMEM((rows, LANES), I32),
            pltpu.VMEM((rows, LANES), I32),
            pltpu.SemaphoreType.DMA((len(pieces),)),
        ]
        + ([pltpu.VMEM(weight.shape, BF), pltpu.SemaphoreType.DMA(())] if wide else []),
        compiler_params=pltpu.CompilerParams(vmem_limit_bytes=56 * 2**20),
        cost_estimate=brief(0),
        name="attend",
    )(info, query_pre, cosine, sine, start, *[piece[0] for piece in pieces], *([weight] if wide else []))


def attend_back_kernel(
    size, tile, heads, by_axis, info_ref, query_ref, grad_ref, out_ref, log_ref, cos_ref, sin_ref, kv_ref, start_ref, index_ref,
    gq_ref, near_ref, far_ref, gout_ref, gk_ref, gv_ref, gqt_ref, dots_ref,
):
    tokens = grad_ref.shape[0]
    width = kv_ref.shape[1] // 2
    half = width // 2
    scale = width**-0.5
    for h in range(heads):
        gout = grad_ref[:, h * width : (h + 1) * width]
        gout_ref[h * tokens : (h + 1) * tokens, :] = gout
        dots = gout.astype(F32) * out_ref[:, h * width : (h + 1) * width]
        dots_ref[h * tokens : (h + 1) * tokens, :] = dots[:, :half] + dots[:, half:]
    delta = jnp.sum(dots_ref[...].T, 0, keepdims=True)
    gk_ref[...] = jnp.zeros(gk_ref.shape, F32)
    gv_ref[...] = jnp.zeros(gv_ref.shape, F32)
    gqt_ref[...] = jnp.zeros(gqt_ref.shape, F32)

    def run(j, masked):
        base = pl.multiple_of(j * size, size)
        at_keys = pl.ds(base, size)
        keys = kv_ref[at_keys, :width]
        values = kv_ref[at_keys, width:]
        for i in range(heads * tokens // tile):
            r = slice(i * tile, (i + 1) * tile)
            query, gout = query_ref[r, :], gout_ref[r, :]
            probs = jnp.exp2(dense_nt(keys, query) * (scale * LOG2E) - log_ref[:, r])
            if masked:
                at = base + lax.broadcasted_iota(I32, (size, tile), 0)
                allowed = (at >= start_ref[:, r]) & (at <= index_ref[:, r])
                probs = jnp.where(allowed, probs, 0.0)
            gscores = (probs * (dense_nt(values, gout) - delta[:, r])).astype(BF)
            gv_ref[at_keys, :] += dense(probs.astype(BF), gout)
            gk_ref[at_keys, :] += dense(gscores, query)
            gqt_ref[:, r] += dense_tn(keys, gscores)
        return None

    over_key_blocks(info_ref, size, tokens, run)
    mine = info_ref[3]
    part = tokens // 2
    for s in range(kv_ref.shape[0] // part):
        rows = slice(s * part, (s + 1) * part)
        chip = s // 4
        if by_axis and s % 2 == 0:
            chip = chip % 2 * 2 + chip // 2
        gk = (gk_ref[rows, :] * scale).astype(BF)
        gv = gv_ref[rows, :].astype(BF)

        @pl.when(mine == s // 2 % 2)
        def _(s=s, chip=chip, gk=gk, gv=gv):
            near_ref[s % 2, chip, :, :width] = gk
            near_ref[s % 2, chip, :, width:] = gv

        @pl.when(mine != s // 2 % 2)
        def _(s=s, chip=chip, gk=gk, gv=gv):
            far_ref[s % 2, chip, :, :width] = gk
            far_ref[s % 2, chip, :, width:] = gv

    gq = (gqt_ref[...] * scale).T.astype(BF).astype(F32)
    cosine, sine = cos_ref[...], sin_ref[...]
    for h in range(heads):
        front = gq[h * tokens : (h + 1) * tokens, :half]
        back = gq[h * tokens : (h + 1) * tokens, half:]
        gq_ref[:, h * width : h * width + half] = (front * cosine + back * sine).astype(BF)
        gq_ref[:, h * width + half : (h + 1) * width] = (back * cosine - front * sine).astype(BF)


def attend_back(info, query, grad, out, log, cosine, sine, kv, start, index, by_axis):
    tokens, all_heads = grad.shape
    keys, width = kv.shape[0], kv.shape[1] // 2
    rows = tokens * (all_heads // width)
    blocks = keys // tokens
    return pl.pallas_call(
        functools.partial(
            attend_back_kernel, key_block(keys, 512), row_tile(rows), all_heads // width, by_axis
        ),
        out_shape=(
            jax.ShapeDtypeStruct((tokens, all_heads), BF),
            jax.ShapeDtypeStruct((2, blocks // 2, tokens // 2, 2 * width), BF),
            jax.ShapeDtypeStruct((2, blocks // 2, tokens // 2, 2 * width), BF),
        ),
        in_specs=[pl.BlockSpec(memory_space=pltpu.SMEM)] + in_vmem(9),
        out_specs=tuple(in_vmem(3)),
        scratch_shapes=[
            pltpu.VMEM((rows, width), BF),
            pltpu.VMEM((keys, width), F32),
            pltpu.VMEM((keys, width), F32),
            pltpu.VMEM((width, rows), F32),
            pltpu.VMEM((rows, width // 2), F32),
        ],
        compiler_params=pltpu.CompilerParams(vmem_limit_bytes=56 * 2**20),
        cost_estimate=brief(0),
        name="attend_back",
    )(info, query, grad, out, log, cosine, sine, kv, start, index)


def feed_kernel(tile, mid_ref, grad_ref, gate_ref, up_ref, hidden_ref, both_ref, part_ref):
    width = gate_ref.shape[1]

    def run(i, carry):
        rows = pl.ds(pl.multiple_of(i * tile, tile), tile)
        mid = mid_ref[rows, :]
        gate = dense(mid, gate_ref[...])
        up = dense(mid, up_ref[...])
        grad = grad_ref[rows, :]
        sigmoid = 1.0 / (1.0 + jnp.exp(-gate))
        active = gate * sigmoid
        hidden_ref[rows, :] = (active * up).astype(BF)
        grad_gate = (grad * up * sigmoid * (1.0 + gate * (1.0 - sigmoid))).astype(BF)
        grad_up = (grad * active).astype(BF)
        both_ref[rows, :width] = grad_gate
        both_ref[rows, width:] = grad_up
        part = dense_nt(grad_gate, gate_ref[...]) + dense_nt(grad_up, up_ref[...])
        part_ref[rows, :] = part.astype(BF)
        return carry

    lax.fori_loop(0, mid_ref.shape[0] // tile, run, None)


def feed_forward(mid, grad, gate, up):
    rows, model = mid.shape
    width = gate.shape[1]
    tile = next(t for t in (288, 192, 144, 96, 64, 48, 32, 16, rows) if rows % t == 0)
    return pl.pallas_call(
        functools.partial(feed_kernel, tile),
        out_shape=(
            jax.ShapeDtypeStruct((rows, width), BF),
            jax.ShapeDtypeStruct((rows, 2 * width), BF),
            jax.ShapeDtypeStruct((rows, model), BF),
        ),
        in_specs=in_vmem(4),
        out_specs=tuple(in_vmem(3)),
        compiler_params=pltpu.CompilerParams(vmem_limit_bytes=40 * 2**20),
        cost_estimate=brief(20),
        name="feed_forward",
    )(mid, grad, gate, up)


class Order:
    last = None


def brief(micros):
    return pl.CostEstimate(flops=int(micros * 1e8), bytes_accessed=0, transcendentals=0)


def call(kernel, outs, args, name, micros=0, scratch=(), grid=None, in_specs=None, out_specs=None, prefetch=None):
    out_shape = tuple(jax.ShapeDtypeStruct(*out) for out in outs)
    prefetch = in_order(prefetch)
    params = dict(
        out_shape=out_shape,
        compiler_params=pltpu.CompilerParams(vmem_limit_bytes=56 * 2**20),
        cost_estimate=brief(micros),
        name=name,
    )
    outs = placed_call(kernel, out_shape, args, params, scratch, grid, in_specs, out_specs, prefetch)
    Order.last = outs[0]
    return outs


def in_order(value):
    return value if Order.last is None else after(value, Order.last)


def wait(*values):
    Order.last = (Order.last, values)


def placed_call(kernel, out_shape, args, params, scratch, grid, in_specs, out_specs, prefetch):
    if grid is None:
        return pl.pallas_call(
            kernel,
            in_specs=[pl.BlockSpec(memory_space=pltpu.SMEM)] + in_vmem(len(args)),
            out_specs=tuple(in_vmem(len(out_shape))),
            scratch_shapes=list(scratch),
            **params,
        )(prefetch, *args)
    return pl.pallas_call(
        kernel,
        grid_spec=pltpu.PrefetchScalarGridSpec(
            num_scalar_prefetch=1,
            grid=grid,
            in_specs=in_specs,
            out_specs=tuple(out_specs),
            scratch_shapes=list(scratch),
        ),
        **params,
    )(prefetch, *args)


def once(shape, index):
    return pl.BlockSpec(shape, index, pipeline_mode=pl.Buffered(1))


def at_block(index, size):
    return pl.ds(pl.multiple_of(index * size, size), size)


CORE, RANK, SEQ = 3, 4, 5


def ahead(info_ref, shift, ranks):
    return lax.rem(info_ref[RANK] + shift, ranks)


def behind(info_ref, shift, ranks):
    return lax.rem(info_ref[RANK] + ranks - shift, ranks)


def chip_of(info_ref):
    return lax.div(info_ref[SEQ], 2)


def rank_blocks(info, index):
    return lambda i, info_ref: index(info_ref[RANK])


def project_kernel(
    info_ref, tokens_ref, gain_ref, down_ref, kv_weight_ref, latent_gain_ref, normed_ref, recip_ref, kv_ref, low_ref
):
    values = tokens_ref[...].astype(F32)
    normed, recip = norm_rows(values, gain_ref[...])
    normed_ref[...] = normed.astype(BF)
    recip_ref[...] = jnp.broadcast_to(recip, recip_ref.shape)
    rows = normed_ref.shape[0]
    low_ref[at_block(pl.program_id(0), rows), :] = dense(normed_ref[...], down_ref[...]).astype(BF)

    @pl.when(pl.program_id(0) == 0)
    def _():
        rest = latent_gain_ref[...]
        parts = []
        for _ in range(3):
            parts.append(rest.astype(BF))
            rest = rest - parts[-1].astype(F32)
        parts.append(jnp.zeros((EXTRA - 3, rest.shape[1]), BF))
        low_ref[low_ref.shape[0] - EXTRA :, :] = jnp.concatenate(parts, 0)

    kv_ref[...] = dense(normed_ref[...], kv_weight_ref[...])


EXTRA = 16


def project(info, tokens, gain, q_down, kv_weight, latent_gain):
    rows, model = tokens.shape
    tile = rows // 2
    widths = ((model, BF), (LANES, F32), (kv_weight.shape[1], F32))
    low = (rows + EXTRA, q_down.shape[1])
    return call(
        project_kernel,
        [((rows, width), dtype) for width, dtype in widths] + [(low, BF)],
        (tokens, gain.reshape(1, -1), q_down, kv_weight, latent_gain.reshape(1, -1)),
        "project",
        grid=(2,),
        in_specs=[
            pl.BlockSpec((tile, model), lambda i, w: (i, 0)),
            once((1, model), lambda i, w: (0, 0)),
            once(q_down.shape, lambda i, w: (0, 0)),
            once(kv_weight.shape, lambda i, w: (0, 0)),
            once((1, q_down.shape[1]), lambda i, w: (0, 0)),
        ],
        out_specs=[pl.BlockSpec((tile, width), lambda i, w: (i, 0)) for width, _ in widths]
        + [pl.BlockSpec(low, lambda i, w: (0, 0))],
        prefetch=info,
    )


def turn_kernel(info_ref, kv_ref, cos_ref, sin_ref, out_ref):
    half = cos_ref.shape[1]
    front, back = kv_ref[:, :half], kv_ref[:, half : 2 * half]
    cosine, sine = cos_ref[...], sin_ref[...]
    out_ref[:, :half] = (front * cosine - back * sine).astype(BF)
    out_ref[:, half : 2 * half] = (front * sine + back * cosine).astype(BF)
    out_ref[:, 2 * half :] = kv_ref[:, 2 * half :].astype(BF)


def turn(info, kv_pre, cosine, sine):
    return call(turn_kernel, [(kv_pre.shape, BF)], (kv_pre, cosine, sine), "turn", prefetch=info)[0]


def query_kernel(info_ref, latent_ref, own_ref, other_ref, low_ref, recip_ref, gain_ref, query_ref):
    rows = low_ref.shape[0]
    parts = latent_ref[rows:, :].astype(F32)
    gain_ref[...] = parts[0:1] + parts[1:2] + parts[2:3]
    normed, recip = norm_rows(latent_ref[:rows, :].astype(F32), gain_ref[...])
    low_ref[...] = normed.astype(BF)
    recip_ref[...] = jnp.broadcast_to(recip, recip_ref.shape)
    half = own_ref.shape[1]
    ranks = 4
    cols = latent_ref.shape[1] // ranks
    totals = [0.0, 0.0]
    for s in range(ranks):
        left = low_ref[:, at_block(behind(info_ref, s, ranks), cols)]
        for n, ref in enumerate((own_ref, other_ref)):
            totals[n] = totals[n] + dense(left, ref[s * cols : (s + 1) * cols, :])
    core = info_ref[CORE]
    query_ref[:, at_block(core, half)] = totals[0]
    query_ref[:, at_block(1 - core, half)] = totals[1]


def queries(info, latent, own, other):
    rows, width = latent.shape[0] - EXTRA, latent.shape[1]
    return call(
        query_kernel,
        [((rows, width), BF), ((rows, LANES), F32), ((1, width), F32), ((rows, 2 * own.shape[1]), F32)],
        (latent, own, other),
        "queries",
        prefetch=info,
    )


def latent_part_kernel(info_ref, grad_ref, own_ref, other_ref, *refs):
    outs, all_ref = refs[:-1], refs[-1]
    ranks, rows = len(outs), outs[0].shape[0]
    half, cols = own_ref.shape[1], own_ref.shape[0] // ranks
    core = info_ref[CORE]
    own_grad = grad_ref[:, at_block(core, half)]
    other_grad = grad_ref[:, at_block(1 - core, half)]
    for s in range(ranks):
        part = slice(s * cols, (s + 1) * cols)
        out = dense_nt(own_grad, own_ref[part, :]) + dense_nt(other_grad, other_ref[part, :])
        all_ref[:, at_block(behind(info_ref, s, ranks), cols)] = out.astype(BF)
    for s in range(ranks):
        outs[s][...] = all_ref[at_block(ahead(info_ref, s, ranks), rows), :]


def latent_parts(info, grad, own, other, ranks):
    rows, width = grad.shape[0], own.shape[0]
    return call(
        latent_part_kernel,
        [((rows // ranks, width), BF)] * ranks,
        (grad, own, other),
        "latent_parts",
        scratch=[pltpu.VMEM((rows, width), BF)],
        prefetch=info,
    )


def latent_back_kernel(info_ref, latent_ref, recip_ref, gain_ref, norm2_ref, *refs):
    parts, grad_ref = refs[:-1], refs[-1]
    grad_in = sum(part[...].astype(F32) for part in parts)
    latent = latent_ref[...].astype(F32)
    recip = recip_ref[:, 0:1]
    gained = grad_in * gain_ref[...]
    stat = jnp.sum(latent * gained, -1, keepdims=True)
    grad = recip * gained - latent * (recip * recip * recip * stat / latent.shape[1])
    rows, width = grad.shape
    grad_ref[:rows, :] = grad.astype(BF)
    sums = [norm2_ref[:, i * width : (i + 1) * width] for i in range(norm2_ref.shape[1] // width)]
    sums = jnp.concatenate(sums + [jnp.sum(grad_in * latent * recip, 0, keepdims=True)], 0)
    high = sums.astype(BF)
    low = (sums - high.astype(F32)).astype(BF)
    fill = jnp.zeros((EXTRA - 2 * sums.shape[0], width), BF)
    grad_ref[rows:, :] = jnp.concatenate([high, low, fill], 0)


def latent_back(info, latent, recip, gain, norm2, parts):
    rows, width = parts[0].shape
    return call(
        latent_back_kernel,
        [((rows + EXTRA, width), BF)],
        (latent, recip, gain, norm2, *parts),
        "latent_back",
        grid=(1,),
        in_specs=[
            pl.BlockSpec((rows, width), lambda i, w: (w[RANK], 0)),
            pl.BlockSpec((rows, LANES), lambda i, w: (w[RANK], 0)),
            pl.BlockSpec((1, width), lambda i, w: (0, 0)),
            pl.BlockSpec(norm2.shape, lambda i, w: (0, 0)),
        ]
        + [pl.BlockSpec((rows, width), lambda i, w: (0, 0)) for _ in parts],
        out_specs=[pl.BlockSpec((rows + EXTRA, width), lambda i, w: (0, 0))],
        prefetch=info,
    )[0]


def kv_back_kernel(info_ref, cos_ref, sin_ref, *refs):
    parts, out_ref = refs[:-1], refs[-1]
    total = sum(part[...].astype(F32) for part in parts).astype(BF).astype(F32)
    half = cos_ref.shape[1]
    front, back = total[:, :half], total[:, half : 2 * half]
    cosine, sine = cos_ref[...], sin_ref[...]
    out_ref[:, :half] = (front * cosine + back * sine).astype(BF)
    out_ref[:, half : 2 * half] = (back * cosine - front * sine).astype(BF)
    out_ref[:, 2 * half :] = total[:, 2 * half :].astype(BF)


def kv_back(info, cosine, sine, parts):
    rows, width = parts[0].shape
    return call(
        kv_back_kernel,
        [((rows, width), BF)],
        (cosine, sine, *parts),
        "kv_back",
        grid=(1,),
        in_specs=[pl.BlockSpec((rows, cosine.shape[1]), lambda i, w: (w[RANK], 0))] * 2
        + [pl.BlockSpec((rows, width), lambda i, w: (0, 0)) for _ in parts],
        out_specs=[pl.BlockSpec((rows, width), lambda i, w: (0, 0))],
        prefetch=info,
    )[0]


def mid_kernel(info_ref, branch_ref, tokens_ref, gain_ref, residual_ref, mid_ref, recip_ref):
    residual = tokens_ref[...].astype(F32) + branch_ref[...].astype(F32)
    normed, recip = norm_rows(residual, gain_ref[...])
    residual_ref[...] = residual
    mid_ref[...] = normed.astype(BF)
    recip_ref[...] = jnp.broadcast_to(recip, recip_ref.shape)


def mid_norm(info, branch, tokens, gain):
    rows, model = branch.shape
    whole = pl.BlockSpec((rows, model), lambda i, w: (0, 0))
    return call(
        mid_kernel,
        [((rows, model), F32), ((rows, model), BF), ((rows, LANES), F32)],
        (branch, tokens, gain.reshape(1, -1)),
        "mid_norm",
        grid=(1,),
        in_specs=[
            whole,
            pl.BlockSpec((rows, model), lambda i, w: (w[RANK], 0)),
            pl.BlockSpec((1, model), lambda i, w: (0, 0)),
        ],
        out_specs=[whole, whole, pl.BlockSpec((rows, LANES), lambda i, w: (0, 0))],
        prefetch=info,
    )


def mid_back_kernel(info_ref, grad_ref, residual_ref, recip_ref, gain_ref, out_grad_ref, branch_ref, gain_grad_ref):
    grad = grad_ref[...].astype(F32)
    residual = residual_ref[...]
    recip = recip_ref[:, 0:1]
    gained = grad * gain_ref[...]
    stat = jnp.sum(residual * gained, -1, keepdims=True)
    out = out_grad_ref[...].astype(F32) + recip * gained
    out = out - residual * (recip * recip * recip * stat / residual.shape[1])
    branch_ref[...] = out.astype(BF)
    gain_grad_ref[...] = jnp.sum(grad * residual * recip, 0, keepdims=True)


def mid_back(info, grad, residual, recip, gain, out_grad):
    rows, model = grad.shape
    whole = pl.BlockSpec((rows, model), lambda i, w: (0, 0))
    return call(
        mid_back_kernel,
        [((rows, model), BF), ((1, model), F32)],
        (grad, residual, recip, gain.reshape(1, -1), out_grad),
        "mid_back",
        grid=(1,),
        in_specs=[
            whole,
            whole,
            pl.BlockSpec((rows, LANES), lambda i, w: (0, 0)),
            pl.BlockSpec((1, model), lambda i, w: (0, 0)),
            pl.BlockSpec((rows, model), lambda i, w: (w[RANK], 0)),
        ],
        out_specs=[whole, pl.BlockSpec((1, model), lambda i, w: (0, 0))],
        prefetch=info,
    )


def matmul_kernel(dims, info_ref, left_ref, right_ref, *refs):
    out = lax.dot_general(left_ref[...], right_ref[...], (dims, ((), ())), preferred_element_type=F32)
    if len(refs) == 1:
        refs[0][...] = out.astype(BF)
        return
    outs, all_ref = refs[:-1], refs[-1]
    all_ref[...] = out.astype(BF)
    for s, out_ref in enumerate(outs):
        out_ref[...] = all_ref[at_block(ahead(info_ref, s, len(outs)), out_ref.shape[0]), :]


def matmul(info, left, right, transposed=False, parts=1):
    rows, depth = left.shape
    cols = right.shape[0 if transposed else 1]
    tile = next(t for t in ((512, 256, LANES) if transposed else (1024, 512, 256, LANES)) if cols % t == 0)
    if transposed:
        dims, spec = ((1,), (1,)), pl.BlockSpec((tile, depth), lambda i, w: (i, 0))
    else:
        dims, spec = ((1,), (0,)), pl.BlockSpec((depth, tile), lambda i, w: (0, i))
    outs = call(
        functools.partial(matmul_kernel, dims),
        [((rows // parts, cols), BF)] * parts,
        (left, right),
        "matmul",
        scratch=[pltpu.VMEM((rows, tile), BF)] if parts > 1 else [],
        grid=(cols // tile,),
        in_specs=[once((rows, depth), lambda i, w: (0, 0)), spec],
        out_specs=[pl.BlockSpec((rows // parts, tile), lambda i, w: (0, i))] * parts,
        prefetch=info,
    )
    return outs if parts > 1 else outs[0]


def quarter_order(info_ref):
    bit_x = lax.rem(chip_of(info_ref), 2)
    bit_y = lax.div(chip_of(info_ref), 2)
    return 1 - bit_x, 3 - bit_y, bit_x, 2 + bit_y


def product_kernel(counts, info_ref, *refs):
    outs, all_ref = refs[4 * len(counts) : 4 * len(counts) + 4], refs[-1]
    order = quarter_order(info_ref)
    rows = outs[0].shape[0]
    first = 0
    for n, count in enumerate(counts):
        own, other, own_right, other_right = refs[4 * n : 4 * n + 4]
        step = pl.program_id(0)

        def mixed(cols):
            out = dense_tn(own[:, cols], own_right[...])
            return (out + dense_tn(other[:, cols], other_right[...])).astype(BF)

        @pl.when((step >= first) & (step < first + count))
        def _():
            if rows >= 256:
                for out_ref, at in zip(outs, order):
                    out_ref[...] = mixed(at_block(at, rows))
            else:
                all_ref[...] = mixed(slice(None))
                for out_ref, at in zip(outs, order):
                    out_ref[...] = all_ref[at_block(at, rows), :]

        first += count


def pair_products(info, terms, tile):
    tokens, rows = terms[0][0].shape[0], terms[0][0].shape[1] // 2
    counts = [term[2].shape[1] // tile for term in terms]
    specs, args, first = [], [], 0
    for term, count in zip(terms, counts):
        specs += [once((tokens, rows), lambda i, w: (0, w[CORE]))] * 2
        place = lambda i, w, first=first, count=count: (0, jnp.clip(i - first, 0, count - 1))
        specs += [pl.BlockSpec((tokens, tile), place)] * 2
        args += term
        first += count
    return call(
        functools.partial(product_kernel, counts),
        [((rows // 4, first * tile), BF)] * 4,
        args,
        "pair_products",
        scratch=[pltpu.VMEM((rows, tile) if rows < 1024 else (16, LANES), BF)],
        grid=(first,),
        in_specs=specs,
        out_specs=[pl.BlockSpec((rows // 4, tile), lambda i, w: (0, i))] * 4,
        prefetch=info,
    )


def add_low(left, right):
    return (left.astype(F32) + right.astype(F32)).astype(BF)


def fold_near_kernel(info_ref, near_ref, got_ref, *outs):
    for out_ref, at in zip(outs, quarter_order(info_ref)):
        p, bit = lax.div(at, 2), lax.rem(at, 2)
        for other in range(2):
            chip = bit * 2 + other
            out_ref[other] = add_low(near_ref[p, chip], got_ref[p, chip])


def fold_near(info, near, got):
    _, chips, rows, cols = near.shape
    tile = rows // 3
    return call(
        fold_near_kernel,
        [((2, rows, cols), BF)] * 4,
        (near, got),
        "fold_near",
        grid=(3,),
        in_specs=[pl.BlockSpec((2, chips, tile, cols), lambda i, w: (0, 0, i, 0))] * 2,
        out_specs=[pl.BlockSpec((2, tile, cols), lambda i, w: (0, i, 0))] * 4,
        prefetch=info,
    )


def fold_first_kernel(info_ref, keep_first, got_first, keep_last, got_last, *outs):
    bit_x = lax.rem(chip_of(info_ref), 2)
    bit_y = lax.div(chip_of(info_ref), 2)
    outs[0][...] = add_low(keep_first[1 - bit_y], got_first[1 - bit_y])
    outs[1][...] = add_low(keep_last[1 - bit_x], got_last[1 - bit_x])
    outs[2][...] = add_low(keep_first[bit_y], got_first[bit_y])
    outs[3][...] = add_low(keep_last[bit_x], got_last[bit_x])


def fold_first(info, arrays, steps, micros=0):
    rows, cols = arrays[0].shape[1:]
    tile = rows // steps
    return call(
        fold_first_kernel,
        [((rows, cols), BF)] * 4,
        arrays,
        "fold_first",
        micros,
        grid=(steps,),
        in_specs=[pl.BlockSpec((2, tile, cols), lambda i, w: (0, i, 0))] * 4,
        out_specs=[pl.BlockSpec((tile, cols), lambda i, w: (i, 0))] * 4,
        prefetch=info,
    )


def fold_last_kernel(info_ref, keep_first, got_first, keep_last, got_last, out_ref):
    out_ref[0] = add_low(keep_first[...], got_first[...])
    out_ref[1] = add_low(keep_last[...], got_last[...])


def fold_last(info, arrays, steps):
    rows, cols = arrays[0].shape
    tile = rows // steps
    return call(
        fold_last_kernel,
        [((2, rows, cols), BF)],
        arrays,
        "fold_last",
        grid=(steps,),
        in_specs=[pl.BlockSpec((tile, cols), lambda i, w: (i, 0))] * 4,
        out_specs=[pl.BlockSpec((2, tile, cols), lambda i, w: (0, i, 0))],
        prefetch=info,
    )[0]


def fold_kv_kernel(info_ref, keep_first, got_first, keep_last, got_last, *refs):
    outs, all_ref = refs[:-1], refs[-1]
    half = keep_first.shape[0]
    all_ref[:half, :] = add_low(keep_first[...], got_first[...])
    all_ref[half:, :] = add_low(keep_last[...], got_last[...])
    for s, out_ref in enumerate(outs):
        out_ref[...] = all_ref[at_block(ahead(info_ref, s, len(outs)), out_ref.shape[0]), :]


def fold_kv(info, arrays, ranks):
    rows, cols = arrays[0].shape
    return call(
        fold_kv_kernel,
        [((2 * rows // ranks, cols), BF)] * ranks,
        arrays,
        "fold_kv",
        scratch=[pltpu.VMEM((2 * rows, cols), BF)],
        prefetch=info,
    )


def fold_up_kernel(info_ref, keep_first, got_first, keep_last, got_last, *refs):
    ups, all_ref = refs[:-1], refs[-1]
    all_ref[0] = add_low(keep_first[...], got_first[...])
    all_ref[1] = add_low(keep_last[...], got_last[...])
    for s, up_ref in enumerate(ups):
        up_ref[...] = all_ref[:, at_block(ahead(info_ref, s, len(ups)), up_ref.shape[1]), :]


def fold_up(info, arrays, ranks):
    rows, cols = arrays[0].shape
    return call(
        fold_up_kernel,
        [((2, rows // ranks, cols), BF)] * ranks,
        arrays,
        "fold_up",
        scratch=[pltpu.VMEM((2, rows, cols), BF)],
        prefetch=info,
    )


def pack_up_kernel(info_ref, *refs):
    ups, all_ref = refs[:-1], refs[-1]
    for s, up_ref in enumerate(ups):
        all_ref[:, at_block(behind(info_ref, s, len(ups)), up_ref.shape[1]), :] = up_ref[...]


def pack_up(info, ups):
    _, rows, cols = ups[0].shape
    return call(pack_up_kernel, [((2, rows * len(ups), cols), BF)], ups, "pack_up", prefetch=info)[0]


def layer_kernel(info_ref, residual_ref, feed_ref, left_ref, right_ref):
    half = left_ref.shape[1]
    out = (residual_ref[...] + feed_ref[...].astype(F32)).astype(BF)
    left_ref[...] = out[:, :half]
    right_ref[...] = out[:, half:]


def layer_halves(info, residual, feed):
    rows, model = residual.shape
    return call(
        layer_kernel, [((rows, model // 2), BF)] * 2, (residual, feed), "layer", prefetch=info
    )


def place_kernel(info_ref, *refs):
    out_ref = refs[-1]
    half = out_ref.shape[1] // 2
    for s in range(len(refs) // 2):

        @pl.when(pl.program_id(0) == s)
        def _(s=s):
            out_ref[:, :half] = refs[2 * s][...]
            out_ref[:, half:] = refs[2 * s + 1][...]


def place(info, lefts, rights):
    rows, cols = lefts[0].shape
    ranks = len(lefts)
    parts = [part for pair in zip(lefts, rights) for part in pair]
    return call(
        place_kernel,
        [((ranks * rows, 2 * cols), BF)],
        parts,
        "place",
        grid=(ranks,),
        in_specs=[once((rows, cols), lambda i, w: (0, 0))] * len(parts),
        out_specs=[pl.BlockSpec((rows, 2 * cols), lambda i, w: (behind(w, i, ranks), 0))],
        prefetch=info,
    )[0]


def input_back_kernel(
    ranks, info_ref, tokens_ref, branch_ref, gain_ref, kv_weight_ref, recip_ref, latent_ref, kv_pre_ref, *refs
):
    latents, kvs, downs = refs[:ranks], refs[ranks : 2 * ranks], refs[2 * ranks : 3 * ranks]
    grad_in_ref, small_ref, own_ref, kv_ref, all_ref, sums_ref = refs[3 * ranks :]
    rows = kvs[0].shape[0]
    cols = own_ref.shape[1]
    sums = 0.0
    for s in range(ranks):
        at = at_block(behind(info_ref, s, ranks), rows)
        all_ref[at, :] = latents[s][:rows, :]
        sums = sums + latents[s][rows:, :].astype(F32)
        kv_ref[at, :] = kvs[s][...]
    grad = dense_nt(kv_ref[...], kv_weight_ref[...])
    for s in range(ranks):
        at = at_block(behind(info_ref, s, ranks), cols)
        grad = grad + dense_nt(all_ref[:, at], downs[s][...])
    own_ref[...] = all_ref[:, at_block(info_ref[RANK], cols)]
    recip = recip_ref[:, 0:1]
    latent = latent_ref[: all_ref.shape[0], :].astype(F32)
    stat = jnp.sum(all_ref[...].astype(F32) * latent, -1, keepdims=True)
    stat = stat + jnp.sum(kv_ref[...].astype(F32) * kv_pre_ref[...], -1, keepdims=True)
    tokens = tokens_ref[...].astype(F32)
    model = tokens.shape[1] * ranks
    out = branch_ref[...].astype(F32) + recip * gain_ref[...] * grad
    grad_in_ref[...] = out - tokens * (recip * recip * stat / model)
    count = sums.shape[0] // 16 * 3
    sums = sums[:count] + sums[count : 2 * count]
    sums_ref[...] = sums[count - 1 :]
    norm1 = jnp.sum(grad * tokens * recip, 0, keepdims=True)
    lines = [sums[r : r + 1, i * cols : (i + 1) * cols] for r in range(count - 1) for i in range(sums.shape[1] // cols)]
    lines += [norm1[:, i * cols : (i + 1) * cols] for i in range(norm1.shape[1] // cols)]
    lines.append(sums_ref[:, at_block(info_ref[RANK], cols)])
    lines += [jnp.zeros_like(lines[0])] * (small_ref.shape[0] - len(lines))
    small_ref[...] = jnp.concatenate(lines, 0).astype(BF)


def input_back(info, tokens, branch, gain, kv_weight, recip, latent, kv_pre, latents, kvs, downs):
    ranks = len(latents)
    rows, model = tokens.shape
    cols = model // ranks
    width, down = kv_weight.shape[1], downs[0].shape[1]
    whole = lambda array: pl.BlockSpec(array.shape, lambda i, w: (0, 0))
    wide = pl.BlockSpec((rows, cols), lambda i, w: (0, w[RANK]))
    outs = [((rows, cols), F32), ((16, down), BF), ((rows, down), BF), ((rows, width), BF)]
    return call(
        functools.partial(input_back_kernel, ranks),
        outs,
        (tokens, branch, gain.reshape(1, -1), kv_weight, recip, latent, kv_pre, *latents, *kvs, *downs),
        "input_back",
        scratch=[pltpu.VMEM((rows, latent.shape[1]), BF), pltpu.VMEM((1, latent.shape[1]), F32)],
        grid=(1,),
        in_specs=[
            wide,
            wide,
            pl.BlockSpec((1, cols), lambda i, w: (0, w[RANK])),
            pl.BlockSpec((cols, width), lambda i, w: (w[RANK], 0)),
        ]
        + [whole(array) for array in (recip, latent, kv_pre, *latents, *kvs, *downs)],
        out_specs=[pl.BlockSpec(shape, lambda i, w: (0, 0)) for shape, _ in outs],
        prefetch=info,
    )


def last_products_kernel(info_ref, normed_ref, latent_ref, kv_ref, small_ref, out_ref):
    rows, width = normed_ref.shape[1], latent_ref.shape[1]
    out_ref[:rows, :] = dense_tn(normed_ref[...], latent_ref[...]).astype(BF)
    count = (out_ref.shape[0] - rows - small_ref.shape[0]) // 2
    wide = dense_tn(normed_ref[:, at_block(info_ref[RANK], count)], kv_ref[...]).astype(BF)
    out_ref[rows : rows + count, :] = wide[:, :width]
    out_ref[rows + count : rows + 2 * count, :] = wide[:, width:]
    out_ref[rows + 2 * count :, :] = small_ref[...]


def last_products(info, normed, latent, kv, small, ranks):
    model, width = normed.shape[1], latent.shape[1]
    shape = (model + 2 * model // ranks + small.shape[0], width)
    return call(
        last_products_kernel, [(shape, BF)], (normed, latent, kv, small), "last_products", prefetch=info
    )[0]


def last_kernel(info_ref, in_ref, down_ref, kv_ref, small_ref):
    rows, width = down_ref.shape
    count = kv_ref.shape[0]
    down_ref[...] = in_ref[:rows, :].astype(F32)
    kv_ref[:, :width] = in_ref[rows : rows + count, :].astype(F32)
    kv_ref[:, width:] = in_ref[rows + count : rows + 2 * count, :].astype(F32)
    small_ref[...] = in_ref[rows + 2 * count :, :].astype(F32)


def store_feed(part, at, gate_ref, up_ref, down_ref):
    rows, width = part.shape[0], gate_ref.shape[1]
    block = slice(at * rows, (at + 1) * rows)
    gate_ref[block, :] = part[:, :width].astype(F32)
    up_ref[block, :] = part[:, width : 2 * width].astype(F32)
    down_ref[:, block] = part[:, 2 * width :].astype(F32).T


def store_same(part, at, out_ref):
    rows = part.shape[0]
    out_ref[at * rows : (at + 1) * rows, :] = part.astype(F32)


def unpack_up_kernel(info_ref, *refs):
    out_ref = refs[-1]
    for mask, ref in enumerate(refs[:-1]):
        source = lax.bitwise_xor(info_ref[SEQ], mask)
        core, chip = lax.rem(source, 2), lax.div(source, 2)
        _, rows, cols = ref.shape
        rows = rows // (out_ref.shape[1] // cols)
        for p in range(2):
            place = lax.rem(chip, 2) * 2 + lax.div(chip, 2) if p == 0 else chip
            at = at_block(core * 8 + p * 4 + place, rows)
            for r in range(out_ref.shape[1] // cols):
                block = ref[p, r * rows : (r + 1) * rows, :].astype(F32)
                out_ref[at, r * cols : (r + 1) * cols] = block


def unpack_up(info, pieces, shape):
    return call(unpack_up_kernel, [(shape, F32)], pieces, "unpack_up", prefetch=info)[0]


def unpack_kernel(store, info_ref, in_ref, *out_refs):
    part = lax.rem(pl.program_id(0), 2)
    for chip in range(4):
        turned = chip % 2 * 2 + chip // 2
        pl.when(part == 0)(lambda chip=chip, at=turned: store(in_ref[chip], at, *out_refs))
        pl.when(part == 1)(lambda chip=chip: store(in_ref[chip], chip, *out_refs))


def unpack(info, whole, store, shapes, along):
    _, _, rows, cols = whole.shape
    whole = whole.reshape(4, 2, 2, rows, cols)
    out_specs = []
    for (height, width), dim in zip(shapes, along):
        if dim == 0:
            out_specs.append(pl.BlockSpec((height // 4, width), lambda i, w: (i, 0)))
        else:
            out_specs.append(pl.BlockSpec((height, width // 4), lambda i, w: (0, i)))
    return call(
        functools.partial(unpack_kernel, store),
        [(shape, F32) for shape in shapes],
        (whole,),
        "unpack",
        grid=(4,),
        in_specs=[
            pl.BlockSpec((4, None, None, rows, cols), lambda i, w: (0, i // 2, i % 2, 0, 0))
        ],
        out_specs=out_specs,
        prefetch=info,
    )


def bit_of(index, bit):
    return (index >> bit) & 1


def exchange(value, mask):
    count = lax.axis_size("seq")
    return lax.ppermute(value, "seq", [(i, i ^ mask) for i in range(count)])


def swap(value, bit):
    return exchange(value, 1 << bit)


def ring(value, shift):
    if not shift:
        return value
    ranks = lax.axis_size("rank")
    return lax.ppermute(value, "rank", [(i, (i + shift) % ranks) for i in range(ranks)])


def rings(values):
    return [ring(value, s) for s, value in enumerate(values)]


def both(first, last):
    return swap(first, 1), swap(last, 2)


def sum_over(value, axis):
    count = lax.axis_size(axis)
    mask = 1
    while mask < count:
        value = value + lax.ppermute(value, axis, [(i, i ^ mask) for i in range(count)])
        mask *= 2
    return value


def after(value, *others):
    return lax.optimization_barrier((value, others))[0]


def per_device_fast(
    tokens_in,
    norm1_gain,
    q_down,
    latent_gain,
    q_up,
    kv_weight,
    out_weight,
    norm2_gain,
    gate_weight,
    up_weight,
    down_weight,
    doc_ids,
    out_grad,
):
    Order.last = None
    row_count, model_width = tokens_in.shape
    ranks = lax.axis_size("rank")
    rank_ix = lax.axis_index("rank")
    seq_ix = lax.axis_index("seq")
    head_dim = kv_weight.shape[1] // 2
    local_heads = out_weight.shape[0] // head_dim
    first_row = seq_ix * row_count
    core = bit_of(seq_ix, 0)
    rank_cols = q_down.shape[1]
    rank_width = rank_cols * ranks
    col_count = model_width // ranks

    up_cols = q_up.shape[1] // ranks
    half_cols = up_cols // 2
    blocks = [
        lax.dynamic_slice_in_dim(
            q_up, lax.rem(rank_ix + s, ranks) * up_cols + core * half_cols, half_cols, 1
        )
        for s in range(ranks)
    ]
    tokens_late = after(tokens_in, blocks)
    up_own = jnp.concatenate(rings(blocks), 0)
    up_other = swap(up_own, 0)

    ids_local = lax.dynamic_slice_in_dim(doc_ids, first_row, row_count, 0)
    start = jnp.sum((doc_ids[None, :] < ids_local[:, None]).astype(I32), 1)
    query_index = first_row + jnp.arange(row_count, dtype=I32)
    position = (query_index - start).astype(F32)
    half_dim = head_dim // 2
    freqs = BASE ** (-jnp.arange(half_dim, dtype=F32) / half_dim)
    angle = position[:, None] * freqs[None, :]
    cosine, sine = jnp.cos(angle), jnp.sin(angle)
    start_rows = jnp.tile(start, local_heads)[None]
    index_rows = jnp.tile(query_index, local_heads)[None]
    place_info = jnp.stack([first_row, first_row, first_row, core, rank_ix, seq_ix]).astype(I32)
    info = jnp.stack([first_row, start[0], start[-1], core, rank_ix, seq_ix]).astype(I32)

    normed_low, recip1, kv_pre, latent = project(
        place_info, tokens_late, norm1_gain, q_down, kv_weight, latent_gain
    )
    latent_all = lax.all_gather(latent, "rank", axis=1, tiled=True)

    kv_local = turn(place_info, kv_pre, cosine, sine)
    half_rows = row_count // 2
    by_x, by_y = lax.optimization_barrier(both(kv_local, kv_local))
    top, bottom = swap(by_x[:half_rows], 2), swap(by_y[half_rows:], 1)
    pieces = [(kv_local, 0, 0), (by_x, 2, 0), (by_y, 4, 0), (top, 6, 0), (bottom, 6, half_rows)]
    pieces += [(swap(array, 0), mask ^ 1, offset) for array, mask, offset in pieces]

    latent_low, recip_c, gain_all, query_pre = queries(place_info, latent_all, up_own, up_other)
    query, attn_vals, attn_low, log_total, kv_all, branch_part = attend(
        in_order(info), query_pre, cosine, sine, start, pieces, out_weight
    )
    Order.last = attn_low

    branch = lax.psum_scatter(branch_part, "rank", scatter_dimension=0, tiled=True)
    grad_hidden = dense_nt(after(out_grad, branch_part), down_weight)
    out_grad_pair = swap(after(out_grad, branch_part), 0)
    attn_pair = swap(attn_low, 0)
    piece_cols = rank_cols // 16
    latent_cut = jnp.transpose(
        after(latent_low, branch_part).reshape(row_count, ranks, 16, piece_cols), (0, 2, 1, 3)
    ).reshape(row_count, rank_width)
    latent_pair = swap(latent_cut, 0)
    down_blocks = [
        lax.dynamic_slice_in_dim(
            after(q_down, branch_part), lax.rem(rank_ix + s, ranks) * col_count, col_count, 0
        )
        for s in range(ranks)
    ]
    branch = after(
        branch, grad_hidden, out_grad_pair, attn_pair, latent_pair, latent_cut, down_blocks
    )
    residual, mid_own, recip2 = mid_norm(info, branch, tokens_in, norm2_gain)
    mid_low = lax.all_gather(mid_own, "rank", axis=0, tiled=True)

    downs = rings(after(down_blocks, mid_low))
    mid_pair = swap(mid_low, 0)
    hidden_low, grad_both, grad_mid_part = feed_forward(
        mid_low, grad_hidden, gate_weight, up_weight
    )
    Order.last = hidden_low
    hidden_low, grad_both, grad_mid_part = after((hidden_low, grad_both, grad_mid_part), downs)
    grad_mid = lax.psum_scatter(grad_mid_part, "rank", scatter_dimension=0, tiled=True)
    both_pair, hidden_pair = swap(grad_both, 0), swap(hidden_low, 0)
    feed_part = matmul(info, hidden_low, down_weight)
    feed_width = gate_weight.shape[1]
    send_first, send_last, keep_first, keep_last = pair_products(
        info,
        [
            (mid_low, mid_pair, grad_both, both_pair),
            (out_grad, out_grad_pair, hidden_low, hidden_pair),
        ],
        feed_width,
    )
    grad_mid = after(grad_mid, send_first)
    branch_own, norm2_part = mid_back(info, grad_mid, residual, recip2, norm2_gain, out_grad)
    grad_branch = lax.all_gather(branch_own, "rank", axis=0, tiled=True)

    two = lambda array: array.reshape((2, -1) + array.shape[1:])
    first, last = both(send_first, send_last)
    arrays = [two(array) for array in (keep_first, first, keep_last, last)]
    arrays = fold_first(info, arrays, 4, 10000)
    last, first = both(arrays[1], arrays[0])
    grad_branch = after(grad_branch, arrays[0])
    grad_attn = matmul(info, grad_branch, out_weight, True)
    third = row_count // 3
    branch_pair = jnp.concatenate(
        [swap(grad_branch[i * third : (i + 1) * third], 0) for i in range(3)], 0
    )
    outs = pair_products(info, [(attn_low, attn_pair, grad_branch, branch_pair)], up_cols)
    feed_piece = fold_last(info, (arrays[2], first, arrays[3], last), 4)
    feed_whole = lax.all_gather(feed_piece, "seq", axis=0, tiled=False)
    feed_sum = lax.psum_scatter(
        after(feed_part, arrays[0]), "rank", scatter_dimension=0, tiled=True
    )
    first, last = both(outs[0], outs[1])
    grad_query, near, far = attend_back(
        in_order(info), query, grad_attn, attn_vals, log_total, cosine, sine, kv_all,
        start_rows, index_rows, True,
    )
    (grad_query, near, far), feed_sum = lax.optimization_barrier(
        (after((grad_query, near, far), first, last), feed_sum)
    )
    Order.last = grad_query

    far, query_pair = swap(far, 0), swap(grad_query, 0)
    outs = [two(array) for array in (outs[2], first, outs[3], last)]
    outs = fold_first(info, outs, 1)
    last, first = both(outs[1], outs[0])
    latent_grads = rings(latent_parts(info, grad_query, up_own, up_other, ranks))
    arrays = fold_near(info, near, far)
    out_piece = fold_last(info, (outs[2], first, outs[3], last), 1)
    out_whole = lax.all_gather(out_piece, "seq", axis=0, tiled=False)
    kv_first, kv_last = both(*after(arrays[:2], out_piece))
    ups = pair_products(info, [(latent_cut, latent_pair, grad_query, query_pair)], up_cols)
    wait(latent_grads, kv_first, kv_last)

    latent_own = latent_back(info, latent_all, recip_c, gain_all, norm2_part, latent_grads)
    latent_blocks = rings([latent_own] * ranks)
    arrays = fold_first(info, (arrays[2], kv_first, arrays[3], kv_last), 1)
    kv_last, kv_first = both(arrays[1], arrays[0])
    kv_sums = rings(fold_kv(info, (arrays[2], kv_first, arrays[3], kv_last), ranks))
    ups_first, ups_last = both(*in_order(ups[:2]))
    ups = fold_first(info, [two(array) for array in (ups[2], ups_first, ups[3], ups_last)], 1)
    ups_last, ups_first = both(ups[1], ups[0])
    layer_left, layer_right = layer_halves(info, residual, feed_sum)
    joined, *latent_blocks = lax.optimization_barrier((info, *latent_blocks))

    ups = rings(fold_up(joined, (ups[2], ups_first, ups[3], ups_last), ranks))
    kv_own = kv_back(info, cosine, sine, kv_sums)
    kv_blocks = rings([kv_own] * ranks)
    wait(kv_blocks)

    grad_in, small, latent_cols, grad_kv = input_back(
        info, tokens_in, grad_branch, norm1_gain, kv_weight, recip1, latent_all, kv_pre,
        latent_blocks, kv_blocks, downs,
    )
    last = last_products(info, normed_low, latent_cols, grad_kv, small, ranks)
    last = lax.psum(last, "seq")
    up_piece = pack_up(info, ups)
    lefts = rings([in_order(layer_left)] * ranks)
    up_pieces = [up_piece] + [exchange(in_order(up_piece), mask) for mask in (1, 2)]
    shape = gate_weight.shape
    grad_gate, grad_up, grad_down = unpack(
        info, feed_whole, store_feed, (shape, shape, shape[::-1]), (0, 0, 1)
    )
    rights = rings([in_order(layer_right)] * ranks)
    up_pieces += [exchange(in_order(up_piece), mask) for mask in range(3, 8)]
    grad_out = unpack(info, out_whole, store_same, [out_weight.shape], [0])[0]
    layer_out = place(info, lefts, rights)
    grad_q_up = unpack_up(info, up_pieces, q_up.shape)
    grad_q_down, grad_kv_weight, small = call(
        last_kernel,
        [(q_down.shape, F32), ((col_count, 2 * head_dim), F32), (small.shape, F32)],
        (last,),
        "last",
        prefetch=info,
    )

    small = small.reshape(-1)
    norm1 = small[model_width : model_width + col_count]
    grad_latent_gain = small[model_width + col_count : model_width + col_count + rank_cols]
    grad_norm2 = small[:model_width]
    return (
        layer_out,
        grad_in,
        norm1,
        grad_q_down,
        grad_latent_gain,
        grad_q_up,
        grad_kv_weight,
        grad_out,
        grad_norm2,
        grad_gate,
        grad_up,
        grad_down,
    )


def add_low(left, right):
    return (left.astype(F32) + right.astype(F32)).astype(BF)


def halve(value, axis, bit, seq_ix):
    own = bit_of(seq_ix, bit)
    keep = lax.dynamic_index_in_dim(value, own, axis, keepdims=False)
    send = lax.dynamic_index_in_dim(value, 1 - own, axis, keepdims=False)
    return add_low(keep, swap(send, bit))


def scatter_chips(value, seq_ix):
    bits = value.shape[0].bit_length() - 1
    shape = (2,) * bits + value.shape[2:]
    first, last = value[:, 0].reshape(shape), value[:, 1].reshape(shape)
    first_axes = list(range(bits))
    last_axes = list(range(bits))
    for step in range(bits):
        bit = step + 1
        axis = first_axes.index(bits - bit)
        first = halve(first, axis, bit, seq_ix)
        del first_axes[axis]
        bit = bits - step
        axis = last_axes.index(bits - bit)
        last = halve(last, axis, bit, seq_ix)
        del last_axes[axis]
    return jnp.stack([first, last])


def scatter_rows(near, far, seq_ix):
    return scatter_chips(add_low(near, swap(far, 0)), seq_ix)


def split_product(left, right, seq_ix):
    chips = lax.axis_size("seq") // 2
    rows = left.shape[1] // 2
    own = bit_of(seq_ix, 0)
    parts = []
    for core in (own, 1 - own):
        piece = lax.dynamic_slice_in_dim(left, core * rows, rows, 1)
        parts.append(dense_tn(piece, right).astype(BF))
    shape = (2, chips, rows // (2 * chips), right.shape[1])
    return [jnp.swapaxes(part.reshape(shape), 0, 1) for part in parts]


def gather_rows(piece):
    seq = lax.axis_size("seq")
    whole = lax.all_gather(piece, "seq", axis=0, tiled=False)
    whole = whole.reshape((seq // 2, 2) + piece.shape)
    whole = jnp.transpose(whole, (1, 2, 0, 3, 4))
    return whole.reshape(seq * piece.shape[0] * piece.shape[1], piece.shape[2])


def reduce_product(left, right, seq_ix):
    near, far = split_product(left, right, seq_ix)
    return gather_rows(scatter_rows(near, far, seq_ix)).astype(F32)


def high_low(values):
    high = values.astype(BF)
    return [high, (values - high.astype(F32)).astype(BF)]


def per_device_general(
    tokens_in,
    norm1_gain,
    q_down,
    latent_gain,
    q_up,
    kv_weight,
    out_weight,
    norm2_gain,
    gate_weight,
    up_weight,
    down_weight,
    doc_ids,
    out_grad,
):
    row_count, model_width = tokens_in.shape
    rank_count = lax.axis_size("rank")
    seq_count = lax.axis_size("seq")
    rank_ix = lax.axis_index("rank")
    seq_ix = lax.axis_index("seq")
    head_dim = kv_weight.shape[1] // 2
    local_heads = out_weight.shape[0] // head_dim
    first_row = seq_ix * row_count
    core = bit_of(seq_ix, 0)
    own_rows = row_count // rank_count
    rank_cols = q_down.shape[1]
    rank_width = rank_cols * rank_count

    half_rows = q_up.shape[0] // 2
    up_half = lax.dynamic_slice_in_dim(q_up, core * half_rows, half_rows, 0)
    up_half = lax.all_to_all(up_half, "rank", 1, 0, tiled=True)
    up_other = swap(up_half, 0)
    up_half = up_half.reshape(rank_count, 1, half_rows, -1)
    up_other = up_other.reshape(rank_count, 1, half_rows, -1)
    q_up_own = jnp.concatenate(
        [jnp.where(core == 0, up_half, up_other), jnp.where(core == 0, up_other, up_half)], 1
    ).reshape(rank_width, -1)

    ids_local = lax.dynamic_slice_in_dim(doc_ids, first_row, row_count, 0)
    start = jnp.sum((doc_ids[None, :] < ids_local[:, None]).astype(I32), 1)
    query_index = first_row + jnp.arange(row_count, dtype=I32)
    position = (query_index - start).astype(F32)
    half_dim = head_dim // 2
    freqs = BASE ** (-jnp.arange(half_dim, dtype=F32) / half_dim)
    angle = position[:, None] * freqs[None, :]
    cosine_rows, sine_rows = jnp.cos(angle), jnp.sin(angle)
    start_rows = jnp.tile(start, local_heads)[None]
    index_rows = jnp.tile(query_index, local_heads)[None]
    info = jnp.stack([first_row, start[0], start[-1], core]).astype(I32)

    tokens = tokens_in.astype(F32)
    normed_in, recip1 = norm_rows(tokens, norm1_gain)
    normed_low = normed_in.astype(BF)
    kv_pre = dense(normed_low, kv_weight)
    key_local = rotate(kv_pre[:, :head_dim], cosine_rows, sine_rows)
    kv_local = jnp.concatenate([key_local, kv_pre[:, head_dim:]], -1).astype(BF)
    kv_all = lax.all_gather(kv_local, "seq", axis=0, tiled=True)

    latent = dense(normed_low, q_down)
    high, rest = high_low(latent_gain)
    low = (latent_gain - high.astype(F32) - rest.astype(F32)).astype(BF)
    gain_rows = jnp.stack([high, rest, low] + [jnp.zeros_like(high)] * 13)
    gathered = lax.all_gather(
        jnp.concatenate([latent.astype(BF), gain_rows], 0), "rank", axis=1, tiled=True
    ).astype(F32)
    latent_all = gathered[:row_count]
    gain_all = gathered[row_count] + gathered[row_count + 1] + gathered[row_count + 2]
    recip_c = lax.rsqrt(jnp.mean(latent_all * latent_all, -1, keepdims=True) + EPS)
    latent_low = (latent_all * recip_c * gain_all).astype(BF)
    query_pre = dense(latent_low, q_up_own)

    query, attn_vals, attn_low, log_total, kv_all = attend(
        info, query_pre, cosine_rows, sine_rows, start, [(kv_all, None, 0)]
    )
    branch = lax.psum_scatter(
        dense(attn_low, out_weight).astype(BF), "rank", scatter_dimension=0, tiled=True
    )
    tokens_rows = lax.dynamic_slice_in_dim(tokens_in, rank_ix * own_rows, own_rows, 0)
    residual = tokens_rows.astype(F32) + branch.astype(F32)
    normed_mid, recip2 = norm_rows(residual, norm2_gain)
    mid_low = lax.all_gather(normed_mid.astype(BF), "rank", axis=0, tiled=True)

    grad_hidden = dense_nt(out_grad, down_weight)
    gate_pre = dense(mid_low, gate_weight)
    up_pre = dense(mid_low, up_weight)
    sigmoid_gate = jax.nn.sigmoid(gate_pre)
    activated = gate_pre * sigmoid_gate
    hidden_low = (activated * up_pre).astype(BF)
    grad_gate_pre = (
        grad_hidden * up_pre * sigmoid_gate * (1.0 + gate_pre * (1.0 - sigmoid_gate))
    ).astype(BF)
    grad_up_pre = (grad_hidden * activated).astype(BF)
    grad_mid = lax.psum_scatter(
        (dense_nt(grad_gate_pre, gate_weight) + dense_nt(grad_up_pre, up_weight)).astype(BF),
        "rank",
        scatter_dimension=0,
        tiled=True,
    ).astype(F32)
    feed_out = lax.psum_scatter(
        dense(hidden_low, down_weight).astype(BF), "rank", scatter_dimension=0, tiled=True
    )
    layer_out = lax.all_gather(
        (residual + feed_out.astype(F32)).astype(BF), "rank", axis=0, tiled=True
    )
    grad_gate = reduce_product(mid_low, grad_gate_pre, seq_ix)
    grad_up = reduce_product(mid_low, grad_up_pre, seq_ix)
    grad_down = reduce_product(hidden_low, out_grad, seq_ix)

    gained_mid = grad_mid * norm2_gain
    stat_mid = jnp.sum(residual * gained_mid, -1, keepdims=True)
    out_grad_rows = lax.dynamic_slice_in_dim(out_grad, rank_ix * own_rows, own_rows, 0)
    grad_residual = (
        out_grad_rows.astype(F32)
        + recip2 * gained_mid
        - residual * recip2**3 * stat_mid / model_width
    )
    grad_norm2 = jnp.sum(grad_mid * residual * recip2, 0)
    grad_branch = lax.all_gather(grad_residual.astype(BF), "rank", axis=0, tiled=True)
    grad_attn = dense_nt(grad_branch, out_weight).astype(BF)
    grad_out = reduce_product(attn_low, grad_branch, seq_ix)
    grad_query, near, far = attend_back(
        info, query, grad_attn, attn_vals, log_total, cosine_rows, sine_rows, kv_all,
        start_rows, index_rows, False,
    )

    chips = seq_count // 2
    summed = scatter_rows(jnp.swapaxes(near, 0, 1), jnp.swapaxes(far, 0, 1), seq_ix)
    summed = lax.psum(summed.reshape(row_count, 2 * head_dim), "rank").astype(F32)
    key_back = rotate(summed[:, :head_dim], cosine_rows, -sine_rows)
    grad_kv = jnp.concatenate([key_back, summed[:, head_dim:]], -1).astype(BF)

    grad_latent_part = dense_nt(grad_query, q_up_own).astype(BF)
    norm2_rows = jnp.concatenate(high_low(grad_norm2)).reshape(-1, rank_width)
    extra = norm2_rows.shape[0]
    norm2_rows = jnp.pad(norm2_rows, ((0, -extra % 16), (0, 0)))
    over_ranks = lax.psum(jnp.concatenate([grad_latent_part, norm2_rows], 0), "rank").astype(F32)
    grad_latent_in = over_ranks[:row_count]
    grad_norm2 = jnp.sum(
        over_ranks[row_count : row_count + extra].reshape(2, model_width), 0
    )
    gained_latent = grad_latent_in * gain_all
    stat_latent = jnp.sum(latent_all * gained_latent, -1, keepdims=True)
    grad_latent = (
        recip_c * gained_latent - latent_all * recip_c**3 * stat_latent / rank_width
    ).astype(BF)
    own_latent = lambda v: lax.dynamic_slice_in_dim(v, rank_ix * rank_cols, rank_cols, 1)
    grad_latent_gain = jnp.sum(own_latent(grad_latent_in) * latent * recip_c, 0)

    near, far = split_product(grad_query, latent_low, seq_ix)
    piece = scatter_rows(near, far, seq_ix)
    piece = lax.all_to_all(piece, "rank", 2, 0, tiled=True)
    piece = piece.reshape(rank_count * 2, piece.shape[1], rank_cols)
    whole = lax.all_gather(piece, "seq", axis=0, tiled=False)
    whole = whole.reshape(chips, 2, rank_count, 2, piece.shape[1], rank_cols)
    grad_q_up = jnp.transpose(whole, (5, 2, 1, 3, 0, 4)).reshape(rank_cols, -1).astype(F32)

    col_count = model_width // rank_count
    col_start = rank_ix * col_count
    cols = lambda v: lax.dynamic_slice_in_dim(v, col_start, col_count, v.ndim - 1)
    q_down_rows = lax.all_to_all(q_down, "rank", 0, 1, tiled=True)
    kv_rows = lax.dynamic_slice_in_dim(kv_weight, col_start, col_count, 0)
    grad_normed = dense_nt(grad_latent, q_down_rows) + dense_nt(grad_kv, kv_rows)
    norm1_stat = (
        jnp.sum(grad_latent.astype(F32) * latent_all, -1, keepdims=True)
        + jnp.sum(grad_kv.astype(F32) * kv_pre, -1, keepdims=True)
    ) / recip1
    tokens_own = cols(tokens_in).astype(F32)
    grad_in = (
        cols(grad_branch).astype(F32)
        + recip1 * cols(norm1_gain) * grad_normed
        - tokens_own * recip1**3 * norm1_stat / model_width
    )
    grad_norm1 = jnp.sum(grad_normed * tokens_own * recip1, 0)

    grad_q_down = lax.psum(
        dense_tn(normed_low, own_latent(grad_latent)).astype(BF), "seq"
    ).astype(F32)
    grad_kv_weight = dense_tn(cols(normed_low), grad_kv).astype(BF)
    small = jnp.concatenate([grad_norm1, grad_latent_gain, grad_norm2])
    small = jnp.concatenate(high_low(small)).reshape(2, -1)
    count = small.shape[1]
    kv_cols = grad_kv_weight.shape[1]
    small_rows = jnp.pad(small.reshape(-1), (0, -2 * count % (16 * kv_cols))).reshape(-1, kv_cols)
    last = lax.psum(jnp.concatenate([grad_kv_weight, small_rows], 0), "seq").astype(F32)
    grad_kv_weight = last[:col_count]
    small = jnp.sum(last[col_count:].reshape(-1)[: 2 * count].reshape(2, count), 0)
    grad_norm1 = small[:col_count]
    grad_latent_gain = small[col_count : col_count + rank_cols]
    grad_norm2 = small[col_count + rank_cols :]
    return (
        layer_out,
        grad_in,
        grad_norm1,
        grad_q_down,
        grad_latent_gain,
        grad_q_up,
        grad_kv_weight,
        grad_out,
        grad_norm2,
        grad_gate,
        grad_up,
        grad_down,
    )


def per_device(*args):
    tokens, out_weight = args[0], args[6]
    fits = (
        lax.axis_size("seq") == 8
        and lax.axis_size("rank") == 4
        and tokens.shape[0] % 64 == 0
        and tokens.shape[1] % 2048 == 0
        and args[2].shape[1] % 256 == 0
        and out_weight.shape[0] % 1024 == 0
        and args[8].shape[1] % LANES == 0
        and args[11].shape[0] % 512 == 0
    )
    return (per_device_fast if fits else per_device_general)(*args)


def solution(mesh):
    return jax.shard_map(
        per_device,
        mesh=mesh,
        in_specs=(
            P("seq", None),
            P(),
            P(None, "rank"),
            P("rank"),
            P("rank", None),
            P(),
            P("rank", None),
            P(),
            P(None, "rank"),
            P(None, "rank"),
            P("rank", None),
            P(),
            P("seq", None),
        ),
        out_specs=(
            P("seq", None),
            P("seq", "rank"),
            P("rank"),
            P(None, "rank"),
            P("rank"),
            P("rank", None),
            P("rank", None),
            P("rank", None),
            P(),
            P(None, "rank"),
            P(None, "rank"),
            P("rank", None),
        ),
        check_vma=False,
    )
```

```python
import functools

import jax
import jax.numpy as jnp
from jax import lax
from jax.experimental import pallas as pl
from jax.experimental.pallas import tpu as pltpu
from jax.sharding import PartitionSpec as P

EPS = 1e-05
BASE = 10000.0
NEG = -1e30
LOG2E = 1.4426950408889634
BF = jnp.bfloat16
F32 = jnp.float32
I32 = jnp.int32
LANES = 128

def norm_rows(values, gain):
    recip = lax.rsqrt(jnp.mean(values * values, -1, keepdims=True) + EPS)
    return (values * recip * gain, recip)


def rotate(values, cosine_rows, sine_rows):
    half_dim = values.shape[-1] // 2
    front_half = values[..., :half_dim]
    back_half = values[..., half_dim:]
    return jnp.concatenate(
        [
            front_half * cosine_rows - back_half * sine_rows,
            front_half * sine_rows + back_half * cosine_rows,
        ],
        -1,
    )


def dense(left, right):
    return jnp.dot(left, right, preferred_element_type=F32)


def dense_tn(left, right):
    return lax.dot_general(left, right, (((0,), (0,)), ((), ())), preferred_element_type=F32)


def dense_nt(left, right):
    return lax.dot_general(left, right, (((1,), (1,)), ((), ())), preferred_element_type=F32)


def key_block(key_count, most):
    for size in (1536, 1024, 512, 256, 128):
        if size <= most and key_count % size == 0:
            return size
    return key_count


def row_tile(rows):
    for parts in (3, 2):
        if rows % (parts * 128) == 0:
            return rows // parts
    return rows


def over_key_blocks(info_ref, size, tokens, run):
    first, low, high = info_ref[0], info_ref[1], info_ref[2]
    begin = low // size
    whole_end = jnp.maximum(first // size, begin)
    whole_begin = jnp.clip((high + size - 1) // size, begin, whole_end)
    end = (first + tokens + size - 1) // size
    lax.fori_loop(begin, whole_begin, lambda j, c: run(j, True), None)
    lax.fori_loop(whole_begin, whole_end, lambda j, c: run(j, False), None)
    lax.fori_loop(whole_end, end, lambda j, c: run(j, True), None)


def attend_kernel(
    size, tile, heads, places, wide, info_ref, pre_ref, cos_ref, sin_ref, first_ref, *refs
):
    pieces_in, refs = refs[: len(places)], refs[len(places) :]
    if wide:
        weight_in, refs = refs[0], refs[1:]
    query_out, out_ref, low_ref, log_ref, kv_out = refs[:5]
    max_ref, sum_ref, acc_ref, scores_ref, start_ref, index_ref, sems = refs[5 + wide : 12 + wide]
    query_ref, kv_ref, out_sems = refs[12 + wide : 15 + wide]
    tokens = pre_ref.shape[0]
    copies = []
    for n, (mask, offset) in enumerate(places):
        at = lax.bitwise_xor(info_ref[5], mask) * tokens + offset if mask is not None else 0
        rows = pl.ds(pl.multiple_of(at, 16), pieces_in[n].shape[0])
        copies.append(pltpu.make_async_copy(pieces_in[n], kv_ref.at[rows, :], sems.at[n]))
    for copy in copies:
        copy.start()
    if wide:
        branch_ref, weight_ref, weight_sem = refs[5], refs[16], refs[17]
        weight_copy = pltpu.make_async_copy(weight_in, weight_ref, weight_sem)
        weight_copy.start()
    width = kv_ref.shape[1] // 2
    half = width // 2
    lanes = max_ref.shape[1]
    scale = width**-0.5 * LOG2E
    cosine, sine = cos_ref[...], sin_ref[...]
    for h in range(heads):
        front = pre_ref[:, h * width : h * width + half]
        back = pre_ref[:, h * width + half : (h + 1) * width]
        rows = slice(h * tokens, (h + 1) * tokens)
        query_ref[rows, :half] = (front * cosine - back * sine).astype(BF)
        query_ref[rows, half:] = (front * sine + back * cosine).astype(BF)
        start_ref[rows, :] = first_ref[...]
        index_ref[rows, :] = info_ref[0] + lax.broadcasted_iota(I32, (tokens, lanes), 0)
    query_copy = pltpu.make_async_copy(query_ref, query_out, out_sems.at[0])
    query_copy.start()
    for copy in copies:
        copy.wait()
    kv_copy = pltpu.make_async_copy(kv_ref, kv_out, out_sems.at[1])
    kv_copy.start()
    pieces = [slice(n * lanes, (n + 1) * lanes) for n in range(size // lanes)]
    for i in range(heads * tokens // tile):
        r = slice(i * tile, (i + 1) * tile)
        max_ref[...] = jnp.full(max_ref.shape, NEG, F32)
        sum_ref[...] = jnp.zeros(sum_ref.shape, F32)
        acc_ref[...] = jnp.zeros(acc_ref.shape, F32)

        def score(j, masked, r=r):
            base = pl.multiple_of(j * size, size)
            scores = dense_nt(query_ref[r, :], kv_ref[pl.ds(base, size), :width])
            most = max_ref[...]
            lane = lax.broadcasted_iota(I32, max_ref.shape, 1)
            for n, piece in enumerate(pieces):
                part = scores[:, piece]
                if masked:
                    at = lane + (base + n * lanes)
                    allowed = (at >= start_ref[r, :]) & (at <= index_ref[r, :])
                    part = jnp.where(allowed, part, NEG)
                scores_ref[j, :, piece] = part
                most = jnp.maximum(most, part)
            max_ref[...] = most
            return None

        over_key_blocks(info_ref, size, tokens, score)
        most = jnp.max(max_ref[...], 1, keepdims=True) * scale
        max_ref[...] = jnp.broadcast_to(most, max_ref.shape)

        def mix(j, carry):
            base = pl.multiple_of(j * size, size)
            most, total = max_ref[...], sum_ref[...]
            probs = []
            for piece in pieces:
                prob = jnp.exp2(scores_ref[j, :, piece] * scale - most)
                total = total + prob
                probs.append(prob.astype(BF))
            sum_ref[...] = total
            acc_ref[...] += dense(jnp.concatenate(probs, 1), kv_ref[pl.ds(base, size), width:])
            return carry

        end = (info_ref[0] + tokens + size - 1) // size
        lax.fori_loop(info_ref[1] // size, end, mix, None)
        total = jnp.sum(sum_ref[...], 1, keepdims=True)
        log_ref[:, r] = jnp.broadcast_to(most + jnp.log2(total), max_ref.shape).T[0:1, :]
        out = acc_ref[...] * (1.0 / total)
        at = i * tile
        while at < (i + 1) * tile:
            h = at // tokens
            stop = min((i + 1) * tile, (h + 1) * tokens)
            rows, cols = slice(at - h * tokens, stop - h * tokens), slice(h * width, (h + 1) * width)
            part = out[at - i * tile : stop - i * tile, :]
            out_ref[rows, cols] = part
            low_ref[rows, cols] = part.astype(BF)
            at = stop

    query_copy.wait()
    kv_copy.wait()
    if wide:
        weight_copy.wait()

        def branch(i, carry):
            cols = pl.ds(pl.multiple_of(i * 512, 512), 512)
            branch_ref[:, cols] = dense(low_ref[...], weight_ref[:, cols]).astype(BF)
            return carry

        lax.fori_loop(0, branch_ref.shape[1] // 512, branch, None)


def in_vmem(count):
    return [pl.BlockSpec(memory_space=pltpu.VMEM) for _ in range(count)]


def attend(info, query_pre, cosine, sine, start, pieces, weight=None):
    tokens, all_heads = query_pre.shape
    width = pieces[0][0].shape[1] // 2
    keys = sum(piece[0].shape[0] for piece in pieces)
    rows = tokens * (all_heads // width)
    size = key_block(keys, 1536)
    tile = rows // 2 if rows % 256 == 0 else row_tile(rows)
    wide = weight is not None
    branch = [((tokens, weight.shape[1]), BF)] if wide else []
    start = jnp.broadcast_to(start[:, None], (tokens, LANES))
    return pl.pallas_call(
        functools.partial(
            attend_kernel, size, tile, all_heads // width, [piece[1:] for piece in pieces], wide
        ),
        out_shape=(
            jax.ShapeDtypeStruct((rows, width), BF),
            jax.ShapeDtypeStruct((tokens, all_heads), F32),
            jax.ShapeDtypeStruct((tokens, all_heads), BF),
            jax.ShapeDtypeStruct((1, rows), F32),
            jax.ShapeDtypeStruct((keys, 2 * width), BF),
            *[jax.ShapeDtypeStruct(*out) for out in branch],
        ),
        in_specs=[pl.BlockSpec(memory_space=pltpu.SMEM)]
        + in_vmem(4)
        + [pl.BlockSpec(memory_space=pl.ANY)] * (len(pieces) + wide),
        out_specs=(
            pl.BlockSpec(memory_space=pltpu.HBM),
            *in_vmem(3),
            pl.BlockSpec(memory_space=pltpu.HBM),
            *in_vmem(int(wide)),
        ),
        scratch_shapes=[
            pltpu.VMEM((tile, LANES), F32),
            pltpu.VMEM((tile, LANES), F32),
            pltpu.VMEM((tile, width), F32),
            pltpu.VMEM((keys // size, tile, size), F32),
            pltpu.VMEM((rows, LANES), I32),
            pltpu.VMEM((rows, LANES), I32),
            pltpu.SemaphoreType.DMA((len(pieces),)),
            pltpu.VMEM((rows, width), BF),
            pltpu.VMEM((keys, 2 * width), BF),
            pltpu.SemaphoreType.DMA((2,)),
        ]
        + ([pltpu.VMEM(weight.shape, BF), pltpu.SemaphoreType.DMA(())] if wide else []),
        compiler_params=pltpu.CompilerParams(vmem_limit_bytes=56 * 2**20),
        cost_estimate=brief(0),
        name="attend",
    )(info, query_pre, cosine, sine, start, *[piece[0] for piece in pieces], *([weight] if wide else []))


def attend_back_kernel(
    size, tile, heads, by_axis, info_ref, query_ref, grad_ref, out_ref, log_ref, cos_ref, sin_ref, kv_ref, start_ref, index_ref,
    gq_ref, near_ref, far_ref, gout_ref, gk_ref, gv_ref, gqt_ref, dots_ref,
):
    tokens = grad_ref.shape[0]
    width = kv_ref.shape[1] // 2
    half = width // 2
    scale = width**-0.5
    for h in range(heads):
        gout = grad_ref[:, h * width : (h + 1) * width]
        gout_ref[h * tokens : (h + 1) * tokens, :] = gout
        dots = gout.astype(F32) * out_ref[:, h * width : (h + 1) * width]
        dots_ref[h * tokens : (h + 1) * tokens, :] = dots[:, :half] + dots[:, half:]
    delta = jnp.sum(dots_ref[...].T, 0, keepdims=True)
    gk_ref[...] = jnp.zeros(gk_ref.shape, F32)
    gv_ref[...] = jnp.zeros(gv_ref.shape, F32)
    gqt_ref[...] = jnp.zeros(gqt_ref.shape, F32)

    def run(j, masked):
        base = pl.multiple_of(j * size, size)
        at_keys = pl.ds(base, size)
        keys = kv_ref[at_keys, :width]
        values = kv_ref[at_keys, width:]
        for i in range(heads * tokens // tile):
            r = slice(i * tile, (i + 1) * tile)
            query, gout = query_ref[r, :], gout_ref[r, :]
            probs = jnp.exp2(dense_nt(keys, query) * (scale * LOG2E) - log_ref[:, r])
            if masked:
                at = base + lax.broadcasted_iota(I32, (size, tile), 0)
                allowed = (at >= start_ref[:, r]) & (at <= index_ref[:, r])
                probs = jnp.where(allowed, probs, 0.0)
            gscores = (probs * (dense_nt(values, gout) - delta[:, r])).astype(BF)
            gv_ref[at_keys, :] += dense(probs.astype(BF), gout)
            gk_ref[at_keys, :] += dense(gscores, query)
            gqt_ref[:, r] += dense_tn(keys, gscores)
        return None

    over_key_blocks(info_ref, size, tokens, run)
    mine = info_ref[3]
    part = tokens // 2
    for s in range(kv_ref.shape[0] // part):
        rows = slice(s * part, (s + 1) * part)
        chip = s // 4
        if by_axis and s % 2 == 0:
            chip = chip % 2 * 2 + chip // 2
        gk = (gk_ref[rows, :] * scale).astype(BF)
        gv = gv_ref[rows, :].astype(BF)

        @pl.when(mine == s // 2 % 2)
        def _(s=s, chip=chip, gk=gk, gv=gv):
            near_ref[s % 2, chip, :, :width] = gk
            near_ref[s % 2, chip, :, width:] = gv

        @pl.when(mine != s // 2 % 2)
        def _(s=s, chip=chip, gk=gk, gv=gv):
            far_ref[s % 2, chip, :, :width] = gk
            far_ref[s % 2, chip, :, width:] = gv

    gq = (gqt_ref[...] * scale).T.astype(BF).astype(F32)
    cosine, sine = cos_ref[...], sin_ref[...]
    for h in range(heads):
        front = gq[h * tokens : (h + 1) * tokens, :half]
        back = gq[h * tokens : (h + 1) * tokens, half:]
        gq_ref[:, h * width : h * width + half] = (front * cosine + back * sine).astype(BF)
        gq_ref[:, h * width + half : (h + 1) * width] = (back * cosine - front * sine).astype(BF)


def attend_back(info, query, grad, out, log, cosine, sine, kv, start, index, by_axis):
    tokens, all_heads = grad.shape
    keys, width = kv.shape[0], kv.shape[1] // 2
    rows = tokens * (all_heads // width)
    blocks = keys // tokens
    return pl.pallas_call(
        functools.partial(
            attend_back_kernel, key_block(keys, 512), row_tile(rows), all_heads // width, by_axis
        ),
        out_shape=(
            jax.ShapeDtypeStruct((tokens, all_heads), BF),
            jax.ShapeDtypeStruct((2, blocks // 2, tokens // 2, 2 * width), BF),
            jax.ShapeDtypeStruct((2, blocks // 2, tokens // 2, 2 * width), BF),
        ),
        in_specs=[pl.BlockSpec(memory_space=pltpu.SMEM)] + in_vmem(9),
        out_specs=tuple(in_vmem(3)),
        scratch_shapes=[
            pltpu.VMEM((rows, width), BF),
            pltpu.VMEM((keys, width), F32),
            pltpu.VMEM((keys, width), F32),
            pltpu.VMEM((width, rows), F32),
            pltpu.VMEM((rows, width // 2), F32),
        ],
        compiler_params=pltpu.CompilerParams(vmem_limit_bytes=56 * 2**20),
        cost_estimate=brief(0),
        name="attend_back",
    )(info, query, grad, out, log, cosine, sine, kv, start, index)


def feed_kernel(tile, mid_ref, grad_ref, gate_ref, up_ref, hidden_ref, both_ref, part_ref):
    width = gate_ref.shape[1]

    def run(i, carry):
        rows = pl.ds(pl.multiple_of(i * tile, tile), tile)
        mid = mid_ref[rows, :]
        gate = dense(mid, gate_ref[...])
        up = dense(mid, up_ref[...])
        grad = grad_ref[rows, :]
        sigmoid = 1.0 / (1.0 + jnp.exp(-gate))
        active = gate * sigmoid
        hidden_ref[rows, :] = (active * up).astype(BF)
        grad_gate = (grad * up * sigmoid * (1.0 + gate * (1.0 - sigmoid))).astype(BF)
        grad_up = (grad * active).astype(BF)
        both_ref[rows, :width] = grad_gate
        both_ref[rows, width:] = grad_up
        part = dense_nt(grad_gate, gate_ref[...]) + dense_nt(grad_up, up_ref[...])
        part_ref[rows, :] = part.astype(BF)
        return carry

    lax.fori_loop(0, mid_ref.shape[0] // tile, run, None)


def feed_forward(mid, grad, gate, up):
    rows, model = mid.shape
    width = gate.shape[1]
    tile = next(t for t in (288, 192, 144, 96, 64, 48, 32, 16, rows) if rows % t == 0)
    return pl.pallas_call(
        functools.partial(feed_kernel, tile),
        out_shape=(
            jax.ShapeDtypeStruct((rows, width), BF),
            jax.ShapeDtypeStruct((rows, 2 * width), BF),
            jax.ShapeDtypeStruct((rows, model), BF),
        ),
        in_specs=in_vmem(4),
        out_specs=tuple(in_vmem(3)),
        compiler_params=pltpu.CompilerParams(vmem_limit_bytes=40 * 2**20),
        cost_estimate=brief(20),
        name="feed_forward",
    )(mid, grad, gate, up)


class Order:
    last = None


def brief(micros):
    return pl.CostEstimate(flops=int(micros * 1e8), bytes_accessed=0, transcendentals=0)


def call(kernel, outs, args, name, micros=0, scratch=(), grid=None, in_specs=None, out_specs=None, prefetch=None):
    out_shape = tuple(jax.ShapeDtypeStruct(*out) for out in outs)
    prefetch = in_order(prefetch)
    params = dict(
        out_shape=out_shape,
        compiler_params=pltpu.CompilerParams(vmem_limit_bytes=56 * 2**20),
        cost_estimate=brief(micros),
        name=name,
    )
    outs = placed_call(kernel, out_shape, args, params, scratch, grid, in_specs, out_specs, prefetch)
    Order.last = outs[0]
    return outs


def in_order(value):
    return value if Order.last is None else after(value, Order.last)


def wait(*values):
    Order.last = (Order.last, values)


def placed_call(kernel, out_shape, args, params, scratch, grid, in_specs, out_specs, prefetch):
    if grid is None:
        return pl.pallas_call(
            kernel,
            in_specs=[pl.BlockSpec(memory_space=pltpu.SMEM)] + in_vmem(len(args)),
            out_specs=tuple(in_vmem(len(out_shape))),
            scratch_shapes=list(scratch),
            **params,
        )(prefetch, *args)
    return pl.pallas_call(
        kernel,
        grid_spec=pltpu.PrefetchScalarGridSpec(
            num_scalar_prefetch=1,
            grid=grid,
            in_specs=in_specs,
            out_specs=tuple(out_specs),
            scratch_shapes=list(scratch),
        ),
        **params,
    )(prefetch, *args)


def once(shape, index):
    return pl.BlockSpec(shape, index, pipeline_mode=pl.Buffered(1))


def at_block(index, size):
    return pl.ds(pl.multiple_of(index * size, size), size)


CORE, RANK, SEQ = 3, 4, 5


def ahead(info_ref, shift, ranks):
    return lax.rem(info_ref[RANK] + shift, ranks)


def behind(info_ref, shift, ranks):
    return lax.rem(info_ref[RANK] + ranks - shift, ranks)


def chip_of(info_ref):
    return lax.div(info_ref[SEQ], 2)


def rank_blocks(info, index):
    return lambda i, info_ref: index(info_ref[RANK])


def project_kernel(
    info_ref, tokens_ref, gain_ref, down_ref, kv_weight_ref, latent_gain_ref, normed_ref, recip_ref, kv_ref, low_ref
):
    values = tokens_ref[...].astype(F32)
    normed, recip = norm_rows(values, gain_ref[...])
    normed_ref[...] = normed.astype(BF)
    recip_ref[...] = jnp.broadcast_to(recip, recip_ref.shape)
    rows = normed_ref.shape[0]
    low_ref[at_block(pl.program_id(0), rows), :] = dense(normed_ref[...], down_ref[...]).astype(BF)

    @pl.when(pl.program_id(0) == 0)
    def _():
        rest = latent_gain_ref[...]
        parts = []
        for _ in range(3):
            parts.append(rest.astype(BF))
            rest = rest - parts[-1].astype(F32)
        parts.append(jnp.zeros((EXTRA - 3, rest.shape[1]), BF))
        low_ref[low_ref.shape[0] - EXTRA :, :] = jnp.concatenate(parts, 0)

    kv_ref[...] = dense(normed_ref[...], kv_weight_ref[...])


EXTRA = 16


def project(info, tokens, gain, q_down, kv_weight, latent_gain):
    rows, model = tokens.shape
    tile = rows // 2
    widths = ((model, BF), (LANES, F32), (kv_weight.shape[1], F32))
    low = (rows + EXTRA, q_down.shape[1])
    return call(
        project_kernel,
        [((rows, width), dtype) for width, dtype in widths] + [(low, BF)],
        (tokens, gain.reshape(1, -1), q_down, kv_weight, latent_gain.reshape(1, -1)),
        "project",
        grid=(2,),
        in_specs=[
            pl.BlockSpec((tile, model), lambda i, w: (i, 0)),
            once((1, model), lambda i, w: (0, 0)),
            once(q_down.shape, lambda i, w: (0, 0)),
            once(kv_weight.shape, lambda i, w: (0, 0)),
            once((1, q_down.shape[1]), lambda i, w: (0, 0)),
        ],
        out_specs=[pl.BlockSpec((tile, width), lambda i, w: (i, 0)) for width, _ in widths]
        + [pl.BlockSpec(low, lambda i, w: (0, 0))],
        prefetch=info,
    )


def turn_kernel(info_ref, kv_ref, cos_ref, sin_ref, out_ref):
    half = cos_ref.shape[1]
    front, back = kv_ref[:, :half], kv_ref[:, half : 2 * half]
    cosine, sine = cos_ref[...], sin_ref[...]
    out_ref[:, :half] = (front * cosine - back * sine).astype(BF)
    out_ref[:, half : 2 * half] = (front * sine + back * cosine).astype(BF)
    out_ref[:, 2 * half :] = kv_ref[:, 2 * half :].astype(BF)


def turn(info, kv_pre, cosine, sine):
    return call(turn_kernel, [(kv_pre.shape, BF)], (kv_pre, cosine, sine), "turn", prefetch=info)[0]


def query_kernel(info_ref, latent_ref, own_ref, other_ref, low_ref, recip_ref, gain_ref, query_ref):
    rows = low_ref.shape[0]
    parts = latent_ref[rows:, :].astype(F32)
    gain_ref[...] = parts[0:1] + parts[1:2] + parts[2:3]
    normed, recip = norm_rows(latent_ref[:rows, :].astype(F32), gain_ref[...])
    low_ref[...] = normed.astype(BF)
    recip_ref[...] = jnp.broadcast_to(recip, recip_ref.shape)
    half = own_ref.shape[1]
    ranks = 4
    cols = latent_ref.shape[1] // ranks
    totals = [0.0, 0.0]
    for s in range(ranks):
        left = low_ref[:, at_block(behind(info_ref, s, ranks), cols)]
        for n, ref in enumerate((own_ref, other_ref)):
            totals[n] = totals[n] + dense(left, ref[s * cols : (s + 1) * cols, :])
    core = info_ref[CORE]
    query_ref[:, at_block(core, half)] = totals[0]
    query_ref[:, at_block(1 - core, half)] = totals[1]


def queries(info, latent, own, other):
    rows, width = latent.shape[0] - EXTRA, latent.shape[1]
    return call(
        query_kernel,
        [((rows, width), BF), ((rows, LANES), F32), ((1, width), F32), ((rows, 2 * own.shape[1]), F32)],
        (latent, own, other),
        "queries",
        prefetch=info,
    )


def latent_part_kernel(info_ref, grad_ref, own_ref, other_ref, *refs):
    outs, all_ref = refs[:-1], refs[-1]
    ranks, rows = len(outs), outs[0].shape[0]
    half, cols = own_ref.shape[1], own_ref.shape[0] // ranks
    core = info_ref[CORE]
    own_grad = grad_ref[:, at_block(core, half)]
    other_grad = grad_ref[:, at_block(1 - core, half)]
    for s in range(ranks):
        part = slice(s * cols, (s + 1) * cols)
        out = dense_nt(own_grad, own_ref[part, :]) + dense_nt(other_grad, other_ref[part, :])
        all_ref[:, at_block(behind(info_ref, s, ranks), cols)] = out.astype(BF)
    for s in range(ranks):
        outs[s][...] = all_ref[at_block(ahead(info_ref, s, ranks), rows), :]


def latent_parts(info, grad, own, other, ranks):
    rows, width = grad.shape[0], own.shape[0]
    return call(
        latent_part_kernel,
        [((rows // ranks, width), BF)] * ranks,
        (grad, own, other),
        "latent_parts",
        scratch=[pltpu.VMEM((rows, width), BF)],
        prefetch=info,
    )


def latent_back_kernel(info_ref, latent_ref, recip_ref, gain_ref, norm2_ref, *refs):
    parts, grad_ref = refs[:-1], refs[-1]
    grad_in = sum(part[...].astype(F32) for part in parts)
    latent = latent_ref[...].astype(F32)
    recip = recip_ref[:, 0:1]
    gained = grad_in * gain_ref[...]
    stat = jnp.sum(latent * gained, -1, keepdims=True)
    grad = recip * gained - latent * (recip * recip * recip * stat / latent.shape[1])
    rows, width = grad.shape
    grad_ref[:rows, :] = grad.astype(BF)
    sums = [norm2_ref[:, i * width : (i + 1) * width] for i in range(norm2_ref.shape[1] // width)]
    sums = jnp.concatenate(sums + [jnp.sum(grad_in * latent * recip, 0, keepdims=True)], 0)
    high = sums.astype(BF)
    low = (sums - high.astype(F32)).astype(BF)
    fill = jnp.zeros((EXTRA - 2 * sums.shape[0], width), BF)
    grad_ref[rows:, :] = jnp.concatenate([high, low, fill], 0)


def latent_back(info, latent, recip, gain, norm2, parts):
    rows, width = parts[0].shape
    return call(
        latent_back_kernel,
        [((rows + EXTRA, width), BF)],
        (latent, recip, gain, norm2, *parts),
        "latent_back",
        grid=(1,),
        in_specs=[
            pl.BlockSpec((rows, width), lambda i, w: (w[RANK], 0)),
            pl.BlockSpec((rows, LANES), lambda i, w: (w[RANK], 0)),
            pl.BlockSpec((1, width), lambda i, w: (0, 0)),
            pl.BlockSpec(norm2.shape, lambda i, w: (0, 0)),
        ]
        + [pl.BlockSpec((rows, width), lambda i, w: (0, 0)) for _ in parts],
        out_specs=[pl.BlockSpec((rows + EXTRA, width), lambda i, w: (0, 0))],
        prefetch=info,
    )[0]


def kv_back_kernel(info_ref, cos_ref, sin_ref, *refs):
    parts, out_ref = refs[:-1], refs[-1]
    total = sum(part[...].astype(F32) for part in parts).astype(BF).astype(F32)
    half = cos_ref.shape[1]
    front, back = total[:, :half], total[:, half : 2 * half]
    cosine, sine = cos_ref[...], sin_ref[...]
    out_ref[:, :half] = (front * cosine + back * sine).astype(BF)
    out_ref[:, half : 2 * half] = (back * cosine - front * sine).astype(BF)
    out_ref[:, 2 * half :] = total[:, 2 * half :].astype(BF)


def kv_back(info, cosine, sine, parts):
    rows, width = parts[0].shape
    return call(
        kv_back_kernel,
        [((rows, width), BF)],
        (cosine, sine, *parts),
        "kv_back",
        grid=(1,),
        in_specs=[pl.BlockSpec((rows, cosine.shape[1]), lambda i, w: (w[RANK], 0))] * 2
        + [pl.BlockSpec((rows, width), lambda i, w: (0, 0)) for _ in parts],
        out_specs=[pl.BlockSpec((rows, width), lambda i, w: (0, 0))],
        prefetch=info,
    )[0]


def mid_kernel(info_ref, branch_ref, tokens_ref, gain_ref, residual_ref, mid_ref, recip_ref):
    residual = tokens_ref[...].astype(F32) + branch_ref[...].astype(F32)
    normed, recip = norm_rows(residual, gain_ref[...])
    residual_ref[...] = residual
    mid_ref[...] = normed.astype(BF)
    recip_ref[...] = jnp.broadcast_to(recip, recip_ref.shape)


def mid_norm(info, branch, tokens, gain):
    rows, model = branch.shape
    whole = pl.BlockSpec((rows, model), lambda i, w: (0, 0))
    return call(
        mid_kernel,
        [((rows, model), F32), ((rows, model), BF), ((rows, LANES), F32)],
        (branch, tokens, gain.reshape(1, -1)),
        "mid_norm",
        grid=(1,),
        in_specs=[
            whole,
            pl.BlockSpec((rows, model), lambda i, w: (w[RANK], 0)),
            pl.BlockSpec((1, model), lambda i, w: (0, 0)),
        ],
        out_specs=[whole, whole, pl.BlockSpec((rows, LANES), lambda i, w: (0, 0))],
        prefetch=info,
    )


def mid_back_kernel(info_ref, grad_ref, residual_ref, recip_ref, gain_ref, out_grad_ref, branch_ref, gain_grad_ref):
    grad = grad_ref[...].astype(F32)
    residual = residual_ref[...]
    recip = recip_ref[:, 0:1]
    gained = grad * gain_ref[...]
    stat = jnp.sum(residual * gained, -1, keepdims=True)
    out = out_grad_ref[...].astype(F32) + recip * gained
    out = out - residual * (recip * recip * recip * stat / residual.shape[1])
    branch_ref[...] = out.astype(BF)
    gain_grad_ref[...] = jnp.sum(grad * residual * recip, 0, keepdims=True)


def mid_back(info, grad, residual, recip, gain, out_grad):
    rows, model = grad.shape
    whole = pl.BlockSpec((rows, model), lambda i, w: (0, 0))
    return call(
        mid_back_kernel,
        [((rows, model), BF), ((1, model), F32)],
        (grad, residual, recip, gain.reshape(1, -1), out_grad),
        "mid_back",
        grid=(1,),
        in_specs=[
            whole,
            whole,
            pl.BlockSpec((rows, LANES), lambda i, w: (0, 0)),
            pl.BlockSpec((1, model), lambda i, w: (0, 0)),
            pl.BlockSpec((rows, model), lambda i, w: (w[RANK], 0)),
        ],
        out_specs=[whole, pl.BlockSpec((1, model), lambda i, w: (0, 0))],
        prefetch=info,
    )


def matmul_kernel(dims, info_ref, left_ref, right_ref, *refs):
    out = lax.dot_general(left_ref[...], right_ref[...], (dims, ((), ())), preferred_element_type=F32)
    if len(refs) == 1:
        refs[0][...] = out.astype(BF)
        return
    outs, all_ref = refs[:-1], refs[-1]
    all_ref[...] = out.astype(BF)
    for s, out_ref in enumerate(outs):
        out_ref[...] = all_ref[at_block(ahead(info_ref, s, len(outs)), out_ref.shape[0]), :]


def matmul(info, left, right, transposed=False, parts=1):
    rows, depth = left.shape
    cols = right.shape[0 if transposed else 1]
    tile = next(t for t in ((512, 256, LANES) if transposed else (1024, 512, 256, LANES)) if cols % t == 0)
    if transposed:
        dims, spec = ((1,), (1,)), pl.BlockSpec((tile, depth), lambda i, w: (i, 0))
    else:
        dims, spec = ((1,), (0,)), pl.BlockSpec((depth, tile), lambda i, w: (0, i))
    outs = call(
        functools.partial(matmul_kernel, dims),
        [((rows // parts, cols), BF)] * parts,
        (left, right),
        "matmul",
        scratch=[pltpu.VMEM((rows, tile), BF)] if parts > 1 else [],
        grid=(cols // tile,),
        in_specs=[once((rows, depth), lambda i, w: (0, 0)), spec],
        out_specs=[pl.BlockSpec((rows // parts, tile), lambda i, w: (0, i))] * parts,
        prefetch=info,
    )
    return outs if parts > 1 else outs[0]


def quarter_order(info_ref):
    bit_x = lax.rem(chip_of(info_ref), 2)
    bit_y = lax.div(chip_of(info_ref), 2)
    return 1 - bit_x, 3 - bit_y, bit_x, 2 + bit_y


def product_kernel(counts, info_ref, *refs):
    outs, all_ref = refs[4 * len(counts) : 4 * len(counts) + 4], refs[-1]
    order = quarter_order(info_ref)
    rows = outs[0].shape[0]
    first = 0
    for n, count in enumerate(counts):
        own, other, own_right, other_right = refs[4 * n : 4 * n + 4]
        step = pl.program_id(0)

        def mixed(cols):
            out = dense_tn(own[:, cols], own_right[...])
            return (out + dense_tn(other[:, cols], other_right[...])).astype(BF)

        @pl.when((step >= first) & (step < first + count))
        def _():
            if rows >= 256:
                for out_ref, at in zip(outs, order):
                    out_ref[...] = mixed(at_block(at, rows))
            else:
                all_ref[...] = mixed(slice(None))
                for out_ref, at in zip(outs, order):
                    out_ref[...] = all_ref[at_block(at, rows), :]

        first += count


def pair_products(info, terms, tile):
    tokens, rows = terms[0][0].shape[0], terms[0][0].shape[1] // 2
    counts = [term[2].shape[1] // tile for term in terms]
    specs, args, first = [], [], 0
    for term, count in zip(terms, counts):
        specs += [once((tokens, rows), lambda i, w: (0, w[CORE]))] * 2
        place = lambda i, w, first=first, count=count: (0, jnp.clip(i - first, 0, count - 1))
        specs += [pl.BlockSpec((tokens, tile), place)] * 2
        args += term
        first += count
    return call(
        functools.partial(product_kernel, counts),
        [((rows // 4, first * tile), BF)] * 4,
        args,
        "pair_products",
        scratch=[pltpu.VMEM((rows, tile) if rows < 1024 else (16, LANES), BF)],
        grid=(first,),
        in_specs=specs,
        out_specs=[pl.BlockSpec((rows // 4, tile), lambda i, w: (0, i))] * 4,
        prefetch=info,
    )


def add_low(left, right):
    return (left.astype(F32) + right.astype(F32)).astype(BF)


def fold_near_kernel(info_ref, near_ref, got_ref, *outs):
    for out_ref, at in zip(outs, quarter_order(info_ref)):
        p, bit = lax.div(at, 2), lax.rem(at, 2)
        for other in range(2):
            chip = bit * 2 + other
            out_ref[other] = add_low(near_ref[p, chip], got_ref[p, chip])


def fold_near(info, near, got):
    _, chips, rows, cols = near.shape
    tile = rows // 3
    return call(
        fold_near_kernel,
        [((2, rows, cols), BF)] * 4,
        (near, got),
        "fold_near",
        grid=(3,),
        in_specs=[pl.BlockSpec((2, chips, tile, cols), lambda i, w: (0, 0, i, 0))] * 2,
        out_specs=[pl.BlockSpec((2, tile, cols), lambda i, w: (0, i, 0))] * 4,
        prefetch=info,
    )


def fold_first_kernel(info_ref, keep_first, got_first, keep_last, got_last, *outs):
    bit_x = lax.rem(chip_of(info_ref), 2)
    bit_y = lax.div(chip_of(info_ref), 2)
    outs[0][...] = add_low(keep_first[1 - bit_y], got_first[1 - bit_y])
    outs[1][...] = add_low(keep_last[1 - bit_x], got_last[1 - bit_x])
    outs[2][...] = add_low(keep_first[bit_y], got_first[bit_y])
    outs[3][...] = add_low(keep_last[bit_x], got_last[bit_x])


def fold_first(info, arrays, steps, micros=0):
    rows, cols = arrays[0].shape[1:]
    tile = rows // steps
    return call(
        fold_first_kernel,
        [((rows, cols), BF)] * 4,
        arrays,
        "fold_first",
        micros,
        grid=(steps,),
        in_specs=[pl.BlockSpec((2, tile, cols), lambda i, w: (0, i, 0))] * 4,
        out_specs=[pl.BlockSpec((tile, cols), lambda i, w: (i, 0))] * 4,
        prefetch=info,
    )


def fold_last_kernel(info_ref, keep_first, got_first, keep_last, got_last, out_ref):
    out_ref[0] = add_low(keep_first[...], got_first[...])
    out_ref[1] = add_low(keep_last[...], got_last[...])


def fold_last(info, arrays, steps):
    rows, cols = arrays[0].shape
    tile = rows // steps
    return call(
        fold_last_kernel,
        [((2, rows, cols), BF)],
        arrays,
        "fold_last",
        grid=(steps,),
        in_specs=[pl.BlockSpec((tile, cols), lambda i, w: (i, 0))] * 4,
        out_specs=[pl.BlockSpec((2, tile, cols), lambda i, w: (0, i, 0))],
        prefetch=info,
    )[0]


def fold_kv_kernel(info_ref, keep_first, got_first, keep_last, got_last, *refs):
    outs, all_ref = refs[:-1], refs[-1]
    half = keep_first.shape[0]
    all_ref[:half, :] = add_low(keep_first[...], got_first[...])
    all_ref[half:, :] = add_low(keep_last[...], got_last[...])
    for s, out_ref in enumerate(outs):
        out_ref[...] = all_ref[at_block(ahead(info_ref, s, len(outs)), out_ref.shape[0]), :]


def fold_kv(info, arrays, ranks):
    rows, cols = arrays[0].shape
    return call(
        fold_kv_kernel,
        [((2 * rows // ranks, cols), BF)] * ranks,
        arrays,
        "fold_kv",
        scratch=[pltpu.VMEM((2 * rows, cols), BF)],
        prefetch=info,
    )


def fold_up_kernel(info_ref, keep_first, got_first, keep_last, got_last, *refs):
    ups, all_ref = refs[:-1], refs[-1]
    all_ref[0] = add_low(keep_first[...], got_first[...])
    all_ref[1] = add_low(keep_last[...], got_last[...])
    for s, up_ref in enumerate(ups):
        up_ref[...] = all_ref[:, at_block(ahead(info_ref, s, len(ups)), up_ref.shape[1]), :]


def fold_up(info, arrays, ranks):
    rows, cols = arrays[0].shape
    return call(
        fold_up_kernel,
        [((2, rows // ranks, cols), BF)] * ranks,
        arrays,
        "fold_up",
        scratch=[pltpu.VMEM((2, rows, cols), BF)],
        prefetch=info,
    )


def pack_up_kernel(info_ref, *refs):
    ups, all_ref = refs[:-1], refs[-1]
    for s, up_ref in enumerate(ups):
        all_ref[:, at_block(behind(info_ref, s, len(ups)), up_ref.shape[1]), :] = up_ref[...]


def pack_up(info, ups):
    _, rows, cols = ups[0].shape
    return call(pack_up_kernel, [((2, rows * len(ups), cols), BF)], ups, "pack_up", prefetch=info)[0]


def layer_kernel(info_ref, residual_ref, feed_ref, left_ref, right_ref):
    half = left_ref.shape[1]
    out = (residual_ref[...] + feed_ref[...].astype(F32)).astype(BF)
    left_ref[...] = out[:, :half]
    right_ref[...] = out[:, half:]


def layer_halves(info, residual, feed):
    rows, model = residual.shape
    return call(
        layer_kernel, [((rows, model // 2), BF)] * 2, (residual, feed), "layer", prefetch=info
    )


def place_kernel(info_ref, *refs):
    out_ref = refs[-1]
    half = out_ref.shape[1] // 2
    for s in range(len(refs) // 2):

        @pl.when(pl.program_id(0) == s)
        def _(s=s):
            out_ref[:, :half] = refs[2 * s][...]
            out_ref[:, half:] = refs[2 * s + 1][...]


def place(info, lefts, rights):
    rows, cols = lefts[0].shape
    ranks = len(lefts)
    parts = [part for pair in zip(lefts, rights) for part in pair]
    return call(
        place_kernel,
        [((ranks * rows, 2 * cols), BF)],
        parts,
        "place",
        grid=(ranks,),
        in_specs=[once((rows, cols), lambda i, w: (0, 0))] * len(parts),
        out_specs=[pl.BlockSpec((rows, 2 * cols), lambda i, w: (behind(w, i, ranks), 0))],
        prefetch=info,
    )[0]


def input_back_kernel(
    ranks, info_ref, tokens_ref, branch_ref, gain_ref, kv_weight_ref, recip_ref, latent_ref, kv_pre_ref, *refs
):
    latents, kvs, downs = refs[:ranks], refs[ranks : 2 * ranks], refs[2 * ranks : 3 * ranks]
    grad_in_ref, small_ref, own_ref, kv_ref, all_ref, sums_ref = refs[3 * ranks :]
    rows = kvs[0].shape[0]
    cols = own_ref.shape[1]
    sums = 0.0
    for s in range(ranks):
        at = at_block(behind(info_ref, s, ranks), rows)
        all_ref[at, :] = latents[s][:rows, :]
        sums = sums + latents[s][rows:, :].astype(F32)
        kv_ref[at, :] = kvs[s][...]
    grad = dense_nt(kv_ref[...], kv_weight_ref[...])
    for s in range(ranks):
        at = at_block(behind(info_ref, s, ranks), cols)
        grad = grad + dense_nt(all_ref[:, at], downs[s][...])
    own_ref[...] = all_ref[:, at_block(info_ref[RANK], cols)]
    recip = recip_ref[:, 0:1]
    latent = latent_ref[: all_ref.shape[0], :].astype(F32)
    stat = jnp.sum(all_ref[...].astype(F32) * latent, -1, keepdims=True)
    stat = stat + jnp.sum(kv_ref[...].astype(F32) * kv_pre_ref[...], -1, keepdims=True)
    tokens = tokens_ref[...].astype(F32)
    model = tokens.shape[1] * ranks
    out = branch_ref[...].astype(F32) + recip * gain_ref[...] * grad
    grad_in_ref[...] = out - tokens * (recip * recip * stat / model)
    count = sums.shape[0] // 16 * 3
    sums = sums[:count] + sums[count : 2 * count]
    sums_ref[...] = sums[count - 1 :]
    norm1 = jnp.sum(grad * tokens * recip, 0, keepdims=True)
    lines = [sums[r : r + 1, i * cols : (i + 1) * cols] for r in range(count - 1) for i in range(sums.shape[1] // cols)]
    lines += [norm1[:, i * cols : (i + 1) * cols] for i in range(norm1.shape[1] // cols)]
    lines.append(sums_ref[:, at_block(info_ref[RANK], cols)])
    lines += [jnp.zeros_like(lines[0])] * (small_ref.shape[0] - len(lines))
    small_ref[...] = jnp.concatenate(lines, 0).astype(BF)


def input_back(info, tokens, branch, gain, kv_weight, recip, latent, kv_pre, latents, kvs, downs):
    ranks = len(latents)
    rows, model = tokens.shape
    cols = model // ranks
    width, down = kv_weight.shape[1], downs[0].shape[1]
    whole = lambda array: pl.BlockSpec(array.shape, lambda i, w: (0, 0))
    wide = pl.BlockSpec((rows, cols), lambda i, w: (0, w[RANK]))
    outs = [((rows, cols), F32), ((16, down), BF), ((rows, down), BF), ((rows, width), BF)]
    return call(
        functools.partial(input_back_kernel, ranks),
        outs,
        (tokens, branch, gain.reshape(1, -1), kv_weight, recip, latent, kv_pre, *latents, *kvs, *downs),
        "input_back",
        scratch=[pltpu.VMEM((rows, latent.shape[1]), BF), pltpu.VMEM((1, latent.shape[1]), F32)],
        grid=(1,),
        in_specs=[
            wide,
            wide,
            pl.BlockSpec((1, cols), lambda i, w: (0, w[RANK])),
            pl.BlockSpec((cols, width), lambda i, w: (w[RANK], 0)),
        ]
        + [whole(array) for array in (recip, latent, kv_pre, *latents, *kvs, *downs)],
        out_specs=[pl.BlockSpec(shape, lambda i, w: (0, 0)) for shape, _ in outs],
        prefetch=info,
    )


def last_products_kernel(info_ref, normed_ref, latent_ref, kv_ref, small_ref, out_ref):
    rows, width = normed_ref.shape[1], latent_ref.shape[1]
    out_ref[:rows, :] = dense_tn(normed_ref[...], latent_ref[...]).astype(BF)
    count = (out_ref.shape[0] - rows - small_ref.shape[0]) // 2
    wide = dense_tn(normed_ref[:, at_block(info_ref[RANK], count)], kv_ref[...]).astype(BF)
    out_ref[rows : rows + count, :] = wide[:, :width]
    out_ref[rows + count : rows + 2 * count, :] = wide[:, width:]
    out_ref[rows + 2 * count :, :] = small_ref[...]


def last_products(info, normed, latent, kv, small, ranks):
    model, width = normed.shape[1], latent.shape[1]
    shape = (model + 2 * model // ranks + small.shape[0], width)
    return call(
        last_products_kernel, [(shape, BF)], (normed, latent, kv, small), "last_products", prefetch=info
    )[0]


def last_kernel(info_ref, in_ref, down_ref, kv_ref, small_ref):
    rows, width = down_ref.shape
    count = kv_ref.shape[0]
    down_ref[...] = in_ref[:rows, :].astype(F32)
    kv_ref[:, :width] = in_ref[rows : rows + count, :].astype(F32)
    kv_ref[:, width:] = in_ref[rows + count : rows + 2 * count, :].astype(F32)
    small_ref[...] = in_ref[rows + 2 * count :, :].astype(F32)


def store_feed(part, at, gate_ref, up_ref, down_ref):
    rows, width = part.shape[0], gate_ref.shape[1]
    block = slice(at * rows, (at + 1) * rows)
    gate_ref[block, :] = part[:, :width].astype(F32)
    up_ref[block, :] = part[:, width : 2 * width].astype(F32)
    down_ref[:, block] = part[:, 2 * width :].astype(F32).T


def store_same(part, at, out_ref):
    rows = part.shape[0]
    out_ref[at * rows : (at + 1) * rows, :] = part.astype(F32)


def unpack_up_kernel(info_ref, *refs):
    out_ref = refs[-1]
    for mask, ref in enumerate(refs[:-1]):
        source = lax.bitwise_xor(info_ref[SEQ], mask)
        core, chip = lax.rem(source, 2), lax.div(source, 2)
        _, rows, cols = ref.shape
        rows = rows // (out_ref.shape[1] // cols)
        for p in range(2):
            place = lax.rem(chip, 2) * 2 + lax.div(chip, 2) if p == 0 else chip
            at = at_block(core * 8 + p * 4 + place, rows)
            for r in range(out_ref.shape[1] // cols):
                block = ref[p, r * rows : (r + 1) * rows, :].astype(F32)
                out_ref[at, r * cols : (r + 1) * cols] = block


def unpack_up(info, pieces, shape):
    return call(unpack_up_kernel, [(shape, F32)], pieces, "unpack_up", prefetch=info)[0]


def unpack_kernel(store, info_ref, in_ref, *out_refs):
    part = lax.rem(pl.program_id(0), 2)
    for chip in range(4):
        turned = chip % 2 * 2 + chip // 2
        pl.when(part == 0)(lambda chip=chip, at=turned: store(in_ref[chip], at, *out_refs))
        pl.when(part == 1)(lambda chip=chip: store(in_ref[chip], chip, *out_refs))


def unpack(info, whole, store, shapes, along):
    _, _, rows, cols = whole.shape
    whole = whole.reshape(4, 2, 2, rows, cols)
    out_specs = []
    for (height, width), dim in zip(shapes, along):
        if dim == 0:
            out_specs.append(pl.BlockSpec((height // 4, width), lambda i, w: (i, 0)))
        else:
            out_specs.append(pl.BlockSpec((height, width // 4), lambda i, w: (0, i)))
    return call(
        functools.partial(unpack_kernel, store),
        [(shape, F32) for shape in shapes],
        (whole,),
        "unpack",
        grid=(4,),
        in_specs=[
            pl.BlockSpec((4, None, None, rows, cols), lambda i, w: (0, i // 2, i % 2, 0, 0))
        ],
        out_specs=out_specs,
        prefetch=info,
    )


def bit_of(index, bit):
    return (index >> bit) & 1


def exchange(value, mask):
    count = lax.axis_size("seq")
    return lax.ppermute(value, "seq", [(i, i ^ mask) for i in range(count)])


def swap(value, bit):
    return exchange(value, 1 << bit)


def ring(value, shift):
    if not shift:
        return value
    ranks = lax.axis_size("rank")
    return lax.ppermute(value, "rank", [(i, (i + shift) % ranks) for i in range(ranks)])


def rings(values):
    return [ring(value, s) for s, value in enumerate(values)]


def both(first, last):
    return swap(first, 1), swap(last, 2)


def sum_over(value, axis):
    count = lax.axis_size(axis)
    mask = 1
    while mask < count:
        value = value + lax.ppermute(value, axis, [(i, i ^ mask) for i in range(count)])
        mask *= 2
    return value


def after(value, *others):
    return lax.optimization_barrier((value, others))[0]


def per_device_fast(
    tokens_in,
    norm1_gain,
    q_down,
    latent_gain,
    q_up,
    kv_weight,
    out_weight,
    norm2_gain,
    gate_weight,
    up_weight,
    down_weight,
    doc_ids,
    out_grad,
):
    Order.last = None
    row_count, model_width = tokens_in.shape
    ranks = lax.axis_size("rank")
    rank_ix = lax.axis_index("rank")
    seq_ix = lax.axis_index("seq")
    head_dim = kv_weight.shape[1] // 2
    local_heads = out_weight.shape[0] // head_dim
    first_row = seq_ix * row_count
    core = bit_of(seq_ix, 0)
    rank_cols = q_down.shape[1]
    rank_width = rank_cols * ranks
    col_count = model_width // ranks

    up_cols = q_up.shape[1] // ranks
    half_cols = up_cols // 2
    blocks = [
        lax.dynamic_slice_in_dim(
            q_up, lax.rem(rank_ix + s, ranks) * up_cols + core * half_cols, half_cols, 1
        )
        for s in range(ranks)
    ]
    tokens_late = after(tokens_in, blocks)
    up_own = jnp.concatenate(rings(blocks), 0)
    up_other = swap(up_own, 0)

    ids_local = lax.dynamic_slice_in_dim(doc_ids, first_row, row_count, 0)
    start = jnp.sum((doc_ids[None, :] < ids_local[:, None]).astype(I32), 1)
    query_index = first_row + jnp.arange(row_count, dtype=I32)
    position = (query_index - start).astype(F32)
    half_dim = head_dim // 2
    freqs = BASE ** (-jnp.arange(half_dim, dtype=F32) / half_dim)
    angle = position[:, None] * freqs[None, :]
    cosine, sine = jnp.cos(angle), jnp.sin(angle)
    start_rows = jnp.tile(start, local_heads)[None]
    index_rows = jnp.tile(query_index, local_heads)[None]
    place_info = jnp.stack([first_row, first_row, first_row, core, rank_ix, seq_ix]).astype(I32)
    info = jnp.stack([first_row, start[0], start[-1], core, rank_ix, seq_ix]).astype(I32)

    normed_low, recip1, kv_pre, latent = project(
        place_info, tokens_late, norm1_gain, q_down, kv_weight, latent_gain
    )
    latent_all = lax.all_gather(latent, "rank", axis=1, tiled=True)

    kv_local = turn(place_info, kv_pre, cosine, sine)
    half_rows = row_count // 2
    by_x, by_y = lax.optimization_barrier(both(kv_local, kv_local))
    top, bottom = swap(by_x[:half_rows], 2), swap(by_y[half_rows:], 1)
    pieces = [(kv_local, 0, 0), (by_x, 2, 0), (by_y, 4, 0), (top, 6, 0), (bottom, 6, half_rows)]
    pieces += [(swap(array, 0), mask ^ 1, offset) for array, mask, offset in pieces]

    latent_low, recip_c, gain_all, query_pre = queries(place_info, latent_all, up_own, up_other)
    query, attn_vals, attn_low, log_total, kv_all, branch_part = attend(
        in_order(info), query_pre, cosine, sine, start, pieces, out_weight
    )
    Order.last = attn_low

    branch = lax.psum_scatter(branch_part, "rank", scatter_dimension=0, tiled=True)
    grad_hidden = dense_nt(after(out_grad, branch_part), down_weight)
    out_grad_pair = swap(after(out_grad, branch_part), 0)
    attn_pair = swap(attn_low, 0)
    piece_cols = rank_cols // 16
    latent_cut = jnp.transpose(
        after(latent_low, branch_part).reshape(row_count, ranks, 16, piece_cols), (0, 2, 1, 3)
    ).reshape(row_count, rank_width)
    latent_pair = swap(latent_cut, 0)
    down_blocks = [
        lax.dynamic_slice_in_dim(
            after(q_down, branch_part), lax.rem(rank_ix + s, ranks) * col_count, col_count, 0
        )
        for s in range(ranks)
    ]
    branch = after(
        branch, grad_hidden, out_grad_pair, attn_pair, latent_pair, latent_cut, down_blocks
    )
    residual, mid_own, recip2 = mid_norm(info, branch, tokens_in, norm2_gain)
    mid_low = lax.all_gather(mid_own, "rank", axis=0, tiled=True)

    downs = rings(after(down_blocks, mid_low))
    mid_pair = swap(mid_low, 0)
    hidden_low, grad_both, grad_mid_part = feed_forward(
        mid_low, grad_hidden, gate_weight, up_weight
    )
    Order.last = hidden_low
    hidden_low, grad_both, grad_mid_part = after((hidden_low, grad_both, grad_mid_part), downs)
    grad_mid = lax.psum_scatter(grad_mid_part, "rank", scatter_dimension=0, tiled=True)
    both_pair, hidden_pair = swap(grad_both, 0), swap(hidden_low, 0)
    feed_part = matmul(info, hidden_low, down_weight)
    feed_width = gate_weight.shape[1]
    send_first, send_last, keep_first, keep_last = pair_products(
        info,
        [
            (mid_low, mid_pair, grad_both, both_pair),
            (out_grad, out_grad_pair, hidden_low, hidden_pair),
        ],
        feed_width,
    )
    grad_mid = after(grad_mid, send_first)
    branch_own, norm2_part = mid_back(info, grad_mid, residual, recip2, norm2_gain, out_grad)
    grad_branch = lax.all_gather(branch_own, "rank", axis=0, tiled=True)

    two = lambda array: array.reshape((2, -1) + array.shape[1:])
    first, last = both(send_first, send_last)
    arrays = [two(array) for array in (keep_first, first, keep_last, last)]
    arrays = fold_first(info, arrays, 4, 10000)
    last, first = both(arrays[1], arrays[0])
    grad_branch = after(grad_branch, arrays[0])
    grad_attn = matmul(info, grad_branch, out_weight, True)
    third = row_count // 3
    branch_pair = jnp.concatenate(
        [swap(grad_branch[i * third : (i + 1) * third], 0) for i in range(3)], 0
    )
    outs = pair_products(info, [(attn_low, attn_pair, grad_branch, branch_pair)], up_cols)
    feed_piece = fold_last(info, (arrays[2], first, arrays[3], last), 4)
    feed_whole = lax.all_gather(feed_piece, "seq", axis=0, tiled=False)
    feed_sum = lax.psum_scatter(
        after(feed_part, arrays[0]), "rank", scatter_dimension=0, tiled=True
    )
    first, last = both(outs[0], outs[1])
    grad_query, near, far = attend_back(
        in_order(info), query, grad_attn, attn_vals, log_total, cosine, sine, kv_all,
        start_rows, index_rows, True,
    )
    (grad_query, near, far), feed_sum = lax.optimization_barrier(
        (after((grad_query, near, far), first, last), feed_sum)
    )
    Order.last = grad_query

    far, query_pair = swap(far, 0), swap(grad_query, 0)
    outs = [two(array) for array in (outs[2], first, outs[3], last)]
    outs = fold_first(info, outs, 1)
    last, first = both(outs[1], outs[0])
    latent_grads = rings(latent_parts(info, grad_query, up_own, up_other, ranks))
    arrays = fold_near(info, near, far)
    out_piece = fold_last(info, (outs[2], first, outs[3], last), 1)
    out_whole = lax.all_gather(out_piece, "seq", axis=0, tiled=False)
    kv_first, kv_last = both(*after(arrays[:2], out_piece))
    ups = pair_products(info, [(latent_cut, latent_pair, grad_query, query_pair)], up_cols)
    wait(latent_grads, kv_first, kv_last)

    latent_own = latent_back(info, latent_all, recip_c, gain_all, norm2_part, latent_grads)
    latent_blocks = rings([latent_own] * ranks)
    arrays = fold_first(info, (arrays[2], kv_first, arrays[3], kv_last), 1)
    kv_last, kv_first = both(arrays[1], arrays[0])
    kv_sums = rings(fold_kv(info, (arrays[2], kv_first, arrays[3], kv_last), ranks))
    ups_first, ups_last = both(*in_order(ups[:2]))
    ups = fold_first(info, [two(array) for array in (ups[2], ups_first, ups[3], ups_last)], 1)
    ups_last, ups_first = both(ups[1], ups[0])
    layer_left, layer_right = layer_halves(info, residual, feed_sum)
    joined, *latent_blocks = lax.optimization_barrier((info, *latent_blocks))

    ups = rings(fold_up(joined, (ups[2], ups_first, ups[3], ups_last), ranks))
    kv_own = kv_back(info, cosine, sine, kv_sums)
    kv_blocks = rings([kv_own] * ranks)
    wait(kv_blocks)

    grad_in, small, latent_cols, grad_kv = input_back(
        info, tokens_in, grad_branch, norm1_gain, kv_weight, recip1, latent_all, kv_pre,
        latent_blocks, kv_blocks, downs,
    )
    last = last_products(info, normed_low, latent_cols, grad_kv, small, ranks)
    last = lax.psum(last, "seq")
    up_piece = pack_up(info, ups)
    lefts = rings([in_order(layer_left)] * ranks)
    up_pieces = [up_piece] + [exchange(in_order(up_piece), mask) for mask in (1, 2)]
    shape = gate_weight.shape
    grad_gate, grad_up, grad_down = unpack(
        info, feed_whole, store_feed, (shape, shape, shape[::-1]), (0, 0, 1)
    )
    rights = rings([in_order(layer_right)] * ranks)
    up_pieces += [exchange(in_order(up_piece), mask) for mask in range(3, 8)]
    grad_out = unpack(info, out_whole, store_same, [out_weight.shape], [0])[0]
    layer_out = place(info, lefts, rights)
    grad_q_up = unpack_up(info, up_pieces, q_up.shape)
    grad_q_down, grad_kv_weight, small = call(
        last_kernel,
        [(q_down.shape, F32), ((col_count, 2 * head_dim), F32), (small.shape, F32)],
        (last,),
        "last",
        prefetch=info,
    )

    small = small.reshape(-1)
    norm1 = small[model_width : model_width + col_count]
    grad_latent_gain = small[model_width + col_count : model_width + col_count + rank_cols]
    grad_norm2 = small[:model_width]
    return (
        layer_out,
        grad_in,
        norm1,
        grad_q_down,
        grad_latent_gain,
        grad_q_up,
        grad_kv_weight,
        grad_out,
        grad_norm2,
        grad_gate,
        grad_up,
        grad_down,
    )


def add_low(left, right):
    return (left.astype(F32) + right.astype(F32)).astype(BF)


def halve(value, axis, bit, seq_ix):
    own = bit_of(seq_ix, bit)
    keep = lax.dynamic_index_in_dim(value, own, axis, keepdims=False)
    send = lax.dynamic_index_in_dim(value, 1 - own, axis, keepdims=False)
    return add_low(keep, swap(send, bit))


def scatter_chips(value, seq_ix):
    bits = value.shape[0].bit_length() - 1
    shape = (2,) * bits + value.shape[2:]
    first, last = value[:, 0].reshape(shape), value[:, 1].reshape(shape)
    first_axes = list(range(bits))
    last_axes = list(range(bits))
    for step in range(bits):
        bit = step + 1
        axis = first_axes.index(bits - bit)
        first = halve(first, axis, bit, seq_ix)
        del first_axes[axis]
        bit = bits - step
        axis = last_axes.index(bits - bit)
        last = halve(last, axis, bit, seq_ix)
        del last_axes[axis]
    return jnp.stack([first, last])


def scatter_rows(near, far, seq_ix):
    return scatter_chips(add_low(near, swap(far, 0)), seq_ix)


def split_product(left, right, seq_ix):
    chips = lax.axis_size("seq") // 2
    rows = left.shape[1] // 2
    own = bit_of(seq_ix, 0)
    parts = []
    for core in (own, 1 - own):
        piece = lax.dynamic_slice_in_dim(left, core * rows, rows, 1)
        parts.append(dense_tn(piece, right).astype(BF))
    shape = (2, chips, rows // (2 * chips), right.shape[1])
    return [jnp.swapaxes(part.reshape(shape), 0, 1) for part in parts]


def gather_rows(piece):
    seq = lax.axis_size("seq")
    whole = lax.all_gather(piece, "seq", axis=0, tiled=False)
    whole = whole.reshape((seq // 2, 2) + piece.shape)
    whole = jnp.transpose(whole, (1, 2, 0, 3, 4))
    return whole.reshape(seq * piece.shape[0] * piece.shape[1], piece.shape[2])


def reduce_product(left, right, seq_ix):
    near, far = split_product(left, right, seq_ix)
    return gather_rows(scatter_rows(near, far, seq_ix)).astype(F32)


def high_low(values):
    high = values.astype(BF)
    return [high, (values - high.astype(F32)).astype(BF)]


def per_device_general(
    tokens_in,
    norm1_gain,
    q_down,
    latent_gain,
    q_up,
    kv_weight,
    out_weight,
    norm2_gain,
    gate_weight,
    up_weight,
    down_weight,
    doc_ids,
    out_grad,
):
    row_count, model_width = tokens_in.shape
    rank_count = lax.axis_size("rank")
    seq_count = lax.axis_size("seq")
    rank_ix = lax.axis_index("rank")
    seq_ix = lax.axis_index("seq")
    head_dim = kv_weight.shape[1] // 2
    local_heads = out_weight.shape[0] // head_dim
    first_row = seq_ix * row_count
    core = bit_of(seq_ix, 0)
    own_rows = row_count // rank_count
    rank_cols = q_down.shape[1]
    rank_width = rank_cols * rank_count

    half_rows = q_up.shape[0] // 2
    up_half = lax.dynamic_slice_in_dim(q_up, core * half_rows, half_rows, 0)
    up_half = lax.all_to_all(up_half, "rank", 1, 0, tiled=True)
    up_other = swap(up_half, 0)
    up_half = up_half.reshape(rank_count, 1, half_rows, -1)
    up_other = up_other.reshape(rank_count, 1, half_rows, -1)
    q_up_own = jnp.concatenate(
        [jnp.where(core == 0, up_half, up_other), jnp.where(core == 0, up_other, up_half)], 1
    ).reshape(rank_width, -1)

    ids_local = lax.dynamic_slice_in_dim(doc_ids, first_row, row_count, 0)
    start = jnp.sum((doc_ids[None, :] < ids_local[:, None]).astype(I32), 1)
    query_index = first_row + jnp.arange(row_count, dtype=I32)
    position = (query_index - start).astype(F32)
    half_dim = head_dim // 2
    freqs = BASE ** (-jnp.arange(half_dim, dtype=F32) / half_dim)
    angle = position[:, None] * freqs[None, :]
    cosine_rows, sine_rows = jnp.cos(angle), jnp.sin(angle)
    start_rows = jnp.tile(start, local_heads)[None]
    index_rows = jnp.tile(query_index, local_heads)[None]
    info = jnp.stack([first_row, start[0], start[-1], core]).astype(I32)

    tokens = tokens_in.astype(F32)
    normed_in, recip1 = norm_rows(tokens, norm1_gain)
    normed_low = normed_in.astype(BF)
    kv_pre = dense(normed_low, kv_weight)
    key_local = rotate(kv_pre[:, :head_dim], cosine_rows, sine_rows)
    kv_local = jnp.concatenate([key_local, kv_pre[:, head_dim:]], -1).astype(BF)
    kv_all = lax.all_gather(kv_local, "seq", axis=0, tiled=True)

    latent = dense(normed_low, q_down)
    high, rest = high_low(latent_gain)
    low = (latent_gain - high.astype(F32) - rest.astype(F32)).astype(BF)
    gain_rows = jnp.stack([high, rest, low] + [jnp.zeros_like(high)] * 13)
    gathered = lax.all_gather(
        jnp.concatenate([latent.astype(BF), gain_rows], 0), "rank", axis=1, tiled=True
    ).astype(F32)
    latent_all = gathered[:row_count]
    gain_all = gathered[row_count] + gathered[row_count + 1] + gathered[row_count + 2]
    recip_c = lax.rsqrt(jnp.mean(latent_all * latent_all, -1, keepdims=True) + EPS)
    latent_low = (latent_all * recip_c * gain_all).astype(BF)
    query_pre = dense(latent_low, q_up_own)

    query, attn_vals, attn_low, log_total, kv_all = attend(
        info, query_pre, cosine_rows, sine_rows, start, [(kv_all, None, 0)]
    )
    branch = lax.psum_scatter(
        dense(attn_low, out_weight).astype(BF), "rank", scatter_dimension=0, tiled=True
    )
    tokens_rows = lax.dynamic_slice_in_dim(tokens_in, rank_ix * own_rows, own_rows, 0)
    residual = tokens_rows.astype(F32) + branch.astype(F32)
    normed_mid, recip2 = norm_rows(residual, norm2_gain)
    mid_low = lax.all_gather(normed_mid.astype(BF), "rank", axis=0, tiled=True)

    grad_hidden = dense_nt(out_grad, down_weight)
    gate_pre = dense(mid_low, gate_weight)
    up_pre = dense(mid_low, up_weight)
    sigmoid_gate = jax.nn.sigmoid(gate_pre)
    activated = gate_pre * sigmoid_gate
    hidden_low = (activated * up_pre).astype(BF)
    grad_gate_pre = (
        grad_hidden * up_pre * sigmoid_gate * (1.0 + gate_pre * (1.0 - sigmoid_gate))
    ).astype(BF)
    grad_up_pre = (grad_hidden * activated).astype(BF)
    grad_mid = lax.psum_scatter(
        (dense_nt(grad_gate_pre, gate_weight) + dense_nt(grad_up_pre, up_weight)).astype(BF),
        "rank",
        scatter_dimension=0,
        tiled=True,
    ).astype(F32)
    feed_out = lax.psum_scatter(
        dense(hidden_low, down_weight).astype(BF), "rank", scatter_dimension=0, tiled=True
    )
    layer_out = lax.all_gather(
        (residual + feed_out.astype(F32)).astype(BF), "rank", axis=0, tiled=True
    )
    grad_gate = reduce_product(mid_low, grad_gate_pre, seq_ix)
    grad_up = reduce_product(mid_low, grad_up_pre, seq_ix)
    grad_down = reduce_product(hidden_low, out_grad, seq_ix)

    gained_mid = grad_mid * norm2_gain
    stat_mid = jnp.sum(residual * gained_mid, -1, keepdims=True)
    out_grad_rows = lax.dynamic_slice_in_dim(out_grad, rank_ix * own_rows, own_rows, 0)
    grad_residual = (
        out_grad_rows.astype(F32)
        + recip2 * gained_mid
        - residual * recip2**3 * stat_mid / model_width
    )
    grad_norm2 = jnp.sum(grad_mid * residual * recip2, 0)
    grad_branch = lax.all_gather(grad_residual.astype(BF), "rank", axis=0, tiled=True)
    grad_attn = dense_nt(grad_branch, out_weight).astype(BF)
    grad_out = reduce_product(attn_low, grad_branch, seq_ix)
    grad_query, near, far = attend_back(
        info, query, grad_attn, attn_vals, log_total, cosine_rows, sine_rows, kv_all,
        start_rows, index_rows, False,
    )

    chips = seq_count // 2
    summed = scatter_rows(jnp.swapaxes(near, 0, 1), jnp.swapaxes(far, 0, 1), seq_ix)
    summed = lax.psum(summed.reshape(row_count, 2 * head_dim), "rank").astype(F32)
    key_back = rotate(summed[:, :head_dim], cosine_rows, -sine_rows)
    grad_kv = jnp.concatenate([key_back, summed[:, head_dim:]], -1).astype(BF)

    grad_latent_part = dense_nt(grad_query, q_up_own).astype(BF)
    norm2_rows = jnp.concatenate(high_low(grad_norm2)).reshape(-1, rank_width)
    extra = norm2_rows.shape[0]
    norm2_rows = jnp.pad(norm2_rows, ((0, -extra % 16), (0, 0)))
    over_ranks = lax.psum(jnp.concatenate([grad_latent_part, norm2_rows], 0), "rank").astype(F32)
    grad_latent_in = over_ranks[:row_count]
    grad_norm2 = jnp.sum(
        over_ranks[row_count : row_count + extra].reshape(2, model_width), 0
    )
    gained_latent = grad_latent_in * gain_all
    stat_latent = jnp.sum(latent_all * gained_latent, -1, keepdims=True)
    grad_latent = (
        recip_c * gained_latent - latent_all * recip_c**3 * stat_latent / rank_width
    ).astype(BF)
    own_latent = lambda v: lax.dynamic_slice_in_dim(v, rank_ix * rank_cols, rank_cols, 1)
    grad_latent_gain = jnp.sum(own_latent(grad_latent_in) * latent * recip_c, 0)

    near, far = split_product(grad_query, latent_low, seq_ix)
    piece = scatter_rows(near, far, seq_ix)
    piece = lax.all_to_all(piece, "rank", 2, 0, tiled=True)
    piece = piece.reshape(rank_count * 2, piece.shape[1], rank_cols)
    whole = lax.all_gather(piece, "seq", axis=0, tiled=False)
    whole = whole.reshape(chips, 2, rank_count, 2, piece.shape[1], rank_cols)
    grad_q_up = jnp.transpose(whole, (5, 2, 1, 3, 0, 4)).reshape(rank_cols, -1).astype(F32)

    col_count = model_width // rank_count
    col_start = rank_ix * col_count
    cols = lambda v: lax.dynamic_slice_in_dim(v, col_start, col_count, v.ndim - 1)
    q_down_rows = lax.all_to_all(q_down, "rank", 0, 1, tiled=True)
    kv_rows = lax.dynamic_slice_in_dim(kv_weight, col_start, col_count, 0)
    grad_normed = dense_nt(grad_latent, q_down_rows) + dense_nt(grad_kv, kv_rows)
    norm1_stat = (
        jnp.sum(grad_latent.astype(F32) * latent_all, -1, keepdims=True)
        + jnp.sum(grad_kv.astype(F32) * kv_pre, -1, keepdims=True)
    ) / recip1
    tokens_own = cols(tokens_in).astype(F32)
    grad_in = (
        cols(grad_branch).astype(F32)
        + recip1 * cols(norm1_gain) * grad_normed
        - tokens_own * recip1**3 * norm1_stat / model_width
    )
    grad_norm1 = jnp.sum(grad_normed * tokens_own * recip1, 0)

    grad_q_down = lax.psum(
        dense_tn(normed_low, own_latent(grad_latent)).astype(BF), "seq"
    ).astype(F32)
    grad_kv_weight = dense_tn(cols(normed_low), grad_kv).astype(BF)
    small = jnp.concatenate([grad_norm1, grad_latent_gain, grad_norm2])
    small = jnp.concatenate(high_low(small)).reshape(2, -1)
    count = small.shape[1]
    kv_cols = grad_kv_weight.shape[1]
    small_rows = jnp.pad(small.reshape(-1), (0, -2 * count % (16 * kv_cols))).reshape(-1, kv_cols)
    last = lax.psum(jnp.concatenate([grad_kv_weight, small_rows], 0), "seq").astype(F32)
    grad_kv_weight = last[:col_count]
    small = jnp.sum(last[col_count:].reshape(-1)[: 2 * count].reshape(2, count), 0)
    grad_norm1 = small[:col_count]
    grad_latent_gain = small[col_count : col_count + rank_cols]
    grad_norm2 = small[col_count + rank_cols :]
    return (
        layer_out,
        grad_in,
        grad_norm1,
        grad_q_down,
        grad_latent_gain,
        grad_q_up,
        grad_kv_weight,
        grad_out,
        grad_norm2,
        grad_gate,
        grad_up,
        grad_down,
    )


def per_device(*args):
    tokens, out_weight = args[0], args[6]
    fits = (
        lax.axis_size("seq") == 8
        and lax.axis_size("rank") == 4
        and tokens.shape[0] % 64 == 0
        and tokens.shape[1] % 2048 == 0
        and args[2].shape[1] % 256 == 0
        and out_weight.shape[0] % 1024 == 0
        and args[8].shape[1] % LANES == 0
        and args[11].shape[0] % 512 == 0
    )
    return (per_device_fast if fits else per_device_general)(*args)


def solution(mesh):
    return jax.shard_map(
        per_device,
        mesh=mesh,
        in_specs=(
            P("seq", None),
            P(),
            P(None, "rank"),
            P("rank"),
            P("rank", None),
            P(),
            P("rank", None),
            P(),
            P(None, "rank"),
            P(None, "rank"),
            P("rank", None),
            P(),
            P("seq", None),
        ),
        out_specs=(
            P("seq", None),
            P("seq", "rank"),
            P("rank"),
            P(None, "rank"),
            P("rank"),
            P("rank", None),
            P("rank", None),
            P("rank", None),
            P(),
            P(None, "rank"),
            P(None, "rank"),
            P("rank", None),
        ),
        check_vma=False,
    )
```
